32 devices in a mesh: seq: 8 (over y, x, core), mp: 4 (over z).
Axes of the slice: x: 2, y: 2, z: 4, core: 2. Of those that a mesh axis runs over, the one named last changes fastest.
Arguments:
- tokens: bfloat16 [2, 2048, 2048], P(None, ('seq', 'mp')), may hold values from -6 to 6
- lengths: int32 [2], replicated, may hold values from 512 to 2048, as said below
- mixer_gain: float32 [2048], replicated, may hold values from 0.5 to 1.5
- query_weight: bfloat16 [2048, 2048], P('seq', 'mp'), may hold values from -0.125 to 0.125
- key_weight: bfloat16 [2048, 2048], P('seq', 'mp'), may hold values from -0.125 to 0.125
- value_weight: bfloat16 [2048, 2048], P('seq', 'mp'), may hold values from -0.125 to 0.125
- beta_weight: bfloat16 [2048, 16], P('seq', 'mp'), may hold values from -0.125 to 0.125
- beta_bias: float32 [16], replicated, may hold values from -4.5 to -1.5
- conv_weight: float32 [3, 4, 2048], replicated, may hold values from -0.6 to 0.6
- head_gain: float32 [128], replicated, may hold values from 0.5 to 1.5
- out_weight: bfloat16 [2048, 2048], P('mp', 'seq'), may hold values from -0.125 to 0.125
- feed_gain: float32 [2048], replicated, may hold values from 0.5 to 1.5
- gate_weight: bfloat16 [2048, 5632], P('seq', 'mp'), may hold values from -0.125 to 0.125
- up_weight: bfloat16 [2048, 5632], P('seq', 'mp'), may hold values from -0.125 to 0.125
- down_weight: bfloat16 [5632, 2048], P('mp', 'seq'), may hold values from -0.078125 to 0.078125
- cotangent: bfloat16 [2, 2048, 2048], P(None, ('seq', 'mp')), may hold values from -6 to 6
Outputs:
- block_output: float32 [2, 2048, 2048], P(None, ('seq', 'mp'))
- grad_tokens: float32 [2, 2048, 2048], P(None, ('seq', 'mp'))
- grad_mixer_gain: float32 [2048], replicated
- grad_query_weight: float32 [2048, 2048], P('seq', 'mp')
- grad_key_weight: float32 [2048, 2048], P('seq', 'mp')
- grad_value_weight: float32 [2048, 2048], P('seq', 'mp')
- grad_beta_weight: float32 [2048, 16], P('seq', 'mp')
- grad_beta_bias: float32 [16], replicated
- grad_conv_weight: float32 [3, 4, 2048], replicated
- grad_head_gain: float32 [128], replicated
- grad_out_weight: float32 [2048, 2048], P('mp', 'seq')
- grad_feed_gain: float32 [2048], replicated
- grad_gate_weight: float32 [2048, 5632], P('seq', 'mp')
- grad_up_weight: float32 [2048, 5632], P('seq', 'mp')
- grad_down_weight: float32 [5632, 2048], P('mp', 'seq')
- state_norm: float32 [], replicated
The draws below stay inside these ranges and needn't reach their ends.
Inputs may be any that keep to these rules, and one draw needn't show every extreme that they name: `lengths`: each length is at least 512; one sequence, drawn from the seed, has exactly 2048 valid positions.
All inputs are finite; a program needn't handle non-finite values.
Results may differ from the reference program's by a relative error of at most 0.0099.
Values may be sent and summed in bfloat16 or wider, within the bound.
A program may use at most 320 MiB of HBM per device.

```python
import jax
import jax.numpy as jnp
from jax import lax

D = 2048
HEADS = 16
HEAD_DIM = 128
FF = 5632
CONV = 4
BLOCK = 64
NSEQ = 2
SEG = 256
LEN = 2048


def draw_lengths(key, part):
    key = jax.random.fold_in(key, 11)
    pick_key, size_key = jax.random.split(key)
    full_index = jax.random.randint(pick_key, (), 0, NSEQ)
    drawn = jax.random.randint(size_key, (NSEQ,), LEN // 4, LEN + 1)
    return jnp.where(jnp.arange(NSEQ) == full_index, LEN, drawn).astype(jnp.int32)


def shard_levels(key, dims, shards, low, high):
    def one(dim, parts):
        heights = jax.random.uniform(jax.random.fold_in(jax.random.fold_in(key, 6), dim), (parts,), jnp.float32, low / len(shards), high / len(shards))
        return jnp.repeat(jnp.exp(heights), dims[dim] // parts).reshape((-1,) + (1,) * (len(dims) - dim - 1))

    factor_of = one(*shards[0])
    for cut in shards[1:]:
        factor_of = factor_of * one(*cut)
    return factor_of


def centred(stream_key, shape, scale, limit, shards=(), kind=jnp.bfloat16):
    values = jax.random.normal(stream_key, shape, jnp.float32) * scale
    if len(shards) > 0:
        values = shard_levels(stream_key, shape, shards, -0.22, 0.18) * values
    return jnp.clip(values, min=-limit, max=limit).astype(kind)


def setup_inputs(seed: int = 0) -> dict:
    key_of = jax.random.split(jax.random.key(seed), 17)
    return {
        "tokens": centred(key_of[0], (NSEQ, LEN, D), 1.0, 6.0, ((1, 32),)),
        "lengths": draw_lengths(jax.random.fold_in(key_of[16], 71), 0),
        "mixer_gain": jnp.clip(1.0 + 0.1 * jax.random.normal(key_of[2], (D,), jnp.float32), 0.5, 1.5),
        "query_weight": centred(key_of[3], (D, D), D ** -0.5, 0.125, ((0, 8), (1, 4))),
        "key_weight": centred(key_of[4], (D, D), D ** -0.5, 0.125, ((0, 8), (1, 4))),
        "value_weight": centred(key_of[5], (D, D), D ** -0.5, 0.125, ((0, 8), (1, 4))),
        "beta_weight": centred(key_of[6], (D, HEADS), D ** -0.5, 0.125, ((0, 8), (1, 4))),
        "beta_bias": jnp.clip(jax.random.uniform(key_of[7], (HEADS,), jnp.float32, -4.5, -1.5), -4.5, -1.5),
        "conv_weight": jnp.clip(jax.random.uniform(key_of[8], (3, CONV, D), jnp.float32, -0.6, 0.6), -0.6, 0.6),
        "head_gain": jnp.clip(1.0 + 0.1 * jax.random.normal(key_of[9], (HEAD_DIM,), jnp.float32), 0.5, 1.5),
        "out_weight": centred(key_of[10], (D, D), D ** -0.5, 0.125, ((0, 4), (1, 8))),
        "feed_gain": jnp.clip(1.0 + 0.1 * jax.random.normal(key_of[11], (D,), jnp.float32), 0.5, 1.5),
        "gate_weight": centred(key_of[12], (D, FF), D ** -0.5, 0.125, ((0, 8), (1, 4))),
        "up_weight": centred(key_of[13], (D, FF), D ** -0.5, 0.125, ((0, 8), (1, 4))),
        "down_weight": centred(key_of[14], (FF, D), FF ** -0.5, 0.078125, ((0, 4), (1, 8))),
        "cotangent": centred(key_of[15], (NSEQ, LEN, D), 1.0, 6.0, ((1, 32),)),
    }


EPSILON = 1e-05
HIGHEST = lax.Precision.HIGHEST

@jax.custom_vjp
def low(v):
    return lax.optimization_barrier(v.astype(jnp.bfloat16)).astype(jnp.float32)

@jax.custom_vjp
def low_back(v):
    return v

def low_keep(v):
    return (low(v), None)

def low_pass(kept, grad):
    return (grad,)

def back_keep(v):
    return (v, None)

def back_low(kept, grad):
    return (low(grad),)
low.defvjp(low_keep, low_pass)
low_back.defvjp(back_keep, back_low)

def matmul_high(left, right):
    return jnp.matmul(left, right, precision=HIGHEST)

def row_scale(values):
    return lax.rsqrt(lax.optimization_barrier(jnp.mean(values * values, -1, keepdims=True)) + EPSILON)

def block_terms(keys, values, betas):
    size = keys.shape[-2]
    identity_mat = jnp.eye(size, dtype=jnp.float32)
    gram = jnp.einsum('...id,...jd->...ij', keys, keys, precision=HIGHEST)
    lower = jnp.tril(gram * betas[..., :, None], -1)
    inverse = identity_mat - lower
    power = lower
    covered = 2
    while covered < size:
        power = matmul_high(power, power)
        inverse = matmul_high(inverse, identity_mat + power)
        covered = covered * 2
    return (matmul_high(inverse, keys * betas[..., None]), matmul_high(inverse, values * betas[..., None]))

def block_advance(carried, queries, keys, values, betas):
    weighted_keys, weighted_values = block_terms(keys, values, betas)
    fresh = weighted_values - matmul_high(weighted_keys, carried)
    scores = jnp.tril(jnp.einsum('...id,...jd->...ij', queries, keys, precision=HIGHEST))
    output = matmul_high(queries, carried) + matmul_high(scores, fresh)
    carried = carried + matmul_high(jnp.swapaxes(keys, -1, -2), fresh)
    return (output, carried)

def project(rows, weight):
    return jnp.einsum('bsd,de->bse', rows, weight, precision=HIGHEST)

def forward(live_mask, tokens, mixer_gain, query_weight, key_weight, value_weight, beta_weight, beta_bias, conv_weight, head_gain, out_weight, feed_gain, gate_weight, up_weight, down_weight):
    seq_count, length, width = tokens.shape
    mixer_in = low(tokens * row_scale(tokens) * mixer_gain)
    projected = jnp.concatenate((low(project(mixer_in, query_weight)), low(project(mixer_in, key_weight)), low(project(mixer_in, value_weight))), -1)
    projected = low_back(projected)
    logits = low_back(project(mixer_in, beta_weight))
    taps = conv_weight.shape[1]
    lead = taps - 1
    conv_rows = conv_weight.transpose(1, 0, 2).reshape(taps, 3 * width)
    extended = jnp.pad(projected, ((0, 0), (lead, 0), (0, 0)))
    mixed = conv_rows[0] * extended[:, lead:lead + length]
    for offset in range(1, taps):
        mixed = mixed + conv_rows[offset] * extended[:, lead - offset:lead - offset + length]
    mixed = jax.nn.silu(mixed)
    head_count = width // HEAD_DIM
    block_count = length // BLOCK

    def to_blocks(values):
        shaped = values.reshape(seq_count, block_count, BLOCK, head_count, HEAD_DIM)
        return shaped.transpose(1, 0, 3, 2, 4)
    queries = mixed[..., :width]
    keys = mixed[..., width:2 * width].reshape(seq_count, length, head_count, HEAD_DIM)
    keys = keys * lax.rsqrt(lax.optimization_barrier(jnp.sum(keys * keys, -1, keepdims=True)) + 1e-06)
    values = mixed[..., 2 * width:]
    betas = jax.nn.sigmoid(logits + beta_bias) * live_mask[..., None]
    betas = betas.reshape(seq_count, block_count, BLOCK, head_count).transpose(1, 0, 3, 2)

    @jax.checkpoint
    def advance(carried, pieces):
        output, carried = block_advance(carried, pieces[0], pieces[1], pieces[2], pieces[3])
        return (carried, (output, jnp.sqrt(lax.optimization_barrier(jnp.sum(carried * carried, (-2, -1))))))
    start = jnp.zeros((seq_count, head_count, HEAD_DIM, HEAD_DIM), jnp.float32)
    final, (outputs, norms) = lax.scan(advance, start, (to_blocks(queries), to_blocks(keys), to_blocks(values), betas))
    outputs = outputs.transpose(1, 0, 3, 2, 4).reshape(seq_count, length, head_count, HEAD_DIM)
    head_rows = low((outputs * row_scale(outputs) * head_gain).reshape(seq_count, length, width))
    hidden_in = tokens + low_back(project(head_rows, out_weight))
    feed_in = low(hidden_in * row_scale(hidden_in) * feed_gain)
    gate_pre = low_back(project(feed_in, gate_weight))
    up_pre = low_back(project(feed_in, up_weight))
    hidden = low(jax.nn.silu(gate_pre) * up_pre)
    result = hidden_in + low_back(project(hidden, down_weight))
    stride = SEG // BLOCK
    return (result, jnp.mean(norms[stride - 1::stride]))

def reference(tokens, lengths, mixer_gain, query_weight, key_weight, value_weight, beta_weight, beta_bias, conv_weight, head_gain, out_weight, feed_gain, gate_weight, up_weight, down_weight, cotangent):
    length = tokens.shape[1]
    positions = jnp.arange(length, dtype=jnp.int32)
    live_mask = (positions[None, :] < lengths[:, None].astype(jnp.int32)).astype(jnp.float32)
    floats = tuple((argument.astype(jnp.float32) for argument in (tokens, mixer_gain, query_weight, key_weight, value_weight, beta_weight, beta_bias, conv_weight, head_gain, out_weight, feed_gain, gate_weight, up_weight, down_weight)))

    def evaluate(*params):
        return forward(live_mask, *params)
    result, pullback, state_norm = jax.vjp(evaluate, *floats, has_aux=True)
    grads = pullback(cotangent.astype(jnp.float32))
    return (result, grads[0], grads[1], grads[2], grads[3], grads[4], grads[5], grads[6], grads[7], grads[8], grads[9], grads[10], grads[11], grads[12], grads[13], state_norm)
```

```python
import functools

import jax
import jax.numpy as jnp
from jax import lax
from jax.experimental import pallas as pl
from jax.experimental.pallas import tpu as pltpu
from jax.sharding import PartitionSpec as P

HEADS = 16
HEAD_DIM = 128
NSEQ = 2
EPSILON = 1e-05
KEY_EPSILON = 1e-06
LANES = 128
LEAD = 8
EDGE = 16
BF = jnp.bfloat16
F32 = jnp.float32
MESH = pl.DeviceIdType.MESH
VMEM = pl.BlockSpec(memory_space=pltpu.VMEM)
SMEM = pl.BlockSpec(memory_space=pltpu.SMEM)
ANY = pl.BlockSpec(memory_space=pl.ANY)
NN = (((1,), (0,)), ((), ()))
NT = (((1,), (1,)), ((), ()))
TN = (((0,), (0,)), ((), ()))
DMA = pltpu.SemaphoreType.DMA


def dot(left, right, dims=NN):
    return lax.dot_general(left, right, dims, preferred_element_type=F32)


def halves(values):
    high = values.astype(BF)
    return high, (values - high.astype(F32)).astype(BF)


def fine(left, right, dims=NN):
    return (
        dot(left[0], right[0], dims)
        + dot(left[0], right[1], dims)
        + dot(left[1], right[0], dims)
    )


def row_scale(values):
    return lax.rsqrt(jnp.mean(values * values, -1, keepdims=True) + EPSILON)


def norm_backward(grad_normed, unit_rows, scale):
    return scale * (grad_normed - unit_rows * jnp.mean(grad_normed * unit_rows, -1, keepdims=True))


def sigmoid(values):
    return 1.0 / (1.0 + jnp.exp(-values))


def iota(shape, dim):
    return lax.broadcasted_iota(jnp.int32, shape, dim)


def lower_mask(size, strict):
    rows, cols = iota((size, size), 0), iota((size, size), 1)
    return rows > cols if strict else rows >= cols


def unit_lower_inverses(lowers):
    size = LANES
    rows, cols = iota((size, size), 0), iota((size, size), 1)
    eye = (rows == cols).astype(F32)
    blocks = [low[at : at + size, at : at + size] for low in lowers for at in (0, size)]
    base = 16
    same = (rows // base) == (cols // base)
    minus = [jnp.where(same, -block, 0.0) for block in blocks]
    inverses = [eye + one for one in minus]
    pairs = [halves(one) for one in minus]
    powers = [fine(pair, pair) for pair in pairs]
    covered = 2
    while covered * 2 < base:
        lefts = [halves(jnp.concatenate((i, p), 0)) for i, p in zip(inverses, powers)]
        both = [fine(left, (left[0][size:], left[1][size:])) for left in lefts]
        inverses = [i + b[:size] for i, b in zip(inverses, both)]
        powers = [b[size:] for b in both]
        covered *= 2
    inverses = [i + fine(halves(i), halves(p)) for i, p in zip(inverses, powers)]
    while base < size:
        joined = (rows // (2 * base)) == (cols // (2 * base))
        cross = jnp.logical_and(joined, jnp.logical_not(same))
        pairs = [halves(i) for i in inverses]
        inner = [fine(halves(jnp.where(cross, b, 0.0)), i) for b, i in zip(blocks, pairs)]
        inverses = [i - fine(p, halves(x)) for i, p, x in zip(inverses, pairs, inner)]
        same = joined
        base *= 2
    pairs = [halves(i) for i in inverses]
    corners = [fine(halves(low[size:, :size]), pairs[2 * k]) for k, low in enumerate(lowers)]
    corners = [-fine(pairs[2 * k + 1], halves(c)) for k, c in enumerate(corners)]
    zero = jnp.zeros((size, size), F32)
    return [
        jnp.concatenate(
            (
                jnp.concatenate((inverses[2 * k], zero), 1),
                jnp.concatenate((corner, inverses[2 * k + 1]), 1),
            ),
            0,
        )
        for k, corner in enumerate(corners)
    ]


def flip(index, mask):
    out = index
    bit = 1
    while bit <= mask:
        if mask & bit:
            out = out + bit * (1 - 2 * ((index // bit) % 2))
        bit *= 2
    return out


def bits_of(count):
    out = []
    bit = 1
    while bit < count:
        out.insert(0, bit)
        bit *= 2
    return out


def two_orders(bits):
    if len(bits) < 2:
        return (bits, bits)
    return (list(bits), [bits[1], bits[0]] + list(bits[2:]))


def spans(bits):
    masks = [0]
    for bit in bits:
        masks = masks + [mask ^ bit for mask in masks]
    return masks


def remote(src, dst, send, recv, target):
    return pltpu.make_async_remote_copy(
        src_ref=src,
        dst_ref=dst,
        send_sem=send,
        recv_sem=recv,
        device_id=target,
        device_id_type=MESH,
    )


def greet(targets):
    barrier = pltpu.get_barrier_semaphore()
    for target in targets:
        pl.semaphore_signal(barrier, inc=1, device_id=target, device_id_type=MESH)


def await_all(targets):
    pl.semaphore_wait(pltpu.get_barrier_semaphore(), len(targets))


def meet(targets):
    greet(targets)
    await_all(targets)


def line_mates(geo):
    s, m = geo.s, geo.m
    return [(s, (m + 1) % geo.nm), (s, (m + geo.nm - 1) % geo.nm)]


def cube_mates(geo):
    return [(flip(geo.s, bit), geo.m) for bit in bits_of(geo.ns)]


def all_mates(geo):
    return [((geo.s + k) % geo.ns, geo.m) for k in range(1, geo.ns)]


class Geo:
    def __init__(self, sizes):
        self.ns, self.nm = sizes
        self.s = lax.axis_index("seq")
        self.m = lax.axis_index("mp")


class CubeGather:
    @staticmethod
    def sems(ns):
        return [DMA((2, ns - 1)), DMA((2, ns - 1)), DMA(())]

    def __init__(self, geo, shard, full, sems):
        self.geo, self.shard, self.full = geo, shard, full
        self.send, self.recv, self.local = sems
        self.rows = shard.shape[0]
        self.orders = two_orders(bits_of(geo.ns))
        self.ids = {}
        for order, bits in enumerate(self.orders):
            count = 0
            for step in range(len(bits)):
                for mask in spans(bits[:step]):
                    self.ids[order, step, mask] = count
                    count += 1
        self.todo = sorted(self.ids, key=lambda key: (key[1], bin(key[2]).count("1"), key[2], key[0]))
        self.started = []

    def block(self, order, mask):
        half = self.rows // 2
        start = flip(self.geo.s, mask) * self.rows + order * half
        return self.full.at[pl.ds(pl.multiple_of(start, half), half)]

    def copy(self, order, step, mask, incoming=False):
        bit = self.orders[order][step]
        half = self.rows // 2
        place = self.block(order, mask ^ bit if incoming else mask)
        src = self.shard.at[pl.ds(order * half, half)] if mask == 0 and not incoming else place
        at = self.ids[order, step, mask]
        return remote(
            src, place, self.send.at[order, at], self.recv.at[order, at],
            (flip(self.geo.s, bit), self.geo.m),
        )

    def own(self):
        start = pl.multiple_of(self.geo.s * self.rows, self.rows)
        return pltpu.make_async_copy(self.shard, self.full.at[pl.ds(start, self.rows)], self.local)

    def begin(self, steps=None):
        depth = len(self.orders[0])
        for step in range(depth) if steps is None else steps:
            for order in range(2):
                self.copy(order, step, 0).start()
            if step == depth - 1:
                self.own().start()

    def advance(self, count=None):
        count = len(self.todo) if count is None else count
        for order, step, mask in self.todo[:count]:
            self.copy(order, step, mask, incoming=True).wait_recv()
            after = mask ^ self.orders[order][step]
            for later in range(step + 1, len(self.orders[order])):
                self.copy(order, later, after).start()
        self.todo = self.todo[count:]

    def settle(self):
        self.advance()
        self.own().wait()

    def finish(self):
        for order, step, mask in self.ids:
            self.copy(order, step, mask).wait_send()


class CubeScatter:
    @staticmethod
    def scratch(ns, rows, cols):
        return [pltpu.VMEM((2, ns - 1, rows // 2, cols), BF), DMA((2, ns - 1)), DMA((2, ns - 1))]

    def __init__(self, geo, total, scratch):
        self.geo, self.total = geo, total
        self.slots, self.send, self.recv = scratch
        self.half = self.slots.shape[2]
        self.orders = [list(reversed(bits)) for bits in two_orders(bits_of(geo.ns))]
        self.ids = {}
        for order, bits in enumerate(self.orders):
            count = 0
            for step in range(len(bits)):
                for mask in reversed(spans(bits[step + 1 :])):
                    self.ids[order, step, mask] = count
                    count += 1
        depth = len(self.orders[0])

        def urgency(key):
            order, step, mask = key
            ahead = [k for k in range(depth) if mask & self.orders[order][k]]
            return (step, ahead[0] if ahead else depth, -mask, order)

        self.todo = sorted(self.ids, key=urgency)

    def rows(self, order, mask):
        start = flip(self.geo.s, mask) * (2 * self.half) + order * self.half
        return pl.ds(pl.multiple_of(start, self.half), self.half)

    def copy(self, order, step, mask):
        bit = self.orders[order][step]
        at = self.ids[order, step, mask]
        return remote(
            self.total.at[self.rows(order, mask ^ bit)], self.slots.at[order, at],
            self.send.at[order, at], self.recv.at[order, at],
            (flip(self.geo.s, bit), self.geo.m),
        )

    def begin(self):
        for order, step, mask in self.todo:
            if step == 0:
                self.copy(order, 0, mask).start()

    def advance(self, count=None):
        count = len(self.todo) if count is None else count
        for order, step, mask in self.todo[:count]:
            self.copy(order, step, mask).wait_recv()
            if mask == 0 and step == len(self.orders[order]) - 1:
                continue
            rows = self.rows(order, mask)
            slot = self.slots[order, self.ids[order, step, mask]]
            self.total[rows, :] = (self.total[rows, :].astype(F32) + slot.astype(F32)).astype(BF)
            bits = self.orders[order]
            if step + 1 < len(bits) and mask & bits[step + 1]:
                self.copy(order, step + 1, mask ^ bits[step + 1]).start()
        self.todo = self.todo[count:]

    def finish(self, out):
        self.advance()
        for order in range(2):
            last = self.ids[order, len(self.orders[order]) - 1, 0]
            out[pl.ds(order * self.half, self.half), :] = self.total[self.rows(order, 0), :].astype(
                F32
            ) + self.slots[order, last].astype(F32)
        for order, step, mask in self.ids:
            self.copy(order, step, mask).wait_send()


class LineGather:
    @staticmethod
    def sems(nm):
        return [DMA((2, NSEQ, nm - 1)), DMA((2, NSEQ, nm - 1))]

    def __init__(self, geo, full, sems):
        self.geo, self.full = geo, full
        self.send, self.recv = sems
        self.span = full.shape[1] // geo.nm

    def place(self, piece, origin):
        return self.full.at[piece, pl.ds(pl.multiple_of(origin * self.span, self.span), self.span)]

    def copy(self, way, piece, hop, incoming=False):
        m = self.geo.m
        sign = 1 if way == 0 else -1
        origin = m - sign * (hop + (1 if incoming else 0))
        place = self.place(piece, origin)
        return remote(
            place, place, self.send.at[way, piece, hop], self.recv.at[way, piece, hop],
            (self.geo.s, m + sign),
        )

    def sends(self, way, hop):
        m, nm = self.geo.m, self.geo.nm
        if way == 0:
            return jnp.logical_and(m >= hop, m < nm - 1)
        return jnp.logical_and(m <= nm - 1 - hop, m > 0)

    def receives(self, way, hop):
        m, nm = self.geo.m, self.geo.nm
        return m >= hop + 1 if way == 0 else m <= nm - 2 - hop

    def begin(self, piece):
        for way in range(2):
            @pl.when(self.sends(way, 0))
            def _(way=way):
                self.copy(way, piece, 0).start()

    def advance(self, piece, hop):
        for way in range(2):
            @pl.when(self.receives(way, hop))
            def _(way=way):
                self.copy(way, piece, hop, incoming=True).wait_recv()

            if hop + 1 < self.geo.nm - 1:
                @pl.when(self.sends(way, hop + 1))
                def _(way=way):
                    self.copy(way, piece, hop + 1).start()

    def finish(self, piece):
        for way in range(2):
            for hop in range(self.geo.nm - 1):
                @pl.when(self.sends(way, hop))
                def _(way=way, hop=hop):
                    self.copy(way, piece, hop).wait_send()


class LineScatter:
    @staticmethod
    def scratch(nm, span, cols):
        return [
            pltpu.VMEM((2, NSEQ, nm, span, cols), BF),
            DMA((2, NSEQ, nm)),
            DMA((2, NSEQ, nm)),
        ]

    def __init__(self, geo, part, scratch):
        self.geo, self.part = geo, part
        self.slots, self.send, self.recv = scratch
        self.span = self.slots.shape[3]

    def place(self, way):
        return self.geo.m if way == 0 else self.geo.nm - 1 - self.geo.m

    def own(self, way, piece, block):
        at = self.geo.nm - 1 - block if way == 0 else block
        start = at * self.span
        if not isinstance(start, int):
            start = pl.multiple_of(start, self.span)
        return self.part.at[piece, pl.ds(start, self.span)]

    def copy(self, way, piece, block, first=False):
        slot = self.slots.at[way, piece, block]
        src = self.own(way, piece, block) if first else slot
        step = 1 if way == 0 else -1
        return remote(
            src, slot, self.send.at[way, piece, block], self.recv.at[way, piece, block],
            (self.geo.s, self.geo.m + step),
        )

    def begin(self, piece):
        for way in range(2):
            @pl.when(self.place(way) == 0)
            def _(way=way):
                self.copy(way, piece, 0, True).start()

    def advance(self, piece, turn):
        forward = turn <= self.geo.nm - 2
        for way in range(2):
            at = self.place(way)
            if forward:
                @pl.when(at == 0)
                def _(way=way):
                    self.copy(way, piece, turn - 1, True).wait_send()
                    self.copy(way, piece, turn, True).start()

            @pl.when(jnp.logical_and(at >= 1, at <= turn))
            def _(way=way, block=turn - at):
                self.copy(way, piece, block).wait_recv()
                if forward:
                    slot = self.slots.at[way, piece, block]
                    own = self.own(way, piece, block)
                    slot[...] = (slot[...].astype(F32) + own[...].astype(F32)).astype(BF)
                    self.copy(way, piece, block).start()

    def result(self, piece, out):
        m, nm = self.geo.m, self.geo.nm
        own = self.part[piece, pl.ds(pl.multiple_of(m * self.span, self.span), self.span), :]
        out[piece] = own.astype(F32)

        @pl.when(m >= 1)
        def _():
            out[piece] = out[piece] + self.slots[0, piece, nm - 1 - m].astype(F32)

        @pl.when(m <= nm - 2)
        def _():
            out[piece] = out[piece] + self.slots[1, piece, m].astype(F32)

    def finish(self, piece):
        nm = self.geo.nm
        for way in range(2):
            at = self.place(way)
            for block in range(nm - 1):
                first = 0 if block == nm - 2 else 1

                @pl.when(jnp.logical_and(at >= first, at <= nm - 2 - block))
                def _(way=way, block=block):
                    self.copy(way, piece, block).wait_send()


def comm_params(collective, limit=60):
    return pltpu.CompilerParams(
        collective_id=collective, has_side_effects=True, vmem_limit_bytes=limit * 2**20
    )


def load(pairs):
    for src, dst, sem in pairs:
        pltpu.make_async_copy(src, dst, sem).start()


def ready(pairs):
    for src, dst, sem in pairs:
        pltpu.make_async_copy(src, dst, sem).wait()


GROUP = 4


def conv_row(conv, group, tap, column):
    return conv[group, pl.ds(tap, 1), pl.ds(pl.multiple_of(column, LANES), LANES)]


def before_silu(extended, conv, piece, group, head, width, rank):
    span = extended.shape[1] - LEAD
    cols = pl.ds(pl.multiple_of(group * width + head * LANES, LANES), LANES)
    total = None
    for tap in range(4):
        term = conv_row(conv, group, tap, rank * width + head * LANES) * extended[
            piece, pl.ds(LEAD - tap, span), cols
        ]
        total = term if total is None else total + term
    return total


def strengths_of(geo, logits, lengths, bias, local_heads, piece):
    span = logits.shape[1]
    lane = iota((span, LANES), 1)
    offset = jnp.zeros((span, LANES), F32)
    for head in range(local_heads):
        offset = jnp.where(lane == head, bias[geo.m * local_heads + head], offset)
    position = geo.s * span + iota((span, LANES), 0)
    live = jnp.where(position < lengths[piece], 1.0, 0.0)
    return sigmoid(logits[piece] + offset), live


def column_of(values, head):
    return jnp.sum(jnp.where(iota(values.shape, 1) == head, values, 0.0), -1, keepdims=True)


def fill_extended(extended, projected, edge, piece):
    extended[piece, LEAD:, :] = projected[piece].astype(F32)
    extended[piece, :LEAD, :] = edge[piece, EDGE - LEAD :, :].astype(F32)


class Chains:
    @staticmethod
    def scratch(ns, chains):
        return [
            pltpu.VMEM((ns, LANES, LANES), F32),
            DMA((chains,)), DMA((ns,)), DMA((ns,)), DMA((chains,)),
        ]

    def __init__(self, geo, chains, pair, links, entries, scratch):
        self.geo, self.chains = geo, chains
        self.pair, self.links, self.entries = pair, links, entries
        self.states, self.pair_send, self.pair_recv, self.back_send, self.back_recv = scratch
        self.stride = geo.ns // chains
        self.mine = geo.s // self.stride
        self.holds = geo.s == self.mine * self.stride

    def link_copy(self, chain):
        s, m = self.geo.s, self.geo.m
        return remote(
            self.pair.at[chain], self.links.at[s], self.pair_send.at[chain], self.pair_recv.at[s],
            (chain * self.stride, m),
        )

    def give(self, chain, link):
        owner = chain * self.stride

        @pl.when(owner == self.geo.s)
        def _():
            self.links[self.geo.s] = link

        @pl.when(owner != self.geo.s)
        def _():
            self.link_copy(chain).start()

    def state_copy(self, other):
        return remote(
            self.states.at[other], self.entries.at[self.mine], self.back_send.at[other],
            self.back_recv.at[self.mine], (other, self.geo.m),
        )

    def run(self, first, count, advance, start, reverse, last):
        ns, s, m = self.geo.ns, self.geo.s, self.geo.m

        @pl.when(jnp.logical_and(self.holds, jnp.logical_and(self.mine >= first, self.mine < first + count)))
        def _():
            def step(lap, carry):
                at = ns - 1 - lap if reverse else lap
                state = carry[0]
                self.states[at] = state

                @pl.when(at == s)
                def _():
                    self.entries[self.mine] = state

                @pl.when(at != s)
                def _():
                    self.state_copy(at).start()
                    remote(
                        self.pair.at[0], self.links.at[at], self.pair_send.at[0],
                        self.pair_recv.at[at], (s, m),
                    ).wait_recv()

                return advance(carry, at)

            last(lax.fori_loop(0, ns, step, start))

    def receive(self, chain):
        @pl.when(chain * self.stride != self.geo.s)
        def _():
            remote(
                self.states.at[0], self.entries.at[chain], self.back_send.at[0],
                self.back_recv.at[chain], (self.geo.s, self.geo.m),
            ).wait_recv()

    def finish(self):
        def sent(chain, carry):
            @pl.when(chain * self.stride != self.geo.s)
            def _():
                self.link_copy(chain).wait_send()

            return carry

        lax.fori_loop(0, self.chains, sent, 0)

        @pl.when(self.holds)
        def _():
            def done(other, carry):
                @pl.when(other != self.geo.s)
                def _():
                    self.state_copy(other).wait_send()

                return carry

            lax.fori_loop(0, self.geo.ns, done, 0)


def mixer_kernel(
    sizes, tokens, cotangent, query_w, key_w, value_w, beta_w, out_in, gate_hbm, up_hbm, down_in,
    conv, lengths, bias, mixer_gain, head_gain, feed_gain,
    rows_o, proj_w_o, out_w_o, gate_w_o, up_w_o, down_w_o, grad_rows_o, feed_rows_o,
    hidden_in, head_rows, projected, logits, edge, links, norm_o, entry_o,
    solve_h, wkeys_h, fresh_h, error_h, outputs_h, queries_h, keys_h,
    solve_o, wkeys_o, fresh_o, error_o, outputs_o, queries_o, keys_o,
    proj_shard, out_shard, gate_shard, up_shard, down_shard,
    rows, weight, out_w, grad_rows, feed_rows, part, extended, betas, wvalues, pair,
    keep, edge_send, edge_recv, *rest,
):
    geo = Geo(sizes)
    ns, nm, s, m = geo.ns, geo.nm, geo.s, geo.m
    mates = line_mates(geo) + all_mates(geo)
    greet(mates)
    shards = [(gate_hbm, gate_shard, keep.at[0]), (up_hbm, up_shard, keep.at[1])]
    load(shards)
    width = query_w.shape[1]
    heads = width // LANES
    chains = NSEQ * heads
    span = projected.shape[1]
    proj_shard[:, 0:width] = query_w[...]
    proj_shard[:, width : 2 * width] = key_w[...]
    proj_shard[:, 2 * width : 3 * width] = value_w[...]
    proj_shard[:, 3 * width :] = jnp.zeros((proj_shard.shape[0], LANES), BF)
    proj_shard[:, 3 * width : 3 * width + heads] = beta_w[...]
    out_shard[...] = out_in[...].T
    await_all(mates)

    weights = CubeGather(geo, proj_shard, weight, rest[0:3])
    outs = CubeGather(geo, out_shard, out_w, rest[3:6])
    gates = CubeGather(geo, gate_shard, gate_w_o, rest[6:9])
    ups = CubeGather(geo, up_shard, up_w_o, rest[9:12])
    downs = CubeGather(geo, down_shard, down_w_o, rest[12:15])
    spread = LineGather(geo, rows, rest[15:17])
    spread_grad = LineGather(geo, grad_rows, rest[17:19])
    spread_feed = LineGather(geo, feed_rows, rest[19:21])
    collect = LineScatter(geo, part, rest[21:24])
    chain = Chains(geo, chains, pair, links, entry_o, rest[24:29])

    weights.begin()
    own_rows = tokens.shape[1]
    mine = pl.ds(pl.multiple_of(m * own_rows, own_rows), own_rows)
    for piece in range(NSEQ):
        values = tokens[piece].astype(F32)
        rows[piece, mine, :] = (values * row_scale(values) * mixer_gain[...]).astype(BF)
        grad_rows[piece, mine, :] = cotangent[piece]
        if piece == 0:
            spread.begin(0)
    down_shard[...] = down_in[...].T
    spread.advance(0, 0)
    spread.begin(1)
    weights.advance(2)
    outs.begin()
    for hop in range(1, nm - 1):
        spread.advance(0, hop)
        weights.advance(2)
        spread.advance(1, hop - 1)
    outs.advance(2)
    weights.settle()
    ready(shards)
    kept = [(weight, proj_w_o, keep.at[2])]
    load(kept)
    strict = lower_mask(span, True)
    whole = lower_mask(span, False)
    norm_o[...] = jnp.zeros(norm_o.shape, F32)

    def edge_copy(piece):
        return remote(
            projected.at[piece, pl.ds(span - EDGE, EDGE)], edge.at[piece],
            edge_send.at[piece], edge_recv.at[piece], (s + 1, m),
        )

    def run_chains(piece):
        def advance(carry, at):
            state, total = carry
            link = links[at]
            high, low = halves(state)
            move = link[:, :LANES]
            state = state - (dot(move, high) + dot(move, low)) + link[:, LANES:].astype(F32)
            return state, total + jnp.sqrt(jnp.sum(state * state, (0, 1), keepdims=True))

        def last(carry):
            norm_o[...] = norm_o[...] + carry[1]

        start = (jnp.zeros((LANES, LANES), F32), jnp.zeros((1, 1), F32))
        chain.run(piece * heads, heads, advance, start, False, last)

    groups = heads // GROUP

    def solve(piece, carry):
        @pl.when(piece == 1)
        def _():
            for hop in range(nm - 2, nm - 1):
                spread.advance(1, hop)

        result = dot(rows[piece], weight[...])
        projected[piece] = result[:, : 3 * width].astype(BF)
        logits[piece] = result[:, 3 * width :]

        @pl.when(s < ns - 1)
        def _():
            edge_copy(piece).start()

        strength, live = strengths_of(geo, logits, lengths, bias, heads, piece)
        betas[piece] = strength * live

        @pl.when(piece == 0)
        def _():
            gates.begin((0,))
            for at in range(NSEQ):
                spread_grad.begin(at)

        @pl.when(piece == 1)
        def _():
            gates.begin(range(1, len(gates.orders[0])))

        @pl.when(s > 0)
        def _():
            edge_copy(piece).wait_recv()

        @pl.when(s == 0)
        def _():
            edge[piece] = jnp.zeros(edge.shape[1:], BF)

        fill_extended(extended, projected, edge, piece)
        for first in range(0, heads, GROUP):
            which = [first + k for k in range(GROUP)]
            mixed = [
                [before_silu(extended, conv, piece, g, head, width, m) for g in range(3)]
                for head in which
            ]
            mixed = [[z * sigmoid(z) for z in three] for three in mixed]
            queries = [three[0] for three in mixed]
            keys = [
                key * lax.rsqrt(jnp.sum(key * key, -1, keepdims=True) + KEY_EPSILON)
                for _, key, _ in mixed
            ]
            values = [three[2] for three in mixed]
            strengths = [column_of(betas[piece], head) for head in which]
            key_pairs = [halves(key) for key in keys]
            grams = [jnp.where(strict, fine(key, key, NT), 0.0) for key in key_pairs]
            inverses = unit_lower_inverses([gram * beta for gram, beta in zip(grams, strengths)])
            both = [
                halves(jnp.concatenate((key * beta, value * beta), 1))
                for key, value, beta in zip(keys, values, strengths)
            ]
            both = [fine(halves(inverse), right) for inverse, right in zip(inverses, both)]
            found = [fine(key, halves(two), TN).astype(BF) for key, two in zip(key_pairs, both)]
            done = list(zip(queries, keys, values, inverses, both, found))
            for k, (query, key, value, inverse, both, link) in enumerate(done):
                at = piece * heads + first + k
                pair[at] = link
                solve_o[at] = inverse
                wkeys_o[at] = both[:, :LANES]
                wvalues[at] = both[:, LANES:]
                queries_o[at] = query
                keys_o[at] = key
                error_o[at] = value
            for k, found in enumerate(done):
                chain.give(piece * heads + first + k, found[-1])
        return carry

    lax.fori_loop(0, NSEQ, solve, 0)
    saved = [
        (solve_o, solve_h, keep.at[7]), (wkeys_o, wkeys_h, keep.at[8]),
        (queries_o, queries_h, keep.at[9]), (keys_o, keys_h, keep.at[10]),
    ]
    load(saved)
    for piece in range(NSEQ):
        spread_grad.advance(piece, 0)
    outs.settle()
    for piece in range(NSEQ):
        run_chains(piece)

    def gates_on():
        gates.advance(4)
        ups.begin()
        downs.begin()

    def apply(piece, then=None):
        def step(lap, carry):
            first = piece * heads + lap * GROUP
            for k in range(GROUP):
                chain.receive(first + k)
            if then is not None:
                then()
            which = [first + k for k in range(GROUP)]
            states = [halves(entry_o[at]) for at in which]
            key_pairs = [halves(keys_o[at]) for at in which]
            query_pairs = [halves(queries_o[at]) for at in which]
            fresh = [
                wvalues[at] - fine(halves(wkeys_o[at]), state) for at, state in zip(which, states)
            ]
            fresh_pairs = [halves(one) for one in fresh]
            grams = [jnp.where(strict, fine(key, key, NT), 0.0) for key in key_pairs]
            scores = [
                jnp.where(whole, fine(query, key, NT), 0.0)
                for query, key in zip(query_pairs, key_pairs)
            ]
            errors = [
                error_o[at] - fine(key, state) - fine(halves(gram), new)
                for at, key, state, gram, new in zip(which, key_pairs, states, grams, fresh_pairs)
            ]
            outputs = [
                fine(query, state) + fine(halves(score), new)
                for query, state, score, new in zip(query_pairs, states, scores, fresh_pairs)
            ]
            done = list(zip(fresh, errors, outputs))
            for k, (fresh, error, output) in enumerate(done):
                at = first + k
                fresh_o[at] = fresh
                error_o[at] = error
                outputs_o[at] = output
                cols = pl.ds(pl.multiple_of((lap * GROUP + k) * LANES, LANES), LANES)
                head_rows[piece, :, cols] = (output * row_scale(output) * head_gain[...]).astype(BF)
            return carry

        lax.fori_loop(0, groups, step, 0)
        part[piece] = dot(head_rows[piece], out_w[...], NT).astype(BF)

    def close(piece):
        collect.result(piece, hidden_in)
        values = hidden_in[piece] + tokens[piece].astype(F32)
        hidden_in[piece] = values
        feed_rows[piece, mine, :] = (values * row_scale(values) * feed_gain[...]).astype(BF)
        spread_feed.begin(piece)

    apply(0)
    collect.begin(0)
    for piece in range(NSEQ):
        spread_grad.advance(piece, 1)
    apply(1, gates_on)
    kept.append((out_w, out_w_o, keep.at[4]))
    later = [
        (fresh_o, fresh_h, keep.at[11]), (error_o, error_h, keep.at[12]),
        (outputs_o, outputs_h, keep.at[13]),
    ]
    load(kept[-1:] + later)
    collect.advance(0, 1)
    for piece in range(NSEQ):
        for hop in range(2, nm - 2):
            spread_grad.advance(piece, hop)
    collect.advance(0, 2)
    collect.begin(1)
    for turn in range(3, nm):
        collect.advance(0, turn)
    close(0)
    collect.advance(1, 1)
    gates.advance(2)
    spread_feed.advance(0, 0)
    collect.advance(1, 2)
    gates.advance()
    spread_feed.advance(0, 1)
    for turn in range(3, nm):
        collect.advance(1, turn)
    close(1)
    ups.advance(4)
    downs.advance(4)
    for hop in range(2, nm - 1):
        spread_feed.advance(0, hop)
    for piece in range(NSEQ):
        spread_grad.advance(piece, nm - 2)
    spread_feed.advance(1, 0)
    ups.advance(2)
    for hop in range(1, nm - 1):
        spread_feed.advance(1, hop)
    downs.advance(2)
    ups.advance()
    downs.advance()
    for piece in range(NSEQ):
        spread.finish(piece)
        collect.finish(piece)
        spread_grad.finish(piece)
        spread_feed.finish(piece)
    late = [
        (feed_rows, feed_rows_o, keep.at[5]), (grad_rows, grad_rows_o, keep.at[6]), (rows, rows_o, keep.at[3])
    ]
    load(late)
    for gather in (gates, ups, downs):
        gather.settle()
    for gather in (weights, outs, gates, ups, downs):
        gather.finish()
    for piece in range(NSEQ):
        @pl.when(s < ns - 1)
        def _(piece=piece):
            edge_copy(piece).wait_send()

    chain.finish()
    ready(kept + saved + later + late)


def mixer(
    sizes, tokens, cotangent, query_w, key_w, value_w, beta_w, out_in, gate_in, up_in, down_in,
    conv, lengths, bias, mixer_gain, head_gain, feed_gain,
):
    ns, nm = sizes
    width = query_w.shape[1]
    shard = query_w.shape[0]
    depth = ns * shard
    cols = gate_in.shape[1]
    own = tokens.shape
    span = own[1] * nm
    heads = width // LANES
    chains = NSEQ * heads
    rows = (NSEQ, span, depth)
    joined = 3 * width + LANES
    shape = jax.ShapeDtypeStruct
    per_chain = (chains, span, LANES)
    return pl.pallas_call(
        functools.partial(mixer_kernel, sizes),
        out_shape=(
            shape(rows, BF), shape((depth, joined), BF), shape((depth, width), BF),
            shape((depth, cols), BF), shape((depth, cols), BF), shape((depth, cols), BF),
            shape(rows, BF), shape(rows, BF),
            shape(own, F32), shape((NSEQ, span, width), BF), shape((NSEQ, span, 3 * width), BF),
            shape((NSEQ, span, LANES), F32), shape((NSEQ, EDGE, 3 * width), BF),
            shape((ns, LANES, 2 * LANES), BF), shape((8, LANES), F32),
            shape((chains, LANES, LANES), F32), shape((chains, span, span), F32),
        )
        + (shape(per_chain, F32),) * 6,
        in_specs=[VMEM] * 7 + [ANY, ANY, VMEM, VMEM, SMEM, SMEM, VMEM, VMEM, VMEM],
        out_specs=(ANY,) * 8 + (VMEM,) * 8 + (ANY,) * 7,
        scratch_shapes=[pltpu.VMEM((chains, span, span), F32)]
        + [pltpu.VMEM(per_chain, F32)] * 6
        + [
            pltpu.VMEM((shard, joined), BF), pltpu.VMEM((shard, width), BF),
            pltpu.VMEM((shard, cols), BF), pltpu.VMEM((shard, cols), BF), pltpu.VMEM((shard, cols), BF),
            pltpu.VMEM(rows, BF), pltpu.VMEM((depth, joined), BF), pltpu.VMEM((depth, width), BF),
            pltpu.VMEM(rows, BF), pltpu.VMEM(rows, BF), pltpu.VMEM(rows, BF),
            pltpu.VMEM((NSEQ, LEAD + span, 3 * width), F32),
            pltpu.VMEM((NSEQ, span, LANES), F32),
            pltpu.VMEM(per_chain, F32),
            pltpu.VMEM((chains, LANES, 2 * LANES), BF),
            DMA((14,)), DMA((NSEQ,)), DMA((NSEQ,)),
        ]
        + CubeGather.sems(ns) * 5
        + LineGather.sems(nm) * 3
        + LineScatter.scratch(nm, own[1], depth)
        + Chains.scratch(ns, chains),
        compiler_params=comm_params(0),
        name="mixer",
    )(
        tokens, cotangent, query_w, key_w, value_w, beta_w, out_in, gate_in, up_in, down_in,
        conv, lengths, bias, mixer_gain, head_gain, feed_gain,
    )


def feed_kernel(
    sizes, feed_rows, grad_rows, gate_hbm, up_hbm, down_hbm, hidden_in, gain, cotangent,
    grad_in, mix_rows_o, grad_gate_o, grad_up_o, grad_down_o, down_part_o, gain_o,
    gate_w, up_w, down_w, hidden, grad_gate, grad_up, part, mix_rows, keep, *rest,
):
    geo = Geo(sizes)
    nm = geo.nm
    weights = [
        (gate_hbm, gate_w, keep.at[0]), (up_hbm, up_w, keep.at[1]), (down_hbm, down_w, keep.at[2])
    ]
    load(weights)
    meet(line_mates(geo) + cube_mates(geo))
    collect = LineScatter(geo, part, rest[0:3])
    spread = LineGather(geo, mix_rows, rest[3:5])
    first = CubeScatter(geo, gate_w, rest[5:8])
    second = CubeScatter(geo, up_w, rest[8:11])
    for piece in range(NSEQ):
        if piece == 0:
            ready(weights[:1])
        gate = dot(feed_rows[piece], gate_w[...])
        if piece == 0:
            ready(weights[1:2])
        up = dot(feed_rows[piece], up_w[...])
        sig = sigmoid(gate)
        active = gate * sig
        hidden[piece] = (active * up).astype(BF)
        if piece == 0:
            ready(weights[2:3])
        grad_hidden = dot(grad_rows[piece], down_w[...])
        grad_gate[piece] = (grad_hidden * up * sig * (1.0 + gate * (1.0 - sig))).astype(BF)
        grad_up[piece] = (grad_hidden * active).astype(BF)
        part[piece] = (
            dot(grad_gate[piece], gate_w[...], NT) + dot(grad_up[piece], up_w[...], NT)
        ).astype(BF)
        if piece == 0:
            collect.begin(0)
    depth, cols = gate_w.shape
    tile = 512
    span = hidden_in.shape[1]
    mine = pl.ds(pl.multiple_of(geo.m * span, span), span)

    def weight_grad(rows, grads, out):
        def step(at, carry):
            window = pl.ds(pl.multiple_of(at * tile, tile), tile)
            total = dot(rows[0, :, window], grads[0], TN) + dot(rows[1, :, window], grads[1], TN)
            out[window, :] = total.astype(BF)
            return carry

        lax.fori_loop(0, depth // tile, step, 0)

    def close(piece):
        collect.result(piece, grad_in)
        grad_feed = grad_in[piece]
        rows = hidden_in[piece]
        scale = row_scale(rows)
        unit = rows * scale
        part_gain = jnp.sum(grad_feed * unit, 0, keepdims=True)
        if piece == 0:
            gain_o[...] = part_gain
        else:
            gain_o[...] = gain_o[...] + part_gain
        back = cotangent[piece].astype(F32) + norm_backward(grad_feed * gain[...], unit, scale)
        grad_in[piece] = back
        mix_rows[piece, mine, :] = back.astype(BF)
        spread.begin(piece)

    collect.advance(0, 1)
    weight_grad(feed_rows, grad_gate, gate_w)
    first.begin()
    collect.advance(0, 2)
    collect.begin(1)
    weight_grad(feed_rows, grad_up, up_w)
    first.advance(4)
    for turn in range(3, nm):
        collect.advance(0, turn)
    close(0)
    first.advance(4)
    collect.advance(1, 1)
    second.begin()
    spread.advance(0, 0)
    collect.advance(1, 2)
    second.advance(8)
    spread.advance(0, 1)
    first.advance(2)
    for turn in range(3, nm):
        collect.advance(1, turn)
    close(1)
    first.advance(2)
    for piece in range(NSEQ):
        collect.finish(piece)
        part[piece] = dot(hidden[piece], down_w[...], NT).astype(BF)
    later = [(part, down_part_o, keep.at[0])]
    load(later)
    for hop in range(2, nm - 1):
        spread.advance(0, hop)
    spread.advance(1, 0)
    weight_grad(grad_rows, hidden, down_w)
    later.append((down_w, grad_down_o, keep.at[1]))
    load(later[1:])
    second.advance(4)
    for hop in range(1, nm - 1):
        spread.advance(1, hop)
    for piece in range(NSEQ):
        spread.finish(piece)
    later.append((mix_rows, mix_rows_o, keep.at[2]))
    load(later[2:])
    first.finish(grad_gate_o)
    second.finish(grad_up_o)
    ready(later)


def feed(sizes, feed_rows, grad_rows, gate_w, up_w, down_w, hidden_in, gain, cotangent):
    ns, nm = sizes
    depth, cols = gate_w.shape
    span = hidden_in.shape[1]
    shard = depth // ns
    rows = (NSEQ, span * nm, depth)
    inner = (NSEQ, span * nm, cols)
    return pl.pallas_call(
        functools.partial(feed_kernel, sizes),
        out_shape=(
            jax.ShapeDtypeStruct((NSEQ, span, depth), F32),
            jax.ShapeDtypeStruct(rows, BF),
            jax.ShapeDtypeStruct((shard, cols), F32),
            jax.ShapeDtypeStruct((shard, cols), F32),
            jax.ShapeDtypeStruct((depth, cols), BF),
            jax.ShapeDtypeStruct(rows, BF),
            jax.ShapeDtypeStruct((1, depth), F32),
        ),
        in_specs=[VMEM, VMEM, ANY, ANY, ANY, VMEM, VMEM, VMEM],
        out_specs=(VMEM, ANY, VMEM, VMEM, ANY, ANY, VMEM),
        scratch_shapes=[
            pltpu.VMEM((depth, cols), BF), pltpu.VMEM((depth, cols), BF), pltpu.VMEM((depth, cols), BF),
            pltpu.VMEM(inner, BF), pltpu.VMEM(inner, BF), pltpu.VMEM(inner, BF),
            pltpu.VMEM(rows, BF), pltpu.VMEM(rows, BF), DMA((3,)),
        ]
        + LineScatter.scratch(nm, span, depth)
        + LineGather.sems(nm)
        + CubeScatter.scratch(ns, shard, cols) * 2,
        compiler_params=comm_params(1, 63),
        name="feed",
    )(feed_rows, grad_rows, gate_w, up_w, down_w, hidden_in, gain, cotangent)


def backward_kernel(
    sizes, mix_rows_h, out_weight_h, head_rows, projected, logits, conv, lengths, bias, gain,
    edge, links, solve_h, wkeys_h, fresh_h, error_h, outputs_h, queries_h, keys_h, entry,
    grad_down_hbm, down_part_hbm, hidden_in,
    grads_o, block_o, grad_out_o, grad_down_o, conv_o, gain_o, bias_o,
    mix_rows, out_weight, solve, fresh, error, queries, keys,
    extended, betas, grad_output, held, grad_mixed, grad_tail, grad_logit,
    pair, gathered, leaving, edge_out, edge_in, out_total, down_total, down_part, keep,
    edge_send, edge_recv, *rest,
):
    geo = Geo(sizes)
    ns, nm, s, m = geo.ns, geo.nm, geo.s, geo.m
    span, width = projected.shape[1], projected.shape[2] // 3
    heads = width // LANES
    chains = NSEQ * heads
    which = range(heads)
    mates = line_mates(geo) + all_mates(geo)
    greet(mates)
    loads = [
        (down_part_hbm, down_part, keep.at[0]), (grad_down_hbm, down_total, keep.at[1]),
        (mix_rows_h, mix_rows, keep.at[2]), (out_weight_h, out_weight, keep.at[3]),
        (outputs_h, grad_output, keep.at[4]), (queries_h, queries, keep.at[5]),
        (keys_h, keys, keep.at[6]), (wkeys_h, held, keep.at[7]),
        (fresh_h, fresh, keep.at[8]), (solve_h, solve, keep.at[9]), (error_h, error, keep.at[10]),
    ]
    load(loads)
    collect = LineScatter(geo, down_part, rest[0:3])
    first = CubeScatter(geo, down_total, rest[3:6])
    second = CubeScatter(geo, out_total, rest[6:9])
    chain = Chains(geo, chains, pair, gathered, leaving, rest[9:14])
    strict = lower_mask(span, True)
    whole = lower_mask(span, False)
    gain_o[...] = jnp.zeros(gain_o.shape, F32)
    conv_o[...] = jnp.zeros(conv_o.shape, F32)
    pad = grad_mixed.shape[1] - LEAD - span
    for piece in range(NSEQ):
        grad_mixed[piece, :LEAD, :] = jnp.zeros((LEAD, 3 * width), F32)
        grad_mixed[piece, LEAD + span :, :] = jnp.zeros((pad, 3 * width), F32)
        fill_extended(extended, projected, edge, piece)
        strength, live = strengths_of(geo, logits, lengths, bias, heads, piece)
        betas[piece] = strength * live
    await_all(mates)
    ready(loads[:2])
    for piece in range(NSEQ):
        collect.begin(piece)
    first.begin()
    ready(loads[2:8])

    def start(piece, carry):
        grad_head = dot(mix_rows[piece], out_weight[...])
        scaled = [grad_output[piece * heads + h] for h in which]
        scales = [row_scale(output) for output in scaled]
        units = [output * scale for output, scale in zip(scaled, scales)]
        grads = [grad_head[:, h * LANES : (h + 1) * LANES] for h in which]
        share = [jnp.sum(grad * unit, 0, keepdims=True) for grad, unit in zip(grads, units)]
        gain_o[...] = gain_o[...] + sum(share)
        grads = [
            norm_backward(grad * gain[...], unit, scale)
            for grad, unit, scale in zip(grads, units, scales)
        ]
        grad_pairs = [halves(grad) for grad in grads]
        query_pairs = [halves(queries[piece * heads + h]) for h in which]
        scores = [
            jnp.where(whole, fine(query, halves(keys[piece * heads + h]), NT), 0.0)
            for h, query in zip(which, query_pairs)
        ]
        spread = [fine(halves(score), grad, TN) for score, grad in zip(scores, grad_pairs)]
        found = [
            fine(query, grad, TN) - fine(halves(held[piece * heads + h]), halves(one), TN)
            for h, query, grad, one in zip(which, query_pairs, grad_pairs, spread)
        ]
        found = [link.astype(BF) for link in found]
        for h in which:
            at = piece * heads + h
            grad_output[at] = grads[h]
            held[at] = spread[h]
            pair[at] = found[h]
        for h in which:
            chain.give(piece * heads + h, found[h])
        return carry

    lax.fori_loop(0, NSEQ, start, 0)
    ready(loads[8:])

    def through_conv(piece, h, group, grad, key=None):
        z = before_silu(extended, conv, piece, group, h, width, m)
        sig = sigmoid(z)
        if key is not None:
            raw = z * sig
            scale = lax.rsqrt(jnp.sum(raw * raw, -1, keepdims=True) + KEY_EPSILON)
            grad = scale * (grad - key * jnp.sum(key * grad, -1, keepdims=True))
        grad = grad * sig * (1.0 + z * (1.0 - sig))
        cols = slice(group * width + h * LANES, group * width + (h + 1) * LANES)
        local = slice(h * LANES, (h + 1) * LANES)
        grad_mixed[piece, pl.ds(LEAD, span), cols] = grad
        back = None
        for tap in range(4):
            share = jnp.sum(grad * extended[piece, pl.ds(LEAD - tap, span), cols], 0, keepdims=True)
            row = slice(group * 4 + tap, group * 4 + tap + 1)
            conv_o[row, local] = conv_o[row, local] + share
            term = (
                conv_row(conv, group, tap, m * width + h * LANES)
                * grad_mixed[piece, pl.ds(tap, LEAD + span), cols]
            )
            back = term if back is None else back + term
        edge_out[piece, :, cols] = back[:LEAD]
        grads_o[piece, :, cols] = back[LEAD:].astype(BF)
        grad_tail[piece, :, cols] = back[LEAD + span - EDGE :]

    def before_exit(piece):
        base = piece * heads
        grad_pairs = [halves(grad_output[base + h]) for h in which]
        key_pairs = [halves(keys[base + h]) for h in which]
        scores = [
            halves(jnp.where(whole, fine(grad, halves(fresh[base + h]), NT), 0.0))
            for h, grad in zip(which, grad_pairs)
        ]
        grads = [
            fine(score, key) + fine(grad, halves(entry[base + h]), NT)
            for h, score, key, grad in zip(which, scores, key_pairs, grad_pairs)
        ]
        to_keys = [
            fine(score, halves(queries[base + h]), TN) for h, score in zip(which, scores)
        ]
        for h in which:
            grad_output[base + h] = to_keys[h]
        for h in which:
            through_conv(piece, h, 0, grads[h])

    def after_exit(piece):
        base = piece * heads
        for h in which:
            chain.receive(base + h)
        key_pairs = [halves(keys[base + h]) for h in which]
        exits = [halves(leaving[base + h]) for h in which]
        fresh_pairs = [halves(fresh[base + h]) for h in which]
        strengths = [column_of(betas[piece], h) for h in which]
        weak = [halves(held[base + h] + fine(key, out)) for h, key, out in zip(which, key_pairs, exits)]
        weak = [fine(halves(solve[base + h]), one, TN) for h, one in zip(which, weak)]
        grad_beta = [jnp.sum(one * error[base + h], -1, keepdims=True) for h, one in zip(which, weak)]
        values = [one * beta for one, beta in zip(weak, strengths)]
        value_pairs = [halves(value) for value in values]
        scores = [
            halves(jnp.where(strict, -fine(value, new, NT), 0.0))
            for value, new in zip(value_pairs, fresh_pairs)
        ]
        grads = [
            grad_output[base + h]
            - fine(value, halves(entry[base + h]), NT)
            + fine(score, key)
            + fine(score, key, TN)
            + fine(new, out, NT)
            for h, value, score, key, new, out in zip(
                which, value_pairs, scores, key_pairs, fresh_pairs, exits
            )
        ]
        lane = iota((span, LANES), 1)
        grad_logit[piece] = sum(jnp.where(lane == h, grad_beta[h], 0.0) for h in which)
        for h in which:
            through_conv(piece, h, 1, grads[h], keys[base + h])
            through_conv(piece, h, 2, values[h])

    def run_chains(piece):
        def advance(carry, at):
            (state,) = carry
            high, low = halves(state)
            move = links[at][:, :LANES]
            state = state - (dot(move, high, TN) + dot(move, low, TN)) + gathered[at].astype(F32)
            return (state,)

        chain.run(
            piece * heads, heads, advance, (jnp.zeros((LANES, LANES), F32),), True, lambda carry: None
        )

    def edge_copy(piece):
        return remote(
            edge_out.at[piece], edge_in.at[piece], edge_send.at[piece], edge_recv.at[piece],
            (s - 1, m),
        )

    depth = out_weight.shape[0]
    tile = 512

    def weight_grad(at, carry):
        window = pl.ds(pl.multiple_of(at * tile, tile), tile)
        total = dot(mix_rows[0, :, window], head_rows[0], TN) + dot(
            mix_rows[1, :, window], head_rows[1], TN
        )
        out_total[window, :] = total.astype(BF)
        return carry

    def leave(piece, carry):
        @pl.when(piece == 0)
        def _():
            first.advance(8)

        before_exit(piece)

        @pl.when(piece == 0)
        def _():
            for at in range(NSEQ):
                run_chains(at)
            for at in range(NSEQ):
                collect.advance(at, 1)
            lax.fori_loop(0, depth // tile, weight_grad, 0)
            second.begin()

        return carry

    lax.fori_loop(0, NSEQ, leave, 0)

    def enter(piece, carry):
        after_exit(piece)

        @pl.when(s > 0)
        def _():
            edge_copy(piece).start()

        @pl.when(piece == 0)
        def _():
            for at in range(NSEQ):
                collect.advance(at, 2)
            second.advance(8)
            first.advance(4)

        return carry

    lax.fori_loop(0, NSEQ, enter, 0)
    bias_sum = jnp.zeros((1, LANES), F32)
    for piece in range(NSEQ):
        sig, live = strengths_of(geo, logits, lengths, bias, heads, piece)
        grad = grad_logit[piece] * live * sig * (1.0 - sig)
        bias_sum = bias_sum + jnp.sum(grad, 0, keepdims=True)
        grads_o[piece, :, pl.ds(3 * width, LANES)] = grad.astype(BF)
    lane = iota((1, LANES), 1)
    spread_bias = jnp.zeros((1, LANES), F32)
    for h in which:
        spread_bias = spread_bias + jnp.where(lane == m * heads + h, column_of(bias_sum, h), 0.0)
    bias_o[...] = spread_bias
    second.advance(4)
    for turn in range(3, nm):
        for piece in range(NSEQ):
            collect.advance(piece, turn)
    for piece in range(NSEQ):
        collect.result(piece, block_o)
        block_o[piece] = block_o[piece] + hidden_in[piece]
        collect.finish(piece)

    for piece in range(NSEQ):
        @pl.when(s < ns - 1)
        def _(piece=piece):
            edge_copy(piece).wait_recv()
            tail = pl.ds(EDGE - LEAD, LEAD)
            grad_tail[piece, tail, :] = grad_tail[piece, tail, :] + edge_in[piece]
            grads_o[piece, pl.ds(span - EDGE, EDGE), pl.ds(0, 3 * width)] = grad_tail[piece].astype(BF)

        @pl.when(s > 0)
        def _(piece=piece):
            edge_copy(piece).wait_send()

    first.finish(grad_down_o)
    second.finish(grad_out_o)
    chain.finish()


def backward(
    sizes, mix_rows, out_weight, head_rows, projected, logits, conv, lengths, bias, gain, saved,
    grad_down, down_part, hidden_in,
):
    ns, nm = sizes
    span, width = projected.shape[1], projected.shape[2] // 3
    heads = width // LANES
    chains = NSEQ * heads
    depth, cols = grad_down.shape
    shard = depth // ns
    local = hidden_in.shape
    rows = (NSEQ, span, depth)
    per_chain = (chains, span, LANES)
    return pl.pallas_call(
        functools.partial(backward_kernel, sizes),
        out_shape=(
            jax.ShapeDtypeStruct((NSEQ, span, 3 * width + LANES), BF),
            jax.ShapeDtypeStruct(local, F32),
            jax.ShapeDtypeStruct((shard, width), F32),
            jax.ShapeDtypeStruct((shard, cols), F32),
            jax.ShapeDtypeStruct((12, width), F32),
            jax.ShapeDtypeStruct((1, LANES), F32),
            jax.ShapeDtypeStruct((1, LANES), F32),
        ),
        in_specs=[ANY, ANY] + [VMEM] * 4 + [SMEM, SMEM] + [VMEM] * 3 + [ANY] * 7 + [VMEM, ANY, ANY, VMEM],
        out_specs=(VMEM,) * 7,
        scratch_shapes=[
            pltpu.VMEM(rows, BF), pltpu.VMEM((depth, width), BF),
            pltpu.VMEM((chains, span, span), F32),
        ]
        + [pltpu.VMEM(per_chain, F32)] * 4
        + [
            pltpu.VMEM((NSEQ, LEAD + span, 3 * width), F32),
            pltpu.VMEM((NSEQ, span, LANES), F32),
            pltpu.VMEM(per_chain, F32),
            pltpu.VMEM(per_chain, F32),
            pltpu.VMEM((NSEQ, LEAD + span + LEAD, 3 * width), F32),
            pltpu.VMEM((NSEQ, EDGE, 3 * width), F32),
            pltpu.VMEM((NSEQ, span, LANES), F32),
            pltpu.VMEM((chains, LANES, LANES), BF),
            pltpu.VMEM((ns, LANES, LANES), BF),
            pltpu.VMEM((chains, LANES, LANES), F32),
            pltpu.VMEM((NSEQ, LEAD, 3 * width), F32),
            pltpu.VMEM((NSEQ, LEAD, 3 * width), F32),
            pltpu.VMEM((depth, width), BF),
            pltpu.VMEM((depth, cols), BF),
            pltpu.VMEM(rows, BF),
            DMA((11,)), DMA((NSEQ,)), DMA((NSEQ,)),
        ]
        + LineScatter.scratch(nm, local[1], depth)
        + CubeScatter.scratch(ns, shard, cols)
        + CubeScatter.scratch(ns, shard, width)
        + Chains.scratch(ns, chains),
        compiler_params=comm_params(2, 63),
        name="recurrence_back",
    )(
        mix_rows, out_weight, head_rows, projected, logits, conv, lengths, bias, gain, *saved,
        grad_down, down_part, hidden_in,
    )


def last_kernel(
    sizes, rows, grads, proj_w, tokens, gain, grad_in, conv_part, head_gain, bias, norms, feed_gain,
    grad_tokens, grad_weight_o, conv_o, head_gain_o, bias_o, norm_o, feed_gain_o, gain_o,
    part, total, vector, over_seq, over_mp,
    seq_send, seq_recv, mp_send, mp_recv, *rest,
):
    geo = Geo(sizes)
    ns, nm, s, m = geo.ns, geo.nm, geo.s, geo.m
    mates = [(s, (m + k) % nm) for k in range(1, nm)] + all_mates(geo)
    greet(mates)
    depth = proj_w.shape[0]
    width = vector.shape[1]
    wide = depth // width
    row = conv_part.shape[0]
    vector[...] = jnp.zeros(vector.shape, F32)
    vector[0:row, :] = conv_part[...]
    vector[row : row + 1, 0:LANES] = head_gain[...]
    vector[row : row + 1, LANES : 2 * LANES] = bias[...]
    vector[row : row + 1, 2 * LANES : 3 * LANES] = norms[0:1, :]
    for at in range(wide):
        vector[row + 1 + at : row + 2 + at, :] = feed_gain[:, at * width : (at + 1) * width]
    await_all(mates)
    collect = LineScatter(geo, part, rest[0:3])
    scatter = CubeScatter(geo, total, rest[3:6])
    shares = []

    def spread(piece):
        value = dot(grads[piece], proj_w[...], NT)
        part[piece] = value.astype(BF)
        collect.begin(piece)
        shares.append(jnp.sum(value * rows[piece].astype(F32), 0, keepdims=True))

    tile = 512

    def weight_grad(at, carry):
        window = pl.ds(pl.multiple_of(at * tile, tile), tile)
        value = dot(rows[0, :, window], grads[0], TN) + dot(rows[1, :, window], grads[1], TN)
        total[window, :] = value.astype(BF)
        return carry

    spread(0)
    lax.fori_loop(0, depth // tile, weight_grad, 0)
    scatter.begin()
    spread(1)
    share = (shares[0] + shares[1]) / gain[...]
    for at in range(wide):
        vector[row + 1 + wide + at : row + 2 + wide + at, :] = share[:, at * width : (at + 1) * width]

    def seq_copy(k):
        return remote(
            vector, over_seq.at[k], seq_send.at[k], seq_recv.at[k], ((s + 1 + k) % ns, m)
        )

    def mp_copy(k):
        return remote(
            over_mp.at[0], over_mp.at[1 + k], mp_send.at[k], mp_recv.at[k], (s, (m + 1 + k) % nm)
        )

    def seq_start(k, carry):
        seq_copy(k).start()
        return carry

    lax.fori_loop(0, ns - 1, seq_start, 0)
    collect.advance(0, 1)
    scatter.advance(8)

    def seq_add(k, value):
        seq_copy(k).wait_recv()
        return value + over_seq[k]

    over_mp[0] = lax.fori_loop(0, ns - 1, seq_add, vector[...])
    for k in range(nm - 1):
        mp_copy(k).start()
    collect.advance(1, 1)
    for turn in range(2, nm):
        for piece in range(NSEQ):
            collect.advance(piece, turn)
        if turn == 2:
            for k in range(nm - 1):
                mp_copy(k).wait_recv()
            scatter.advance(2)
    for piece in range(NSEQ):
        collect.result(piece, grad_tokens)
        values = tokens[piece].astype(F32)
        scale = row_scale(values)
        grad_tokens[piece] = grad_in[piece] + norm_backward(
            grad_tokens[piece] * gain[...], values * scale, scale
        )
        collect.finish(piece)
    for k in range(nm):
        origin = (m + nm - k) % nm
        cols = pl.ds(pl.multiple_of(origin * width, width), width)
        for group in range(3):
            for tap in range(4):
                at = group * 4 + tap
                conv_o[group, tap : tap + 1, cols] = over_mp[k, at : at + 1, :]
    summed = over_mp[0]
    for k in range(1, nm):
        summed = summed + over_mp[k]
    head_gain_o[...] = summed[row : row + 1, 0:LANES]
    bias_o[...] = summed[row : row + 1, LANES : 2 * LANES]
    norm_o[...] = summed[row : row + 1, 2 * LANES : 3 * LANES] / (NSEQ * HEADS * ns)
    for at in range(wide):
        cols = slice(at * width, (at + 1) * width)
        feed_gain_o[:, cols] = summed[row + 1 + at : row + 2 + at, :]
        gain_o[:, cols] = summed[row + 1 + wide + at : row + 2 + wide + at, :]
    scatter.finish(grad_weight_o)

    def seq_done(k, carry):
        seq_copy(k).wait_send()
        return carry

    lax.fori_loop(0, ns - 1, seq_done, 0)
    for k in range(nm - 1):
        mp_copy(k).wait_send()


def last(sizes, rows, grads, proj_w, tokens, gain, grad_in, small):
    ns, nm = sizes
    depth, cols = proj_w.shape
    span = tokens.shape[1]
    shard = depth // ns
    width = (cols - LANES) // 3
    vector = (-(-(13 + 2 * (depth // width)) // 8) * 8, width)
    shape = jax.ShapeDtypeStruct
    line = shape((1, LANES), F32)
    return pl.pallas_call(
        functools.partial(last_kernel, sizes),
        out_shape=(
            shape(grad_in.shape, F32), shape((shard, cols), F32), shape((3, 4, depth), F32),
            line, line, line, shape((1, depth), F32), shape((1, depth), F32),
        ),
        in_specs=[VMEM] * 11,
        out_specs=(VMEM,) * 8,
        scratch_shapes=[
            pltpu.VMEM(rows.shape, BF),
            pltpu.VMEM((depth, cols), BF),
            pltpu.VMEM(vector, F32),
            pltpu.VMEM((ns - 1,) + vector, F32),
            pltpu.VMEM((nm,) + vector, F32),
            DMA((ns - 1,)), DMA((ns - 1,)), DMA((nm - 1,)), DMA((nm - 1,)),
        ]
        + LineScatter.scratch(nm, span, depth)
        + CubeScatter.scratch(ns, shard, cols),
        compiler_params=comm_params(3),
        name="last",
    )(rows, grads, proj_w, tokens, gain, grad_in, *small)


def deliver_kernel(
    block, grad_tokens, grad_proj, grad_gate, grad_up, grad_down, grad_out, conv, *rest
):
    lines, rest = rest[:5], rest[5:]
    (
        block_o, grad_tokens_o, query_o, key_o, value_o, grad_gate_o, grad_up_o, beta_o, grad_down_o,
        grad_out_o, conv_o,
    ) = rest[:11]
    line_os, rest = rest[11:16], rest[16:]
    block_v, tokens_v, proj_v, gate_v, up_v, down_v, out_v, down_t, out_t, conv_v = rest[:10]
    line_vs, sems = rest[10:15], rest[15]
    width = query_o.shape[1]
    coming = [
        (src, held, sems.at[k])
        for k, (src, held) in enumerate(
            (
                (grad_down, down_v), (grad_out, out_v), (grad_gate, gate_v), (grad_up, up_v),
                (block, block_v), (grad_tokens, tokens_v), (grad_proj, proj_v), (conv, conv_v),
            )
            + tuple(zip(lines, line_vs))
        )
    ]
    load(coming)
    going = []

    def send(held, dst):
        going.append((held, dst, sems.at[len(coming) + len(going)]))
        load(going[-1:])

    ready(coming[0:2])
    down_t[...] = down_v[...].T
    send(down_t, grad_down_o)
    out_t[...] = out_v[...].T
    send(out_t, grad_out_o)
    ready(coming[2:6])
    send(gate_v, grad_gate_o)
    send(up_v, grad_up_o)
    send(block_v, block_o)
    send(tokens_v, grad_tokens_o)
    ready(coming[6:])
    for k, dst in enumerate((query_o, key_o, value_o)):
        send(proj_v.at[:, pl.ds(k * width, width)], dst)
    beta_o[...] = proj_v[:, 3 * width :].T[: beta_o.shape[0], :]
    conv_o[...] = conv_v[...]
    for line, dst in zip(line_vs, line_os):
        dst[...] = line[:, : dst.shape[1]]
    ready(going)


def deliver(block, grad_tokens, grad_proj, grad_gate, grad_up, grad_down, grad_out, conv, lines, counts):
    shard, cols = grad_gate.shape
    width = (grad_proj.shape[1] - LANES) // 3
    heads = width // LANES
    shape = jax.ShapeDtypeStruct
    square = shape((shard, width), F32)
    wide = shape((shard, cols), F32)
    there = pl.BlockSpec(memory_space=pltpu.HBM)
    held = [
        block.shape, grad_tokens.shape, grad_proj.shape, (shard, cols), (shard, cols), (shard, cols),
        (shard, width), (cols, shard), (width, shard), conv.shape,
    ] + [line.shape for line in lines]
    return pl.pallas_call(
        deliver_kernel,
        out_shape=(
            shape(block.shape, F32), shape(grad_tokens.shape, F32), square, square, square, wide, wide,
            shape((heads, shard), F32), shape((cols, shard), F32), shape((width, shard), F32),
            shape(conv.shape, F32),
        )
        + tuple(shape((1, count), F32) for count in counts),
        in_specs=[there] * 13,
        out_specs=(there,) * 7 + (VMEM, there, there) + (VMEM,) * 6,
        scratch_shapes=[pltpu.VMEM(dims, F32) for dims in held] + [DMA((24,))],
        compiler_params=pltpu.CompilerParams(vmem_limit_bytes=63 * 2**20),
        name="deliver",
    )(block, grad_tokens, grad_proj, grad_gate, grad_up, grad_down, grad_out, conv, *lines)


def on_device(
    sizes,
    tokens,
    lengths,
    mixer_gain,
    query_weight,
    key_weight,
    value_weight,
    beta_weight,
    beta_bias,
    conv_weight,
    head_gain,
    out_weight,
    feed_gain,
    gate_weight,
    up_weight,
    down_weight,
    cotangent,
):
    ns, nm = sizes
    depth = tokens.shape[2]
    width = query_weight.shape[1]
    heads = width // LANES
    mixer_gain_row = mixer_gain.reshape(1, depth)
    feed_gain_row = feed_gain.reshape(1, depth)
    head_gain_row = head_gain.reshape(1, LANES)
    (
        rows, proj_w, out_w, gate_w, up_w, down_w, grad_rows, feed_rows,
        hidden_in, head_rows, projected, logits, edge, links, norms, entry, *saved,
    ) = mixer(
        sizes, tokens, cotangent, query_weight, key_weight, value_weight, beta_weight, out_weight,
        gate_weight, up_weight, down_weight, conv_weight, lengths, beta_bias, mixer_gain_row,
        head_gain_row, feed_gain_row,
    )
    grad_in, mix_rows, grad_gate, grad_up, grad_down_part, down_part, feed_gain_part = feed(
        sizes, feed_rows, grad_rows, gate_w, up_w, down_w, hidden_in, feed_gain_row, cotangent
    )
    grads, block_output, grad_out, grad_down, conv_part, gain_part, bias_part = backward(
        sizes, mix_rows, out_w, head_rows, projected, logits, conv_weight, lengths, beta_bias,
        head_gain_row, (edge, links, *saved, entry), grad_down_part, down_part, hidden_in,
    )
    grad_tokens, grad_proj_w, conv_grad, gain_grad, bias_grad, norm, feed_gain_grad, mixer_grad = last(
        sizes, rows, grads, proj_w, tokens, mixer_gain_row, grad_in,
        (conv_part, gain_part, bias_part, norms, feed_gain_part),
    )
    (
        block_output, grad_tokens, grad_query, grad_key, grad_value, grad_gate, grad_up, grad_beta,
        grad_down, grad_out, conv_grad, mixer_grad, feed_gain_grad, gain_grad, bias_grad, norm,
    ) = deliver(
        block_output, grad_tokens, grad_proj_w, grad_gate, grad_up, grad_down, grad_out, conv_grad,
        (mixer_grad, feed_gain_grad, gain_grad, bias_grad, norm), (depth, depth, LANES, nm * heads, 1),
    )
    return (
        block_output,
        grad_tokens,
        mixer_grad.reshape(depth),
        grad_query,
        grad_key,
        grad_value,
        grad_beta.T,
        bias_grad.reshape(nm * heads),
        conv_grad,
        gain_grad.reshape(LANES),
        grad_out,
        feed_gain_grad.reshape(depth),
        grad_gate,
        grad_up,
        grad_down,
        norm[0, 0],
    )


def solution(mesh):
    sizes = (mesh.shape["seq"], mesh.shape["mp"])
    by_rows = P("seq", "mp")
    by_cols = P("mp", "seq")
    placed = P(None, ("seq", "mp"), None)
    return jax.shard_map(
        functools.partial(on_device, sizes),
        mesh=mesh,
        in_specs=(
            placed, P(), P(), by_rows, by_rows, by_rows, by_rows, P(), P(), P(), by_cols, P(),
            by_rows, by_rows, by_cols, placed,
        ),
        out_specs=(
            placed, placed, P(), by_rows, by_rows, by_rows, by_rows, P(), P(), P(), by_cols, P(),
            by_rows, by_rows, by_cols, P(),
        ),
        check_vma=False,
    )
```

```python
import functools

import jax
import jax.numpy as jnp
from jax import lax
from jax.experimental import pallas as pl
from jax.experimental.pallas import tpu as pltpu
from jax.sharding import PartitionSpec as P

HEADS = 16
HEAD_DIM = 128
NSEQ = 2
EPSILON = 1e-05
KEY_EPSILON = 1e-06
LANES = 128
LEAD = 8
EDGE = 16
BF = jnp.bfloat16
F32 = jnp.float32
MESH = pl.DeviceIdType.MESH
VMEM = pl.BlockSpec(memory_space=pltpu.VMEM)
SMEM = pl.BlockSpec(memory_space=pltpu.SMEM)
ANY = pl.BlockSpec(memory_space=pl.ANY)
NN = (((1,), (0,)), ((), ()))
NT = (((1,), (1,)), ((), ()))
TN = (((0,), (0,)), ((), ()))
DMA = pltpu.SemaphoreType.DMA


def dot(left, right, dims=NN):
    return lax.dot_general(left, right, dims, preferred_element_type=F32)


def halves(values):
    high = values.astype(BF)
    return high, (values - high.astype(F32)).astype(BF)


def fine(left, right, dims=NN):
    return (
        dot(left[0], right[0], dims)
        + dot(left[0], right[1], dims)
        + dot(left[1], right[0], dims)
    )


def row_scale(values):
    return lax.rsqrt(jnp.mean(values * values, -1, keepdims=True) + EPSILON)


def norm_backward(grad_normed, unit_rows, scale):
    return scale * (grad_normed - unit_rows * jnp.mean(grad_normed * unit_rows, -1, keepdims=True))


def sigmoid(values):
    return 1.0 / (1.0 + jnp.exp(-values))


def iota(shape, dim):
    return lax.broadcasted_iota(jnp.int32, shape, dim)


def lower_mask(size, strict):
    rows, cols = iota((size, size), 0), iota((size, size), 1)
    return rows > cols if strict else rows >= cols


def unit_lower_inverses(lowers):
    size = LANES
    rows, cols = iota((size, size), 0), iota((size, size), 1)
    eye = (rows == cols).astype(F32)
    blocks = [low[at : at + size, at : at + size] for low in lowers for at in (0, size)]
    base = 16
    same = (rows // base) == (cols // base)
    minus = [jnp.where(same, -block, 0.0) for block in blocks]
    inverses = [eye + one for one in minus]
    pairs = [halves(one) for one in minus]
    powers = [fine(pair, pair) for pair in pairs]
    covered = 2
    while covered * 2 < base:
        lefts = [halves(jnp.concatenate((i, p), 0)) for i, p in zip(inverses, powers)]
        both = [fine(left, (left[0][size:], left[1][size:])) for left in lefts]
        inverses = [i + b[:size] for i, b in zip(inverses, both)]
        powers = [b[size:] for b in both]
        covered *= 2
    inverses = [i + fine(halves(i), halves(p)) for i, p in zip(inverses, powers)]
    while base < size:
        joined = (rows // (2 * base)) == (cols // (2 * base))
        cross = jnp.logical_and(joined, jnp.logical_not(same))
        pairs = [halves(i) for i in inverses]
        inner = [fine(halves(jnp.where(cross, b, 0.0)), i) for b, i in zip(blocks, pairs)]
        inverses = [i - fine(p, halves(x)) for i, p, x in zip(inverses, pairs, inner)]
        same = joined
        base *= 2
    pairs = [halves(i) for i in inverses]
    corners = [fine(halves(low[size:, :size]), pairs[2 * k]) for k, low in enumerate(lowers)]
    corners = [-fine(pairs[2 * k + 1], halves(c)) for k, c in enumerate(corners)]
    zero = jnp.zeros((size, size), F32)
    return [
        jnp.concatenate(
            (
                jnp.concatenate((inverses[2 * k], zero), 1),
                jnp.concatenate((corner, inverses[2 * k + 1]), 1),
            ),
            0,
        )
        for k, corner in enumerate(corners)
    ]


def flip(index, mask):
    out = index
    bit = 1
    while bit <= mask:
        if mask & bit:
            out = out + bit * (1 - 2 * ((index // bit) % 2))
        bit *= 2
    return out


def bits_of(count):
    out = []
    bit = 1
    while bit < count:
        out.insert(0, bit)
        bit *= 2
    return out


def two_orders(bits):
    if len(bits) < 2:
        return (bits, bits)
    return (list(bits), [bits[1], bits[0]] + list(bits[2:]))


def spans(bits):
    masks = [0]
    for bit in bits:
        masks = masks + [mask ^ bit for mask in masks]
    return masks


def remote(src, dst, send, recv, target):
    return pltpu.make_async_remote_copy(
        src_ref=src,
        dst_ref=dst,
        send_sem=send,
        recv_sem=recv,
        device_id=target,
        device_id_type=MESH,
    )


def greet(targets):
    barrier = pltpu.get_barrier_semaphore()
    for target in targets:
        pl.semaphore_signal(barrier, inc=1, device_id=target, device_id_type=MESH)


def await_all(targets):
    pl.semaphore_wait(pltpu.get_barrier_semaphore(), len(targets))


def meet(targets):
    greet(targets)
    await_all(targets)


def line_mates(geo):
    s, m = geo.s, geo.m
    return [(s, (m + 1) % geo.nm), (s, (m + geo.nm - 1) % geo.nm)]


def cube_mates(geo):
    return [(flip(geo.s, bit), geo.m) for bit in bits_of(geo.ns)]


def all_mates(geo):
    return [((geo.s + k) % geo.ns, geo.m) for k in range(1, geo.ns)]


class Geo:
    def __init__(self, sizes):
        self.ns, self.nm = sizes
        self.s = lax.axis_index("seq")
        self.m = lax.axis_index("mp")


class CubeGather:
    @staticmethod
    def sems(ns):
        return [DMA((2, ns - 1)), DMA((2, ns - 1)), DMA(())]

    def __init__(self, geo, shard, full, sems):
        self.geo, self.shard, self.full = geo, shard, full
        self.send, self.recv, self.local = sems
        self.rows = shard.shape[0]
        self.orders = two_orders(bits_of(geo.ns))
        self.ids = {}
        for order, bits in enumerate(self.orders):
            count = 0
            for step in range(len(bits)):
                for mask in spans(bits[:step]):
                    self.ids[order, step, mask] = count
                    count += 1
        self.todo = sorted(self.ids, key=lambda key: (key[1], bin(key[2]).count("1"), key[2], key[0]))
        self.started = []

    def block(self, order, mask):
        half = self.rows // 2
        start = flip(self.geo.s, mask) * self.rows + order * half
        return self.full.at[pl.ds(pl.multiple_of(start, half), half)]

    def copy(self, order, step, mask, incoming=False):
        bit = self.orders[order][step]
        half = self.rows // 2
        place = self.block(order, mask ^ bit if incoming else mask)
        src = self.shard.at[pl.ds(order * half, half)] if mask == 0 and not incoming else place
        at = self.ids[order, step, mask]
        return remote(
            src, place, self.send.at[order, at], self.recv.at[order, at],
            (flip(self.geo.s, bit), self.geo.m),
        )

    def own(self):
        start = pl.multiple_of(self.geo.s * self.rows, self.rows)
        return pltpu.make_async_copy(self.shard, self.full.at[pl.ds(start, self.rows)], self.local)

    def begin(self, steps=None):
        depth = len(self.orders[0])
        for step in range(depth) if steps is None else steps:
            for order in range(2):
                self.copy(order, step, 0).start()
            if step == depth - 1:
                self.own().start()

    def advance(self, count=None):
        count = len(self.todo) if count is None else count
        for order, step, mask in self.todo[:count]:
            self.copy(order, step, mask, incoming=True).wait_recv()
            after = mask ^ self.orders[order][step]
            for later in range(step + 1, len(self.orders[order])):
                self.copy(order, later, after).start()
        self.todo = self.todo[count:]

    def settle(self):
        self.advance()
        self.own().wait()

    def finish(self):
        for order, step, mask in self.ids:
            self.copy(order, step, mask).wait_send()


class CubeScatter:
    @staticmethod
    def scratch(ns, rows, cols):
        return [pltpu.VMEM((2, ns - 1, rows // 2, cols), BF), DMA((2, ns - 1)), DMA((2, ns - 1))]

    def __init__(self, geo, total, scratch):
        self.geo, self.total = geo, total
        self.slots, self.send, self.recv = scratch
        self.half = self.slots.shape[2]
        self.orders = [list(reversed(bits)) for bits in two_orders(bits_of(geo.ns))]
        self.ids = {}
        for order, bits in enumerate(self.orders):
            count = 0
            for step in range(len(bits)):
                for mask in reversed(spans(bits[step + 1 :])):
                    self.ids[order, step, mask] = count
                    count += 1
        depth = len(self.orders[0])

        def urgency(key):
            order, step, mask = key
            ahead = [k for k in range(depth) if mask & self.orders[order][k]]
            return (step, ahead[0] if ahead else depth, -mask, order)

        self.todo = sorted(self.ids, key=urgency)

    def rows(self, order, mask):
        start = flip(self.geo.s, mask) * (2 * self.half) + order * self.half
        return pl.ds(pl.multiple_of(start, self.half), self.half)

    def copy(self, order, step, mask):
        bit = self.orders[order][step]
        at = self.ids[order, step, mask]
        return remote(
            self.total.at[self.rows(order, mask ^ bit)], self.slots.at[order, at],
            self.send.at[order, at], self.recv.at[order, at],
            (flip(self.geo.s, bit), self.geo.m),
        )

    def begin(self):
        for order, step, mask in self.todo:
            if step == 0:
                self.copy(order, 0, mask).start()

    def advance(self, count=None):
        count = len(self.todo) if count is None else count
        for order, step, mask in self.todo[:count]:
            self.copy(order, step, mask).wait_recv()
            if mask == 0 and step == len(self.orders[order]) - 1:
                continue
            rows = self.rows(order, mask)
            slot = self.slots[order, self.ids[order, step, mask]]
            self.total[rows, :] = (self.total[rows, :].astype(F32) + slot.astype(F32)).astype(BF)
            bits = self.orders[order]
            if step + 1 < len(bits) and mask & bits[step + 1]:
                self.copy(order, step + 1, mask ^ bits[step + 1]).start()
        self.todo = self.todo[count:]

    def finish(self, out):
        self.advance()
        for order in range(2):
            last = self.ids[order, len(self.orders[order]) - 1, 0]
            out[pl.ds(order * self.half, self.half), :] = self.total[self.rows(order, 0), :].astype(
                F32
            ) + self.slots[order, last].astype(F32)
        for order, step, mask in self.ids:
            self.copy(order, step, mask).wait_send()


class LineGather:
    @staticmethod
    def sems(nm):
        return [DMA((2, NSEQ, nm - 1)), DMA((2, NSEQ, nm - 1))]

    def __init__(self, geo, full, sems):
        self.geo, self.full = geo, full
        self.send, self.recv = sems
        self.span = full.shape[1] // geo.nm

    def place(self, piece, origin):
        return self.full.at[piece, pl.ds(pl.multiple_of(origin * self.span, self.span), self.span)]

    def copy(self, way, piece, hop, incoming=False):
        m = self.geo.m
        sign = 1 if way == 0 else -1
        origin = m - sign * (hop + (1 if incoming else 0))
        place = self.place(piece, origin)
        return remote(
            place, place, self.send.at[way, piece, hop], self.recv.at[way, piece, hop],
            (self.geo.s, m + sign),
        )

    def sends(self, way, hop):
        m, nm = self.geo.m, self.geo.nm
        if way == 0:
            return jnp.logical_and(m >= hop, m < nm - 1)
        return jnp.logical_and(m <= nm - 1 - hop, m > 0)

    def receives(self, way, hop):
        m, nm = self.geo.m, self.geo.nm
        return m >= hop + 1 if way == 0 else m <= nm - 2 - hop

    def begin(self, piece):
        for way in range(2):
            @pl.when(self.sends(way, 0))
            def _(way=way):
                self.copy(way, piece, 0).start()

    def advance(self, piece, hop):
        for way in range(2):
            @pl.when(self.receives(way, hop))
            def _(way=way):
                self.copy(way, piece, hop, incoming=True).wait_recv()

            if hop + 1 < self.geo.nm - 1:
                @pl.when(self.sends(way, hop + 1))
                def _(way=way):
                    self.copy(way, piece, hop + 1).start()

    def finish(self, piece):
        for way in range(2):
            for hop in range(self.geo.nm - 1):
                @pl.when(self.sends(way, hop))
                def _(way=way, hop=hop):
                    self.copy(way, piece, hop).wait_send()


class LineScatter:
    @staticmethod
    def scratch(nm, span, cols):
        return [
            pltpu.VMEM((2, NSEQ, nm, span, cols), BF),
            DMA((2, NSEQ, nm)),
            DMA((2, NSEQ, nm)),
        ]

    def __init__(self, geo, part, scratch):
        self.geo, self.part = geo, part
        self.slots, self.send, self.recv = scratch
        self.span = self.slots.shape[3]

    def place(self, way):
        return self.geo.m if way == 0 else self.geo.nm - 1 - self.geo.m

    def own(self, way, piece, block):
        at = self.geo.nm - 1 - block if way == 0 else block
        start = at * self.span
        if not isinstance(start, int):
            start = pl.multiple_of(start, self.span)
        return self.part.at[piece, pl.ds(start, self.span)]

    def copy(self, way, piece, block, first=False):
        slot = self.slots.at[way, piece, block]
        src = self.own(way, piece, block) if first else slot
        step = 1 if way == 0 else -1
        return remote(
            src, slot, self.send.at[way, piece, block], self.recv.at[way, piece, block],
            (self.geo.s, self.geo.m + step),
        )

    def begin(self, piece):
        for way in range(2):
            @pl.when(self.place(way) == 0)
            def _(way=way):
                self.copy(way, piece, 0, True).start()

    def advance(self, piece, turn):
        forward = turn <= self.geo.nm - 2
        for way in range(2):
            at = self.place(way)
            if forward:
                @pl.when(at == 0)
                def _(way=way):
                    self.copy(way, piece, turn - 1, True).wait_send()
                    self.copy(way, piece, turn, True).start()

            @pl.when(jnp.logical_and(at >= 1, at <= turn))
            def _(way=way, block=turn - at):
                self.copy(way, piece, block).wait_recv()
                if forward:
                    slot = self.slots.at[way, piece, block]
                    own = self.own(way, piece, block)
                    slot[...] = (slot[...].astype(F32) + own[...].astype(F32)).astype(BF)
                    self.copy(way, piece, block).start()

    def result(self, piece, out):
        m, nm = self.geo.m, self.geo.nm
        own = self.part[piece, pl.ds(pl.multiple_of(m * self.span, self.span), self.span), :]
        out[piece] = own.astype(F32)

        @pl.when(m >= 1)
        def _():
            out[piece] = out[piece] + self.slots[0, piece, nm - 1 - m].astype(F32)

        @pl.when(m <= nm - 2)
        def _():
            out[piece] = out[piece] + self.slots[1, piece, m].astype(F32)

    def finish(self, piece):
        nm = self.geo.nm
        for way in range(2):
            at = self.place(way)
            for block in range(nm - 1):
                first = 0 if block == nm - 2 else 1

                @pl.when(jnp.logical_and(at >= first, at <= nm - 2 - block))
                def _(way=way, block=block):
                    self.copy(way, piece, block).wait_send()


def comm_params(collective, limit=60):
    return pltpu.CompilerParams(
        collective_id=collective, has_side_effects=True, vmem_limit_bytes=limit * 2**20
    )


def load(pairs):
    for src, dst, sem in pairs:
        pltpu.make_async_copy(src, dst, sem).start()


def ready(pairs):
    for src, dst, sem in pairs:
        pltpu.make_async_copy(src, dst, sem).wait()


GROUP = 4


def conv_row(conv, group, tap, column):
    return conv[group, pl.ds(tap, 1), pl.ds(pl.multiple_of(column, LANES), LANES)]


def before_silu(extended, conv, piece, group, head, width, rank):
    span = extended.shape[1] - LEAD
    cols = pl.ds(pl.multiple_of(group * width + head * LANES, LANES), LANES)
    total = None
    for tap in range(4):
        term = conv_row(conv, group, tap, rank * width + head * LANES) * extended[
            piece, pl.ds(LEAD - tap, span), cols
        ]
        total = term if total is None else total + term
    return total


def strengths_of(geo, logits, lengths, bias, local_heads, piece):
    span = logits.shape[1]
    lane = iota((span, LANES), 1)
    offset = jnp.zeros((span, LANES), F32)
    for head in range(local_heads):
        offset = jnp.where(lane == head, bias[geo.m * local_heads + head], offset)
    position = geo.s * span + iota((span, LANES), 0)
    live = jnp.where(position < lengths[piece], 1.0, 0.0)
    return sigmoid(logits[piece] + offset), live


def column_of(values, head):
    return jnp.sum(jnp.where(iota(values.shape, 1) == head, values, 0.0), -1, keepdims=True)


def fill_extended(extended, projected, edge, piece):
    extended[piece, LEAD:, :] = projected[piece].astype(F32)
    extended[piece, :LEAD, :] = edge[piece, EDGE - LEAD :, :].astype(F32)


class Chains:
    @staticmethod
    def scratch(ns, chains):
        return [
            pltpu.VMEM((ns, LANES, LANES), F32),
            DMA((chains,)), DMA((ns,)), DMA((ns,)), DMA((chains,)),
        ]

    def __init__(self, geo, chains, pair, links, entries, scratch):
        self.geo, self.chains = geo, chains
        self.pair, self.links, self.entries = pair, links, entries
        self.states, self.pair_send, self.pair_recv, self.back_send, self.back_recv = scratch
        self.stride = geo.ns // chains
        self.mine = geo.s // self.stride
        self.holds = geo.s == self.mine * self.stride

    def link_copy(self, chain):
        s, m = self.geo.s, self.geo.m
        return remote(
            self.pair.at[chain], self.links.at[s], self.pair_send.at[chain], self.pair_recv.at[s],
            (chain * self.stride, m),
        )

    def give(self, chain, link):
        owner = chain * self.stride

        @pl.when(owner == self.geo.s)
        def _():
            self.links[self.geo.s] = link

        @pl.when(owner != self.geo.s)
        def _():
            self.link_copy(chain).start()

    def state_copy(self, other):
        return remote(
            self.states.at[other], self.entries.at[self.mine], self.back_send.at[other],
            self.back_recv.at[self.mine], (other, self.geo.m),
        )

    def run(self, first, count, advance, start, reverse, last):
        ns, s, m = self.geo.ns, self.geo.s, self.geo.m

        @pl.when(jnp.logical_and(self.holds, jnp.logical_and(self.mine >= first, self.mine < first + count)))
        def _():
            def step(lap, carry):
                at = ns - 1 - lap if reverse else lap
                state = carry[0]
                self.states[at] = state

                @pl.when(at == s)
                def _():
                    self.entries[self.mine] = state

                @pl.when(at != s)
                def _():
                    self.state_copy(at).start()
                    remote(
                        self.pair.at[0], self.links.at[at], self.pair_send.at[0],
                        self.pair_recv.at[at], (s, m),
                    ).wait_recv()

                return advance(carry, at)

            last(lax.fori_loop(0, ns, step, start))

    def receive(self, chain):
        @pl.when(chain * self.stride != self.geo.s)
        def _():
            remote(
                self.states.at[0], self.entries.at[chain], self.back_send.at[0],
                self.back_recv.at[chain], (self.geo.s, self.geo.m),
            ).wait_recv()

    def finish(self):
        def sent(chain, carry):
            @pl.when(chain * self.stride != self.geo.s)
            def _():
                self.link_copy(chain).wait_send()

            return carry

        lax.fori_loop(0, self.chains, sent, 0)

        @pl.when(self.holds)
        def _():
            def done(other, carry):
                @pl.when(other != self.geo.s)
                def _():
                    self.state_copy(other).wait_send()

                return carry

            lax.fori_loop(0, self.geo.ns, done, 0)


def mixer_kernel(
    sizes, tokens, cotangent, query_w, key_w, value_w, beta_w, out_in, gate_hbm, up_hbm, down_in,
    conv, lengths, bias, mixer_gain, head_gain, feed_gain,
    rows_o, proj_w_o, out_w_o, gate_w_o, up_w_o, down_w_o, grad_rows_o, feed_rows_o,
    hidden_in, head_rows, projected, logits, edge, links, norm_o, entry_o,
    solve_h, wkeys_h, fresh_h, error_h, outputs_h, queries_h, keys_h,
    solve_o, wkeys_o, fresh_o, error_o, outputs_o, queries_o, keys_o,
    proj_shard, out_shard, gate_shard, up_shard, down_shard,
    rows, weight, out_w, grad_rows, feed_rows, part, extended, betas, wvalues, pair,
    keep, edge_send, edge_recv, *rest,
):
    geo = Geo(sizes)
    ns, nm, s, m = geo.ns, geo.nm, geo.s, geo.m
    mates = line_mates(geo) + all_mates(geo)
    greet(mates)
    shards = [(gate_hbm, gate_shard, keep.at[0]), (up_hbm, up_shard, keep.at[1])]
    load(shards)
    width = query_w.shape[1]
    heads = width // LANES
    chains = NSEQ * heads
    span = projected.shape[1]
    proj_shard[:, 0:width] = query_w[...]
    proj_shard[:, width : 2 * width] = key_w[...]
    proj_shard[:, 2 * width : 3 * width] = value_w[...]
    proj_shard[:, 3 * width :] = jnp.zeros((proj_shard.shape[0], LANES), BF)
    proj_shard[:, 3 * width : 3 * width + heads] = beta_w[...].astype(F32).T.astype(BF)
    out_shard[...] = out_in[...].T
    await_all(mates)

    weights = CubeGather(geo, proj_shard, weight, rest[0:3])
    outs = CubeGather(geo, out_shard, out_w, rest[3:6])
    gates = CubeGather(geo, gate_shard, gate_w_o, rest[6:9])
    ups = CubeGather(geo, up_shard, up_w_o, rest[9:12])
    downs = CubeGather(geo, down_shard, down_w_o, rest[12:15])
    spread = LineGather(geo, rows, rest[15:17])
    spread_grad = LineGather(geo, grad_rows, rest[17:19])
    spread_feed = LineGather(geo, feed_rows, rest[19:21])
    collect = LineScatter(geo, part, rest[21:24])
    chain = Chains(geo, chains, pair, links, entry_o, rest[24:29])

    weights.begin()
    own_rows = tokens.shape[1]
    mine = pl.ds(pl.multiple_of(m * own_rows, own_rows), own_rows)
    for piece in range(NSEQ):
        values = tokens[piece].astype(F32)
        rows[piece, mine, :] = (values * row_scale(values) * mixer_gain[...]).astype(BF)
        grad_rows[piece, mine, :] = cotangent[piece]
        if piece == 0:
            spread.begin(0)
    down_shard[...] = down_in[...].T
    spread.advance(0, 0)
    spread.begin(1)
    weights.advance(2)
    outs.begin()
    for hop in range(1, nm - 1):
        spread.advance(0, hop)
        weights.advance(2)
        spread.advance(1, hop - 1)
    outs.advance(2)
    weights.settle()
    ready(shards)
    kept = [(weight, proj_w_o, keep.at[2])]
    load(kept)
    strict = lower_mask(span, True)
    whole = lower_mask(span, False)
    norm_o[...] = jnp.zeros(norm_o.shape, F32)

    def edge_copy(piece):
        return remote(
            projected.at[piece, pl.ds(span - EDGE, EDGE)], edge.at[piece],
            edge_send.at[piece], edge_recv.at[piece], (s + 1, m),
        )

    def run_chains(piece):
        def advance(carry, at):
            state, total = carry
            link = links[at]
            high, low = halves(state)
            move = link[:, :LANES]
            state = state - (dot(move, high) + dot(move, low)) + link[:, LANES:].astype(F32)
            return state, total + jnp.sqrt(jnp.sum(state * state, (0, 1), keepdims=True))

        def last(carry):
            norm_o[...] = norm_o[...] + carry[1]

        start = (jnp.zeros((LANES, LANES), F32), jnp.zeros((1, 1), F32))
        chain.run(piece * heads, heads, advance, start, False, last)

    groups = heads // GROUP

    def solve(piece, carry):
        @pl.when(piece == 1)
        def _():
            for hop in range(nm - 2, nm - 1):
                spread.advance(1, hop)

        result = dot(rows[piece], weight[...])
        projected[piece] = result[:, : 3 * width].astype(BF)
        logits[piece] = result[:, 3 * width :]

        @pl.when(s < ns - 1)
        def _():
            edge_copy(piece).start()

        strength, live = strengths_of(geo, logits, lengths, bias, heads, piece)
        betas[piece] = strength * live

        @pl.when(piece == 0)
        def _():
            gates.begin((0,))
            for at in range(NSEQ):
                spread_grad.begin(at)

        @pl.when(s > 0)
        def _():
            edge_copy(piece).wait_recv()

        @pl.when(s == 0)
        def _():
            edge[piece] = jnp.zeros(edge.shape[1:], BF)

        fill_extended(extended, projected, edge, piece)
        for first in range(0, heads, GROUP):
            which = [first + k for k in range(GROUP)]
            mixed = [
                [before_silu(extended, conv, piece, g, head, width, m) for g in range(3)]
                for head in which
            ]
            mixed = [[z * sigmoid(z) for z in three] for three in mixed]
            queries = [three[0] for three in mixed]
            keys = [
                key * lax.rsqrt(jnp.sum(key * key, -1, keepdims=True) + KEY_EPSILON)
                for _, key, _ in mixed
            ]
            values = [three[2] for three in mixed]
            strengths = [column_of(betas[piece], head) for head in which]
            key_pairs = [halves(key) for key in keys]
            grams = [jnp.where(strict, fine(key, key, NT), 0.0) for key in key_pairs]
            inverses = unit_lower_inverses([gram * beta for gram, beta in zip(grams, strengths)])
            both = [
                halves(jnp.concatenate((key * beta, value * beta), 1))
                for key, value, beta in zip(keys, values, strengths)
            ]
            both = [fine(halves(inverse), right) for inverse, right in zip(inverses, both)]
            found = [fine(key, halves(two), TN).astype(BF) for key, two in zip(key_pairs, both)]
            done = list(zip(queries, keys, values, inverses, both, found))
            for k, (query, key, value, inverse, both, link) in enumerate(done):
                at = piece * heads + first + k
                pair[at] = link
                solve_o[at] = inverse
                wkeys_o[at] = both[:, :LANES]
                wvalues[at] = both[:, LANES:]
                queries_o[at] = query
                keys_o[at] = key
                error_o[at] = value
            for k, found in enumerate(done):
                chain.give(piece * heads + first + k, found[-1])
        return carry

    lax.fori_loop(0, NSEQ, solve, 0)
    saved = [
        (solve_o, solve_h, keep.at[7]), (wkeys_o, wkeys_h, keep.at[8]),
        (queries_o, queries_h, keep.at[9]), (keys_o, keys_h, keep.at[10]),
    ]
    load(saved)
    for piece in range(NSEQ):
        spread_grad.advance(piece, 0)
    outs.settle()
    for piece in range(NSEQ):
        run_chains(piece)

    def gates_on():
        gates.begin(range(1, len(gates.orders[0])))
        gates.advance(2)
        ups.begin()
        downs.begin()

    def apply(piece, then=None):
        def step(lap, carry):
            first = piece * heads + lap * GROUP
            for k in range(GROUP):
                chain.receive(first + k)
            if then is not None:
                then()
            which = [first + k for k in range(GROUP)]
            states = [halves(entry_o[at]) for at in which]
            key_pairs = [halves(keys_o[at]) for at in which]
            query_pairs = [halves(queries_o[at]) for at in which]
            fresh = [
                wvalues[at] - fine(halves(wkeys_o[at]), state) for at, state in zip(which, states)
            ]
            fresh_pairs = [halves(one) for one in fresh]
            grams = [jnp.where(strict, fine(key, key, NT), 0.0) for key in key_pairs]
            scores = [
                jnp.where(whole, fine(query, key, NT), 0.0)
                for query, key in zip(query_pairs, key_pairs)
            ]
            errors = [
                error_o[at] - fine(key, state) - fine(halves(gram), new)
                for at, key, state, gram, new in zip(which, key_pairs, states, grams, fresh_pairs)
            ]
            outputs = [
                fine(query, state) + fine(halves(score), new)
                for query, state, score, new in zip(query_pairs, states, scores, fresh_pairs)
            ]
            done = list(zip(fresh, errors, outputs))
            for k, (fresh, error, output) in enumerate(done):
                at = first + k
                fresh_o[at] = fresh
                error_o[at] = error
                outputs_o[at] = output
                cols = pl.ds(pl.multiple_of((lap * GROUP + k) * LANES, LANES), LANES)
                head_rows[piece, :, cols] = (output * row_scale(output) * head_gain[...]).astype(BF)
            return carry

        lax.fori_loop(0, groups, step, 0)
        part[piece] = dot(head_rows[piece], out_w[...], NT).astype(BF)

    def close(piece):
        collect.result(piece, hidden_in)
        values = hidden_in[piece] + tokens[piece].astype(F32)
        hidden_in[piece] = values
        feed_rows[piece, mine, :] = (values * row_scale(values) * feed_gain[...]).astype(BF)
        spread_feed.begin(piece)

    for piece in range(NSEQ):
        spread_grad.advance(piece, 1)
    apply(0)
    collect.begin(0)
    apply(1, gates_on)
    kept.append((out_w, out_w_o, keep.at[4]))
    later = [
        (fresh_o, fresh_h, keep.at[11]), (error_o, error_h, keep.at[12]),
        (outputs_o, outputs_h, keep.at[13]),
    ]
    load(kept[-1:] + later)
    collect.advance(0, 1)
    for piece in range(NSEQ):
        for hop in range(2, nm - 2):
            spread_grad.advance(piece, hop)
    collect.advance(0, 2)
    collect.begin(1)
    for turn in range(3, nm):
        collect.advance(0, turn)
    close(0)
    collect.advance(1, 1)
    gates.advance(4)
    spread_feed.advance(0, 0)
    collect.advance(1, 2)
    gates.advance()
    spread_feed.advance(0, 1)
    for turn in range(3, nm):
        collect.advance(1, turn)
    close(1)
    ups.advance(4)
    downs.advance(4)
    for hop in range(2, nm - 1):
        spread_feed.advance(0, hop)
    for piece in range(NSEQ):
        spread_grad.advance(piece, nm - 2)
    spread_feed.advance(1, 0)
    ups.advance(2)
    for hop in range(1, nm - 1):
        spread_feed.advance(1, hop)
    downs.advance(2)
    ups.advance()
    downs.advance()
    for piece in range(NSEQ):
        spread.finish(piece)
        collect.finish(piece)
        spread_grad.finish(piece)
        spread_feed.finish(piece)
    late = [
        (feed_rows, feed_rows_o, keep.at[5]), (grad_rows, grad_rows_o, keep.at[6]), (rows, rows_o, keep.at[3])
    ]
    load(late)
    for gather in (gates, ups, downs):
        gather.settle()
    for gather in (weights, outs, gates, ups, downs):
        gather.finish()
    for piece in range(NSEQ):
        @pl.when(s < ns - 1)
        def _(piece=piece):
            edge_copy(piece).wait_send()

    chain.finish()
    ready(kept + saved + later + late)


def mixer(
    sizes, tokens, cotangent, query_w, key_w, value_w, beta_w, out_in, gate_in, up_in, down_in,
    conv, lengths, bias, mixer_gain, head_gain, feed_gain,
):
    ns, nm = sizes
    width = query_w.shape[1]
    shard = query_w.shape[0]
    depth = ns * shard
    cols = gate_in.shape[1]
    own = tokens.shape
    span = own[1] * nm
    heads = width // LANES
    chains = NSEQ * heads
    rows = (NSEQ, span, depth)
    joined = 3 * width + LANES
    shape = jax.ShapeDtypeStruct
    per_chain = (chains, span, LANES)
    return pl.pallas_call(
        functools.partial(mixer_kernel, sizes),
        out_shape=(
            shape(rows, BF), shape((depth, joined), BF), shape((depth, width), BF),
            shape((depth, cols), BF), shape((depth, cols), BF), shape((depth, cols), BF),
            shape(rows, BF), shape(rows, BF),
            shape(own, F32), shape((NSEQ, span, width), BF), shape((NSEQ, span, 3 * width), BF),
            shape((NSEQ, span, LANES), F32), shape((NSEQ, EDGE, 3 * width), BF),
            shape((ns, LANES, 2 * LANES), BF), shape((8, LANES), F32),
            shape((chains, LANES, LANES), F32), shape((chains, span, span), F32),
        )
        + (shape(per_chain, F32),) * 6,
        in_specs=[VMEM] * 7 + [ANY, ANY, VMEM, VMEM, SMEM, SMEM, VMEM, VMEM, VMEM],
        out_specs=(ANY,) * 8 + (VMEM,) * 8 + (ANY,) * 7,
        scratch_shapes=[pltpu.VMEM((chains, span, span), F32)]
        + [pltpu.VMEM(per_chain, F32)] * 6
        + [
            pltpu.VMEM((shard, joined), BF), pltpu.VMEM((shard, width), BF),
            pltpu.VMEM((shard, cols), BF), pltpu.VMEM((shard, cols), BF), pltpu.VMEM((shard, cols), BF),
            pltpu.VMEM(rows, BF), pltpu.VMEM((depth, joined), BF), pltpu.VMEM((depth, width), BF),
            pltpu.VMEM(rows, BF), pltpu.VMEM(rows, BF), pltpu.VMEM(rows, BF),
            pltpu.VMEM((NSEQ, LEAD + span, 3 * width), F32),
            pltpu.VMEM((NSEQ, span, LANES), F32),
            pltpu.VMEM(per_chain, F32),
            pltpu.VMEM((chains, LANES, 2 * LANES), BF),
            DMA((14,)), DMA((NSEQ,)), DMA((NSEQ,)),
        ]
        + CubeGather.sems(ns) * 5
        + LineGather.sems(nm) * 3
        + LineScatter.scratch(nm, own[1], depth)
        + Chains.scratch(ns, chains),
        compiler_params=comm_params(0),
        name="mixer",
    )(
        tokens, cotangent, query_w, key_w, value_w, beta_w, out_in, gate_in, up_in, down_in,
        conv, lengths, bias, mixer_gain, head_gain, feed_gain,
    )


def feed_kernel(
    sizes, feed_rows, grad_rows, gate_hbm, up_hbm, down_hbm, hidden_in, gain, cotangent,
    grad_in, mix_rows_o, grad_gate_o, grad_up_o, grad_down_o, down_part_o, gain_o,
    gate_w, up_w, down_w, hidden, grad_gate, grad_up, part, mix_rows, keep, *rest,
):
    geo = Geo(sizes)
    nm = geo.nm
    weights = [
        (gate_hbm, gate_w, keep.at[0]), (up_hbm, up_w, keep.at[1]), (down_hbm, down_w, keep.at[2])
    ]
    load(weights)
    meet(line_mates(geo) + cube_mates(geo))
    collect = LineScatter(geo, part, rest[0:3])
    spread = LineGather(geo, mix_rows, rest[3:5])
    first = CubeScatter(geo, gate_w, rest[5:8])
    second = CubeScatter(geo, up_w, rest[8:11])
    for piece in range(NSEQ):
        if piece == 0:
            ready(weights[:1])
        gate = dot(feed_rows[piece], gate_w[...])
        if piece == 0:
            ready(weights[1:2])
        up = dot(feed_rows[piece], up_w[...])
        sig = sigmoid(gate)
        active = gate * sig
        hidden[piece] = (active * up).astype(BF)
        if piece == 0:
            ready(weights[2:3])
        grad_hidden = dot(grad_rows[piece], down_w[...])
        grad_gate[piece] = (grad_hidden * up * sig * (1.0 + gate * (1.0 - sig))).astype(BF)
        grad_up[piece] = (grad_hidden * active).astype(BF)
        part[piece] = (
            dot(grad_gate[piece], gate_w[...], NT) + dot(grad_up[piece], up_w[...], NT)
        ).astype(BF)
        if piece == 0:
            collect.begin(0)
    depth, cols = gate_w.shape
    tile = 512
    span = hidden_in.shape[1]
    mine = pl.ds(pl.multiple_of(geo.m * span, span), span)

    def weight_grad(rows, grads, out):
        def step(at, carry):
            window = pl.ds(pl.multiple_of(at * tile, tile), tile)
            total = dot(rows[0, :, window], grads[0], TN) + dot(rows[1, :, window], grads[1], TN)
            out[window, :] = total.astype(BF)
            return carry

        lax.fori_loop(0, depth // tile, step, 0)

    def close(piece):
        collect.result(piece, grad_in)
        grad_feed = grad_in[piece]
        rows = hidden_in[piece]
        scale = row_scale(rows)
        unit = rows * scale
        part_gain = jnp.sum(grad_feed * unit, 0, keepdims=True)
        if piece == 0:
            gain_o[...] = part_gain
        else:
            gain_o[...] = gain_o[...] + part_gain
        back = cotangent[piece].astype(F32) + norm_backward(grad_feed * gain[...], unit, scale)
        grad_in[piece] = back
        mix_rows[piece, mine, :] = back.astype(BF)
        spread.begin(piece)

    collect.advance(0, 1)
    weight_grad(feed_rows, grad_gate, gate_w)
    first.begin()
    collect.advance(0, 2)
    collect.begin(1)
    weight_grad(feed_rows, grad_up, up_w)
    second.begin()
    first.advance(8)
    for turn in range(3, nm):
        collect.advance(0, turn)
    close(0)
    collect.advance(1, 1)
    second.advance(8)
    spread.advance(0, 0)
    collect.advance(1, 2)
    first.advance(4)
    spread.advance(0, 1)
    for turn in range(3, nm):
        collect.advance(1, turn)
    close(1)
    for piece in range(NSEQ):
        collect.finish(piece)
        part[piece] = dot(hidden[piece], down_w[...], NT).astype(BF)
    later = [(part, down_part_o, keep.at[0])]
    load(later)
    for hop in range(2, nm - 1):
        spread.advance(0, hop)
    second.advance(4)
    spread.advance(1, 0)
    weight_grad(grad_rows, hidden, down_w)
    later.append((down_w, grad_down_o, keep.at[1]))
    load(later[1:])
    for hop in range(1, nm - 1):
        spread.advance(1, hop)
    for piece in range(NSEQ):
        spread.finish(piece)
    later.append((mix_rows, mix_rows_o, keep.at[2]))
    load(later[2:])
    first.finish(grad_gate_o)
    second.finish(grad_up_o)
    ready(later)


def feed(sizes, feed_rows, grad_rows, gate_w, up_w, down_w, hidden_in, gain, cotangent):
    ns, nm = sizes
    depth, cols = gate_w.shape
    span = hidden_in.shape[1]
    shard = depth // ns
    rows = (NSEQ, span * nm, depth)
    inner = (NSEQ, span * nm, cols)
    return pl.pallas_call(
        functools.partial(feed_kernel, sizes),
        out_shape=(
            jax.ShapeDtypeStruct((NSEQ, span, depth), F32),
            jax.ShapeDtypeStruct(rows, BF),
            jax.ShapeDtypeStruct((shard, cols), F32),
            jax.ShapeDtypeStruct((shard, cols), F32),
            jax.ShapeDtypeStruct((depth, cols), BF),
            jax.ShapeDtypeStruct(rows, BF),
            jax.ShapeDtypeStruct((1, depth), F32),
        ),
        in_specs=[VMEM, VMEM, ANY, ANY, ANY, VMEM, VMEM, VMEM],
        out_specs=(VMEM, ANY, VMEM, VMEM, ANY, ANY, VMEM),
        scratch_shapes=[
            pltpu.VMEM((depth, cols), BF), pltpu.VMEM((depth, cols), BF), pltpu.VMEM((depth, cols), BF),
            pltpu.VMEM(inner, BF), pltpu.VMEM(inner, BF), pltpu.VMEM(inner, BF),
            pltpu.VMEM(rows, BF), pltpu.VMEM(rows, BF), DMA((3,)),
        ]
        + LineScatter.scratch(nm, span, depth)
        + LineGather.sems(nm)
        + CubeScatter.scratch(ns, shard, cols) * 2,
        compiler_params=comm_params(1, 63),
        name="feed",
    )(feed_rows, grad_rows, gate_w, up_w, down_w, hidden_in, gain, cotangent)


def backward_kernel(
    sizes, mix_rows_h, out_weight_h, head_rows, projected, logits, conv, lengths, bias, gain,
    edge, links, solve_h, wkeys_h, fresh_h, error_h, outputs_h, queries_h, keys_h, entry,
    grad_down_hbm, down_part_hbm, hidden_in,
    grads_o, block_o, grad_down_o, conv_o, gain_o, bias_o, out_total_o,
    mix_rows, out_weight, solve, fresh, error, queries, keys,
    extended, betas, grad_output, held, grad_mixed, grad_tail, grad_logit,
    pair, gathered, leaving, edge_out, edge_in, out_total, down_total, down_part, keep,
    edge_send, edge_recv, *rest,
):
    geo = Geo(sizes)
    ns, nm, s, m = geo.ns, geo.nm, geo.s, geo.m
    span, width = projected.shape[1], projected.shape[2] // 3
    heads = width // LANES
    chains = NSEQ * heads
    which = range(heads)
    mates = line_mates(geo) + all_mates(geo)
    greet(mates)
    kept = [(out_total, out_total_o, keep.at[11])]
    loads = [
        (down_part_hbm, down_part, keep.at[0]), (grad_down_hbm, down_total, keep.at[1]),
        (mix_rows_h, mix_rows, keep.at[2]), (out_weight_h, out_weight, keep.at[3]),
        (outputs_h, grad_output, keep.at[4]), (queries_h, queries, keep.at[5]),
        (keys_h, keys, keep.at[6]), (wkeys_h, held, keep.at[7]),
        (fresh_h, fresh, keep.at[8]), (solve_h, solve, keep.at[9]), (error_h, error, keep.at[10]),
    ]
    load(loads)
    collect = LineScatter(geo, down_part, rest[0:3])
    first = CubeScatter(geo, down_total, rest[3:6])
    chain = Chains(geo, chains, pair, gathered, leaving, rest[6:11])
    strict = lower_mask(span, True)
    whole = lower_mask(span, False)
    gain_o[...] = jnp.zeros(gain_o.shape, F32)
    conv_o[...] = jnp.zeros(conv_o.shape, F32)
    pad = grad_mixed.shape[1] - LEAD - span
    for piece in range(NSEQ):
        grad_mixed[piece, :LEAD, :] = jnp.zeros((LEAD, 3 * width), F32)
        grad_mixed[piece, LEAD + span :, :] = jnp.zeros((pad, 3 * width), F32)
        fill_extended(extended, projected, edge, piece)
        strength, live = strengths_of(geo, logits, lengths, bias, heads, piece)
        betas[piece] = strength * live
    await_all(mates)
    ready(loads[:1])
    for piece in range(NSEQ):
        collect.begin(piece)
    ready(loads[1:2])
    first.begin()
    ready(loads[2:8])

    def start(piece, carry):
        grad_head = dot(mix_rows[piece], out_weight[...])
        scaled = [grad_output[piece * heads + h] for h in which]
        scales = [row_scale(output) for output in scaled]
        units = [output * scale for output, scale in zip(scaled, scales)]
        grads = [grad_head[:, h * LANES : (h + 1) * LANES] for h in which]
        share = [jnp.sum(grad * unit, 0, keepdims=True) for grad, unit in zip(grads, units)]
        gain_o[...] = gain_o[...] + sum(share)
        grads = [
            norm_backward(grad * gain[...], unit, scale)
            for grad, unit, scale in zip(grads, units, scales)
        ]
        grad_pairs = [halves(grad) for grad in grads]
        query_pairs = [halves(queries[piece * heads + h]) for h in which]
        scores = [
            jnp.where(whole, fine(query, halves(keys[piece * heads + h]), NT), 0.0)
            for h, query in zip(which, query_pairs)
        ]
        spread = [fine(halves(score), grad, TN) for score, grad in zip(scores, grad_pairs)]
        found = [
            fine(query, grad, TN) - fine(halves(held[piece * heads + h]), halves(one), TN)
            for h, query, grad, one in zip(which, query_pairs, grad_pairs, spread)
        ]
        found = [link.astype(BF) for link in found]
        for h in which:
            at = piece * heads + h
            grad_output[at] = grads[h]
            held[at] = spread[h]
            pair[at] = found[h]
        for h in which:
            chain.give(piece * heads + h, found[h])
        return carry

    lax.fori_loop(0, NSEQ, start, 0)
    first.advance(2)
    ready(loads[8:])

    def through_conv(piece, h, group, grad, key=None):
        z = before_silu(extended, conv, piece, group, h, width, m)
        sig = sigmoid(z)
        if key is not None:
            raw = z * sig
            scale = lax.rsqrt(jnp.sum(raw * raw, -1, keepdims=True) + KEY_EPSILON)
            grad = scale * (grad - key * jnp.sum(key * grad, -1, keepdims=True))
        grad = grad * sig * (1.0 + z * (1.0 - sig))
        cols = slice(group * width + h * LANES, group * width + (h + 1) * LANES)
        local = slice(h * LANES, (h + 1) * LANES)
        grad_mixed[piece, pl.ds(LEAD, span), cols] = grad
        back = None
        for tap in range(4):
            share = jnp.sum(grad * extended[piece, pl.ds(LEAD - tap, span), cols], 0, keepdims=True)
            row = slice(group * 4 + tap, group * 4 + tap + 1)
            conv_o[row, local] = conv_o[row, local] + share
            term = (
                conv_row(conv, group, tap, m * width + h * LANES)
                * grad_mixed[piece, pl.ds(tap, LEAD + span), cols]
            )
            back = term if back is None else back + term
        edge_out[piece, :, cols] = back[:LEAD]
        grads_o[piece, :, cols] = back[LEAD:].astype(BF)
        grad_tail[piece, :, cols] = back[LEAD + span - EDGE :]

    def before_exit(piece):
        base = piece * heads
        grad_pairs = [halves(grad_output[base + h]) for h in which]
        key_pairs = [halves(keys[base + h]) for h in which]
        scores = [
            halves(jnp.where(whole, fine(grad, halves(fresh[base + h]), NT), 0.0))
            for h, grad in zip(which, grad_pairs)
        ]
        grads = [
            fine(score, key) + fine(grad, halves(entry[base + h]), NT)
            for h, score, key, grad in zip(which, scores, key_pairs, grad_pairs)
        ]
        to_keys = [
            fine(score, halves(queries[base + h]), TN) for h, score in zip(which, scores)
        ]
        for h in which:
            grad_output[base + h] = to_keys[h]
        for h in which:
            through_conv(piece, h, 0, grads[h])

    def after_exit(piece):
        base = piece * heads
        for h in which:
            chain.receive(base + h)

        @pl.when(piece == 0)
        def _():
            first.advance(6)

        key_pairs = [halves(keys[base + h]) for h in which]
        exits = [halves(leaving[base + h]) for h in which]
        fresh_pairs = [halves(fresh[base + h]) for h in which]
        strengths = [column_of(betas[piece], h) for h in which]
        weak = [halves(held[base + h] + fine(key, out)) for h, key, out in zip(which, key_pairs, exits)]
        weak = [fine(halves(solve[base + h]), one, TN) for h, one in zip(which, weak)]
        grad_beta = [jnp.sum(one * error[base + h], -1, keepdims=True) for h, one in zip(which, weak)]
        values = [one * beta for one, beta in zip(weak, strengths)]
        value_pairs = [halves(value) for value in values]
        scores = [
            halves(jnp.where(strict, -fine(value, new, NT), 0.0))
            for value, new in zip(value_pairs, fresh_pairs)
        ]
        grads = [
            grad_output[base + h]
            - fine(value, halves(entry[base + h]), NT)
            + fine(score, key)
            + fine(score, key, TN)
            + fine(new, out, NT)
            for h, value, score, key, new, out in zip(
                which, value_pairs, scores, key_pairs, fresh_pairs, exits
            )
        ]
        lane = iota((span, LANES), 1)
        grad_logit[piece] = sum(jnp.where(lane == h, grad_beta[h], 0.0) for h in which)
        for h in which:
            through_conv(piece, h, 1, grads[h], keys[base + h])
            through_conv(piece, h, 2, values[h])

    def run_chains(piece):
        def advance(carry, at):
            (state,) = carry
            high, low = halves(state)
            move = links[at][:, :LANES]
            state = state - (dot(move, high, TN) + dot(move, low, TN)) + gathered[at].astype(F32)
            return (state,)

        chain.run(
            piece * heads, heads, advance, (jnp.zeros((LANES, LANES), F32),), True, lambda carry: None
        )

    def edge_copy(piece):
        return remote(
            edge_out.at[piece], edge_in.at[piece], edge_send.at[piece], edge_recv.at[piece],
            (s - 1, m),
        )

    depth = out_weight.shape[0]
    tile = 512

    def weight_grad(at, carry):
        window = pl.ds(pl.multiple_of(at * tile, tile), tile)
        total = dot(mix_rows[0, :, window], head_rows[0], TN) + dot(
            mix_rows[1, :, window], head_rows[1], TN
        )
        out_total[window, :] = total.astype(BF)
        return carry

    def leave(piece, carry):
        before_exit(piece)

        @pl.when(piece == 0)
        def _():
            for at in range(NSEQ):
                run_chains(at)
            lax.fori_loop(0, depth // tile, weight_grad, 0)
            load(kept)
            for at in range(NSEQ):
                collect.advance(at, 1)

        return carry

    lax.fori_loop(0, NSEQ, leave, 0)

    def enter(piece, carry):
        after_exit(piece)

        @pl.when(s > 0)
        def _():
            edge_copy(piece).start()

        @pl.when(piece == 0)
        def _():
            for at in range(NSEQ):
                collect.advance(at, 2)

        return carry

    lax.fori_loop(0, NSEQ, enter, 0)
    bias_sum = jnp.zeros((1, LANES), F32)
    for piece in range(NSEQ):
        sig, live = strengths_of(geo, logits, lengths, bias, heads, piece)
        grad = grad_logit[piece] * live * sig * (1.0 - sig)
        bias_sum = bias_sum + jnp.sum(grad, 0, keepdims=True)
        grads_o[piece, :, pl.ds(3 * width, LANES)] = grad.astype(BF)
    lane = iota((1, LANES), 1)
    spread_bias = jnp.zeros((1, LANES), F32)
    for h in which:
        spread_bias = spread_bias + jnp.where(lane == m * heads + h, column_of(bias_sum, h), 0.0)
    bias_o[...] = spread_bias
    first.advance(4)
    for turn in range(3, nm):
        for piece in range(NSEQ):
            collect.advance(piece, turn)
    for piece in range(NSEQ):
        collect.result(piece, block_o)
        block_o[piece] = block_o[piece] + hidden_in[piece]
        collect.finish(piece)

    for piece in range(NSEQ):
        @pl.when(s < ns - 1)
        def _(piece=piece):
            edge_copy(piece).wait_recv()
            tail = pl.ds(EDGE - LEAD, LEAD)
            grad_tail[piece, tail, :] = grad_tail[piece, tail, :] + edge_in[piece]
            grads_o[piece, pl.ds(span - EDGE, EDGE), pl.ds(0, 3 * width)] = grad_tail[piece].astype(BF)

        @pl.when(s > 0)
        def _(piece=piece):
            edge_copy(piece).wait_send()

    first.finish(grad_down_o)
    chain.finish()
    ready(kept)


def backward(
    sizes, mix_rows, out_weight, head_rows, projected, logits, conv, lengths, bias, gain, saved,
    grad_down, down_part, hidden_in,
):
    ns, nm = sizes
    span, width = projected.shape[1], projected.shape[2] // 3
    heads = width // LANES
    chains = NSEQ * heads
    depth, cols = grad_down.shape
    shard = depth // ns
    local = hidden_in.shape
    rows = (NSEQ, span, depth)
    per_chain = (chains, span, LANES)
    return pl.pallas_call(
        functools.partial(backward_kernel, sizes),
        out_shape=(
            jax.ShapeDtypeStruct((NSEQ, span, 3 * width + LANES), BF),
            jax.ShapeDtypeStruct(local, F32),
            jax.ShapeDtypeStruct((shard, cols), F32),
            jax.ShapeDtypeStruct((12, width), F32),
            jax.ShapeDtypeStruct((1, LANES), F32),
            jax.ShapeDtypeStruct((1, LANES), F32),
            jax.ShapeDtypeStruct((depth, width), BF),
        ),
        in_specs=[ANY, ANY] + [VMEM] * 4 + [SMEM, SMEM] + [VMEM] * 3 + [ANY] * 7 + [VMEM, ANY, ANY, VMEM],
        out_specs=(VMEM,) * 6 + (ANY,),
        scratch_shapes=[
            pltpu.VMEM(rows, BF), pltpu.VMEM((depth, width), BF),
            pltpu.VMEM((chains, span, span), F32),
        ]
        + [pltpu.VMEM(per_chain, F32)] * 4
        + [
            pltpu.VMEM((NSEQ, LEAD + span, 3 * width), F32),
            pltpu.VMEM((NSEQ, span, LANES), F32),
            pltpu.VMEM(per_chain, F32),
            pltpu.VMEM(per_chain, F32),
            pltpu.VMEM((NSEQ, LEAD + span + LEAD, 3 * width), F32),
            pltpu.VMEM((NSEQ, EDGE, 3 * width), F32),
            pltpu.VMEM((NSEQ, span, LANES), F32),
            pltpu.VMEM((chains, LANES, LANES), BF),
            pltpu.VMEM((ns, LANES, LANES), BF),
            pltpu.VMEM((chains, LANES, LANES), F32),
            pltpu.VMEM((NSEQ, LEAD, 3 * width), F32),
            pltpu.VMEM((NSEQ, LEAD, 3 * width), F32),
            pltpu.VMEM((depth, width), BF),
            pltpu.VMEM((depth, cols), BF),
            pltpu.VMEM(rows, BF),
            DMA((12,)), DMA((NSEQ,)), DMA((NSEQ,)),
        ]
        + LineScatter.scratch(nm, local[1], depth)
        + CubeScatter.scratch(ns, shard, cols)
        + Chains.scratch(ns, chains),
        compiler_params=comm_params(2, 63),
        name="recurrence_back",
    )(
        mix_rows, out_weight, head_rows, projected, logits, conv, lengths, bias, gain, *saved,
        grad_down, down_part, hidden_in,
    )


def last_kernel(
    sizes, rows_h, grads, proj_w, out_total_h, tokens, gain, grad_in,
    conv_part, head_gain, bias, norms, feed_gain,
    grad_tokens, grad_weight_o, grad_out_o,
    conv_o, head_gain_o, bias_o, norm_o, feed_gain_o, gain_o,
    rows, part, total, out_total, vector, over_seq, over_mp,
    keep, seq_send, seq_recv, mp_send, mp_recv, *rest,
):
    geo = Geo(sizes)
    ns, nm, s, m = geo.ns, geo.nm, geo.s, geo.m
    mates = [(s, (m + k) % nm) for k in range(1, nm)] + all_mates(geo)
    greet(mates)
    loads = [(out_total_h, out_total, keep.at[0]), (rows_h, rows, keep.at[1])]
    load(loads)
    depth = proj_w.shape[0]
    width = vector.shape[1]
    wide = depth // width
    row = conv_part.shape[0]
    vector[...] = jnp.zeros(vector.shape, F32)
    vector[0:row, :] = conv_part[...]
    vector[row : row + 1, 0:LANES] = head_gain[...]
    vector[row : row + 1, LANES : 2 * LANES] = bias[...]
    vector[row : row + 1, 2 * LANES : 3 * LANES] = norms[0:1, :]
    for at in range(wide):
        vector[row + 1 + at : row + 2 + at, :] = feed_gain[:, at * width : (at + 1) * width]
    await_all(mates)
    collect = LineScatter(geo, part, rest[0:3])
    scatter = CubeScatter(geo, total, rest[3:6])
    outs = CubeScatter(geo, out_total, rest[6:9])
    shares = []

    def spread(piece):
        value = dot(grads[piece], proj_w[...], NT)
        part[piece] = value.astype(BF)
        collect.begin(piece)
        if piece == 0:
            ready(loads[1:])
        shares.append(jnp.sum(value * rows[piece].astype(F32), 0, keepdims=True))

    tile = 512

    def weight_grad(left, right, out):
        def step(at, carry):
            window = pl.ds(pl.multiple_of(at * tile, tile), tile)
            value = dot(left[0, :, window], right[0], TN) + dot(left[1, :, window], right[1], TN)
            out[window, :] = value.astype(BF)
            return carry

        lax.fori_loop(0, depth // tile, step, 0)

    ready(loads[:1])
    outs.begin()
    spread(0)
    outs.advance(8)
    weight_grad(rows, grads, total)
    scatter.begin()
    spread(1)
    outs.advance(2)
    share = (shares[0] + shares[1]) / gain[...]
    for at in range(wide):
        vector[row + 1 + wide + at : row + 2 + wide + at, :] = share[:, at * width : (at + 1) * width]

    def seq_copy(k):
        return remote(
            vector, over_seq.at[k], seq_send.at[k], seq_recv.at[k], ((s + 1 + k) % ns, m)
        )

    def mp_copy(k):
        return remote(
            over_mp.at[0], over_mp.at[1 + k], mp_send.at[k], mp_recv.at[k], (s, (m + 1 + k) % nm)
        )

    def seq_start(k, carry):
        seq_copy(k).start()
        return carry

    lax.fori_loop(0, ns - 1, seq_start, 0)
    collect.advance(0, 1)
    scatter.advance(8)

    def seq_add(k, value):
        seq_copy(k).wait_recv()
        return value + over_seq[k]

    over_mp[0] = lax.fori_loop(0, ns - 1, seq_add, vector[...])
    for k in range(nm - 1):
        mp_copy(k).start()
    collect.advance(1, 1)
    collect.advance(0, 2)
    outs.advance(2)
    for k in range(nm - 1):
        mp_copy(k).wait_recv()
    scatter.advance(2)
    collect.advance(1, 2)
    for turn in range(3, nm):
        collect.advance(0, turn)
        scatter.advance(2)
        collect.advance(1, turn)
    for piece in range(NSEQ):
        collect.result(piece, grad_tokens)
        values = tokens[piece].astype(F32)
        scale = row_scale(values)
        grad_tokens[piece] = grad_in[piece] + norm_backward(
            grad_tokens[piece] * gain[...], values * scale, scale
        )
        collect.finish(piece)
    for k in range(nm):
        origin = (m + nm - k) % nm
        cols = pl.ds(pl.multiple_of(origin * width, width), width)
        for group in range(3):
            for tap in range(4):
                at = group * 4 + tap
                conv_o[group, tap : tap + 1, cols] = over_mp[k, at : at + 1, :]
    summed = over_mp[0]
    for k in range(1, nm):
        summed = summed + over_mp[k]
    head_gain_o[...] = summed[row : row + 1, 0:LANES]
    bias_o[...] = summed[row : row + 1, LANES : 2 * LANES]
    norm_o[...] = summed[row : row + 1, 2 * LANES : 3 * LANES] / (NSEQ * HEADS * ns)
    for at in range(wide):
        cols = slice(at * width, (at + 1) * width)
        feed_gain_o[:, cols] = summed[row + 1 + at : row + 2 + at, :]
        gain_o[:, cols] = summed[row + 1 + wide + at : row + 2 + wide + at, :]
    outs.finish(grad_out_o)
    scatter.finish(grad_weight_o)

    def seq_done(k, carry):
        seq_copy(k).wait_send()
        return carry

    lax.fori_loop(0, ns - 1, seq_done, 0)
    for k in range(nm - 1):
        mp_copy(k).wait_send()


def last(sizes, rows, grads, proj_w, out_total, tokens, gain, grad_in, small):
    ns, nm = sizes
    depth, cols = proj_w.shape
    span = tokens.shape[1]
    shard = depth // ns
    width = (cols - LANES) // 3
    vector = (-(-(13 + 2 * (depth // width)) // 8) * 8, width)
    shape = jax.ShapeDtypeStruct
    line = shape((1, LANES), F32)
    return pl.pallas_call(
        functools.partial(last_kernel, sizes),
        out_shape=(
            shape(grad_in.shape, F32), shape((shard, cols), F32), shape((shard, width), F32),
            shape((3, 4, depth), F32), line, line, line, shape((1, depth), F32), shape((1, depth), F32),
        ),
        in_specs=[ANY, VMEM, VMEM, ANY] + [VMEM] * 8,
        out_specs=(VMEM,) * 9,
        scratch_shapes=[
            pltpu.VMEM(rows.shape, BF),
            pltpu.VMEM(rows.shape, BF),
            pltpu.VMEM((depth, cols), BF),
            pltpu.VMEM((depth, width), BF),
            pltpu.VMEM(vector, F32),
            pltpu.VMEM((ns - 1,) + vector, F32),
            pltpu.VMEM((nm,) + vector, F32),
            DMA((2,)), DMA((ns - 1,)), DMA((ns - 1,)), DMA((nm - 1,)), DMA((nm - 1,)),
        ]
        + LineScatter.scratch(nm, span, depth)
        + CubeScatter.scratch(ns, shard, cols)
        + CubeScatter.scratch(ns, shard, width),
        compiler_params=comm_params(3),
        name="last",
    )(rows, grads, proj_w, out_total, tokens, gain, grad_in, *small)


def deliver_kernel(
    block, grad_tokens, grad_proj, grad_gate, grad_up, grad_down, grad_out, conv, *rest
):
    lines, rest = rest[:5], rest[5:]
    (
        block_o, grad_tokens_o, query_o, key_o, value_o, grad_gate_o, grad_up_o, beta_o, grad_down_o,
        grad_out_o, conv_o,
    ) = rest[:11]
    line_os, rest = rest[11:16], rest[16:]
    block_v, tokens_v, proj_v, gate_v, up_v, down_v, out_v, down_t, out_t, conv_v = rest[:10]
    line_vs, sems = rest[10:15], rest[15]
    width = query_o.shape[1]
    coming = [
        (src, held, sems.at[k])
        for k, (src, held) in enumerate(
            (
                (grad_down, down_v), (grad_out, out_v), (grad_gate, gate_v), (grad_up, up_v),
                (block, block_v), (grad_tokens, tokens_v), (grad_proj, proj_v), (conv, conv_v),
            )
            + tuple(zip(lines, line_vs))
        )
    ]
    load(coming)
    going = []

    def send(held, dst):
        going.append((held, dst, sems.at[len(coming) + len(going)]))
        load(going[-1:])

    ready(coming[0:2])
    down_t[...] = down_v[...].T
    send(down_t, grad_down_o)
    out_t[...] = out_v[...].T
    send(out_t, grad_out_o)
    ready(coming[2:6])
    send(gate_v, grad_gate_o)
    send(up_v, grad_up_o)
    send(block_v, block_o)
    send(tokens_v, grad_tokens_o)
    ready(coming[6:])
    for k, dst in enumerate((query_o, key_o, value_o)):
        send(proj_v.at[:, pl.ds(k * width, width)], dst)
    beta_o[...] = proj_v[:, 3 * width :].T[: beta_o.shape[0], :]
    conv_o[...] = conv_v[...]
    for line, dst in zip(line_vs, line_os):
        dst[...] = line[:, : dst.shape[1]]
    ready(going)


def deliver(block, grad_tokens, grad_proj, grad_gate, grad_up, grad_down, grad_out, conv, lines, counts):
    shard, cols = grad_gate.shape
    width = (grad_proj.shape[1] - LANES) // 3
    heads = width // LANES
    shape = jax.ShapeDtypeStruct
    square = shape((shard, width), F32)
    wide = shape((shard, cols), F32)
    there = pl.BlockSpec(memory_space=pltpu.HBM)
    held = [
        block.shape, grad_tokens.shape, grad_proj.shape, (shard, cols), (shard, cols), (shard, cols),
        (shard, width), (cols, shard), (width, shard), conv.shape,
    ] + [line.shape for line in lines]
    return pl.pallas_call(
        deliver_kernel,
        out_shape=(
            shape(block.shape, F32), shape(grad_tokens.shape, F32), square, square, square, wide, wide,
            shape((heads, shard), F32), shape((cols, shard), F32), shape((width, shard), F32),
            shape(conv.shape, F32),
        )
        + tuple(shape((1, count), F32) for count in counts),
        in_specs=[there] * 13,
        out_specs=(there,) * 7 + (VMEM, there, there) + (VMEM,) * 6,
        scratch_shapes=[pltpu.VMEM(dims, F32) for dims in held] + [DMA((24,))],
        compiler_params=pltpu.CompilerParams(vmem_limit_bytes=63 * 2**20),
        name="deliver",
    )(block, grad_tokens, grad_proj, grad_gate, grad_up, grad_down, grad_out, conv, *lines)


def on_device(
    sizes,
    tokens,
    lengths,
    mixer_gain,
    query_weight,
    key_weight,
    value_weight,
    beta_weight,
    beta_bias,
    conv_weight,
    head_gain,
    out_weight,
    feed_gain,
    gate_weight,
    up_weight,
    down_weight,
    cotangent,
):
    ns, nm = sizes
    depth = tokens.shape[2]
    width = query_weight.shape[1]
    heads = width // LANES
    mixer_gain_row = mixer_gain.reshape(1, depth)
    feed_gain_row = feed_gain.reshape(1, depth)
    head_gain_row = head_gain.reshape(1, LANES)
    (
        rows, proj_w, out_w, gate_w, up_w, down_w, grad_rows, feed_rows,
        hidden_in, head_rows, projected, logits, edge, links, norms, entry, *saved,
    ) = mixer(
        sizes, tokens, cotangent, query_weight, key_weight, value_weight, beta_weight.T, out_weight,
        gate_weight, up_weight, down_weight, conv_weight, lengths, beta_bias, mixer_gain_row,
        head_gain_row, feed_gain_row,
    )
    grad_in, mix_rows, grad_gate, grad_up, grad_down_part, down_part, feed_gain_part = feed(
        sizes, feed_rows, grad_rows, gate_w, up_w, down_w, hidden_in, feed_gain_row, cotangent
    )
    grads, block_output, grad_down, conv_part, gain_part, bias_part, grad_out_part = backward(
        sizes, mix_rows, out_w, head_rows, projected, logits, conv_weight, lengths, beta_bias,
        head_gain_row, (edge, links, *saved, entry), grad_down_part, down_part, hidden_in,
    )
    (
        grad_tokens, grad_proj_w, grad_out, conv_grad, gain_grad, bias_grad, norm, feed_gain_grad,
        mixer_grad,
    ) = last(
        sizes, rows, grads, proj_w, grad_out_part, tokens, mixer_gain_row, grad_in,
        (conv_part, gain_part, bias_part, norms, feed_gain_part),
    )
    (
        block_output, grad_tokens, grad_query, grad_key, grad_value, grad_gate, grad_up, grad_beta,
        grad_down, grad_out, conv_grad, mixer_grad, feed_gain_grad, gain_grad, bias_grad, norm,
    ) = deliver(
        block_output, grad_tokens, grad_proj_w, grad_gate, grad_up, grad_down, grad_out, conv_grad,
        (mixer_grad, feed_gain_grad, gain_grad, bias_grad, norm), (depth, depth, LANES, nm * heads, 1),
    )
    return (
        block_output,
        grad_tokens,
        mixer_grad.reshape(depth),
        grad_query,
        grad_key,
        grad_value,
        grad_beta.T,
        bias_grad.reshape(nm * heads),
        conv_grad,
        gain_grad.reshape(LANES),
        grad_out,
        feed_gain_grad.reshape(depth),
        grad_gate,
        grad_up,
        grad_down,
        norm[0, 0],
    )


def solution(mesh):
    sizes = (mesh.shape["seq"], mesh.shape["mp"])
    by_rows = P("seq", "mp")
    by_cols = P("mp", "seq")
    placed = P(None, ("seq", "mp"), None)
    return jax.shard_map(
        functools.partial(on_device, sizes),
        mesh=mesh,
        in_specs=(
            placed, P(), P(), by_rows, by_rows, by_rows, by_rows, P(), P(), P(), by_cols, P(),
            by_rows, by_rows, by_cols, placed,
        ),
        out_specs=(
            placed, placed, P(), by_rows, by_rows, by_rows, by_rows, P(), P(), P(), by_cols, P(),
            by_rows, by_rows, by_cols, P(),
        ),
        check_vma=False,
    )
```

```python
import functools

import jax
import jax.numpy as jnp
from jax import lax
from jax.experimental import pallas as pl
from jax.experimental.pallas import tpu as pltpu
from jax.sharding import PartitionSpec as P

HEADS = 16
HEAD_DIM = 128
NSEQ = 2
EPSILON = 1e-05
KEY_EPSILON = 1e-06
LANES = 128
LEAD = 8
EDGE = 16
BF = jnp.bfloat16
F32 = jnp.float32
MESH = pl.DeviceIdType.MESH
VMEM = pl.BlockSpec(memory_space=pltpu.VMEM)
SMEM = pl.BlockSpec(memory_space=pltpu.SMEM)
ANY = pl.BlockSpec(memory_space=pl.ANY)
NN = (((1,), (0,)), ((), ()))
NT = (((1,), (1,)), ((), ()))
TN = (((0,), (0,)), ((), ()))
DMA = pltpu.SemaphoreType.DMA


def dot(left, right, dims=NN):
    return lax.dot_general(left, right, dims, preferred_element_type=F32)


def halves(values):
    high = values.astype(BF)
    return high, (values - high.astype(F32)).astype(BF)


def fine(left, right, dims=NN):
    return (
        dot(left[0], right[0], dims)
        + dot(left[0], right[1], dims)
        + dot(left[1], right[0], dims)
    )


def row_scale(values):
    return lax.rsqrt(jnp.mean(values * values, -1, keepdims=True) + EPSILON)


def norm_backward(grad_normed, unit_rows, scale):
    return scale * (grad_normed - unit_rows * jnp.mean(grad_normed * unit_rows, -1, keepdims=True))


def sigmoid(values):
    return 1.0 / (1.0 + jnp.exp(-values))


def iota(shape, dim):
    return lax.broadcasted_iota(jnp.int32, shape, dim)


def lower_mask(size, strict):
    rows, cols = iota((size, size), 0), iota((size, size), 1)
    return rows > cols if strict else rows >= cols


def unit_lower_inverses(lowers):
    size = LANES
    rows, cols = iota((size, size), 0), iota((size, size), 1)
    eye = (rows == cols).astype(F32)
    blocks = [low[at : at + size, at : at + size] for low in lowers for at in (0, size)]
    base = 16
    same = (rows // base) == (cols // base)
    minus = [jnp.where(same, -block, 0.0) for block in blocks]
    inverses = [eye + one for one in minus]
    pairs = [halves(one) for one in minus]
    powers = [fine(pair, pair) for pair in pairs]
    covered = 2
    while covered * 2 < base:
        lefts = [halves(jnp.concatenate((i, p), 0)) for i, p in zip(inverses, powers)]
        both = [fine(left, (left[0][size:], left[1][size:])) for left in lefts]
        inverses = [i + b[:size] for i, b in zip(inverses, both)]
        powers = [b[size:] for b in both]
        covered *= 2
    inverses = [i + fine(halves(i), halves(p)) for i, p in zip(inverses, powers)]
    while base < size:
        joined = (rows // (2 * base)) == (cols // (2 * base))
        cross = jnp.logical_and(joined, jnp.logical_not(same))
        pairs = [halves(i) for i in inverses]
        inner = [fine(halves(jnp.where(cross, b, 0.0)), i) for b, i in zip(blocks, pairs)]
        inverses = [i - fine(p, halves(x)) for i, p, x in zip(inverses, pairs, inner)]
        same = joined
        base *= 2
    pairs = [halves(i) for i in inverses]
    corners = [fine(halves(low[size:, :size]), pairs[2 * k]) for k, low in enumerate(lowers)]
    corners = [-fine(pairs[2 * k + 1], halves(c)) for k, c in enumerate(corners)]
    zero = jnp.zeros((size, size), F32)
    return [
        jnp.concatenate(
            (
                jnp.concatenate((inverses[2 * k], zero), 1),
                jnp.concatenate((corner, inverses[2 * k + 1]), 1),
            ),
            0,
        )
        for k, corner in enumerate(corners)
    ]


def flip(index, mask):
    out = index
    bit = 1
    while bit <= mask:
        if mask & bit:
            out = out + bit * (1 - 2 * ((index // bit) % 2))
        bit *= 2
    return out


def bits_of(count):
    out = []
    bit = 1
    while bit < count:
        out.insert(0, bit)
        bit *= 2
    return out


def two_orders(bits):
    if len(bits) < 2:
        return (bits, bits)
    return (list(bits), [bits[1], bits[0]] + list(bits[2:]))


def spans(bits):
    masks = [0]
    for bit in bits:
        masks = masks + [mask ^ bit for mask in masks]
    return masks


def remote(src, dst, send, recv, target):
    return pltpu.make_async_remote_copy(
        src_ref=src,
        dst_ref=dst,
        send_sem=send,
        recv_sem=recv,
        device_id=target,
        device_id_type=MESH,
    )


def greet(targets):
    barrier = pltpu.get_barrier_semaphore()
    for target in targets:
        pl.semaphore_signal(barrier, inc=1, device_id=target, device_id_type=MESH)


def await_all(targets):
    pl.semaphore_wait(pltpu.get_barrier_semaphore(), len(targets))


def meet(targets):
    greet(targets)
    await_all(targets)


def line_mates(geo):
    s, m = geo.s, geo.m
    return [(s, (m + 1) % geo.nm), (s, (m + geo.nm - 1) % geo.nm)]


def cube_mates(geo):
    return [(flip(geo.s, bit), geo.m) for bit in bits_of(geo.ns)]


def all_mates(geo):
    return [((geo.s + k) % geo.ns, geo.m) for k in range(1, geo.ns)]


class Geo:
    def __init__(self, sizes):
        self.ns, self.nm = sizes
        self.s = lax.axis_index("seq")
        self.m = lax.axis_index("mp")


class CubeGather:
    @staticmethod
    def sems(ns):
        return [DMA((2, ns - 1)), DMA((2, ns - 1)), DMA(())]

    def __init__(self, geo, shard, full, sems):
        self.geo, self.shard, self.full = geo, shard, full
        self.send, self.recv, self.local = sems
        self.rows = shard.shape[0]
        self.orders = two_orders(bits_of(geo.ns))
        self.ids = {}
        for order, bits in enumerate(self.orders):
            count = 0
            for step in range(len(bits)):
                for mask in spans(bits[:step]):
                    self.ids[order, step, mask] = count
                    count += 1
        self.todo = sorted(self.ids, key=lambda key: (key[1], bin(key[2]).count("1"), key[2], key[0]))
        self.started = []

    def block(self, order, mask):
        half = self.rows // 2
        start = flip(self.geo.s, mask) * self.rows + order * half
        return self.full.at[pl.ds(pl.multiple_of(start, half), half)]

    def copy(self, order, step, mask, incoming=False):
        bit = self.orders[order][step]
        half = self.rows // 2
        place = self.block(order, mask ^ bit if incoming else mask)
        src = self.shard.at[pl.ds(order * half, half)] if mask == 0 and not incoming else place
        at = self.ids[order, step, mask]
        return remote(
            src, place, self.send.at[order, at], self.recv.at[order, at],
            (flip(self.geo.s, bit), self.geo.m),
        )

    def own(self):
        start = pl.multiple_of(self.geo.s * self.rows, self.rows)
        return pltpu.make_async_copy(self.shard, self.full.at[pl.ds(start, self.rows)], self.local)

    def begin(self, steps=None):
        depth = len(self.orders[0])
        for step in range(depth) if steps is None else steps:
            for order in range(2):
                self.copy(order, step, 0).start()
            if step == depth - 1:
                self.own().start()

    def advance(self, count=None):
        count = len(self.todo) if count is None else count
        for order, step, mask in self.todo[:count]:
            self.copy(order, step, mask, incoming=True).wait_recv()
            after = mask ^ self.orders[order][step]
            for later in range(step + 1, len(self.orders[order])):
                self.copy(order, later, after).start()
        self.todo = self.todo[count:]

    def settle(self):
        self.advance()
        self.own().wait()

    def finish(self):
        for order, step, mask in self.ids:
            self.copy(order, step, mask).wait_send()


class CubeScatter:
    @staticmethod
    def scratch(ns, rows, cols):
        return [pltpu.VMEM((2, ns - 1, rows // 2, cols), BF), DMA((2, ns - 1)), DMA((2, ns - 1))]

    def __init__(self, geo, total, scratch):
        self.geo, self.total = geo, total
        self.slots, self.send, self.recv = scratch
        self.half = self.slots.shape[2]
        self.orders = [list(reversed(bits)) for bits in two_orders(bits_of(geo.ns))]
        self.ids = {}
        for order, bits in enumerate(self.orders):
            count = 0
            for step in range(len(bits)):
                for mask in reversed(spans(bits[step + 1 :])):
                    self.ids[order, step, mask] = count
                    count += 1
        depth = len(self.orders[0])

        def urgency(key):
            order, step, mask = key
            ahead = [k for k in range(depth) if mask & self.orders[order][k]]
            return (step, ahead[0] if ahead else depth, -mask, order)

        self.todo = sorted(self.ids, key=urgency)

    def rows(self, order, mask):
        start = flip(self.geo.s, mask) * (2 * self.half) + order * self.half
        return pl.ds(pl.multiple_of(start, self.half), self.half)

    def copy(self, order, step, mask):
        bit = self.orders[order][step]
        at = self.ids[order, step, mask]
        return remote(
            self.total.at[self.rows(order, mask ^ bit)], self.slots.at[order, at],
            self.send.at[order, at], self.recv.at[order, at],
            (flip(self.geo.s, bit), self.geo.m),
        )

    def begin(self):
        for order, step, mask in self.todo:
            if step == 0:
                self.copy(order, 0, mask).start()

    def advance(self, count=None):
        count = len(self.todo) if count is None else count
        for order, step, mask in self.todo[:count]:
            self.copy(order, step, mask).wait_recv()
            if mask == 0 and step == len(self.orders[order]) - 1:
                continue
            rows = self.rows(order, mask)
            slot = self.slots[order, self.ids[order, step, mask]]
            self.total[rows, :] = (self.total[rows, :].astype(F32) + slot.astype(F32)).astype(BF)
            bits = self.orders[order]
            if step + 1 < len(bits) and mask & bits[step + 1]:
                self.copy(order, step + 1, mask ^ bits[step + 1]).start()
        self.todo = self.todo[count:]

    def finish(self, out):
        self.advance()
        for order in range(2):
            last = self.ids[order, len(self.orders[order]) - 1, 0]
            out[pl.ds(order * self.half, self.half), :] = self.total[self.rows(order, 0), :].astype(
                F32
            ) + self.slots[order, last].astype(F32)
        for order, step, mask in self.ids:
            self.copy(order, step, mask).wait_send()


class LineGather:
    @staticmethod
    def sems(nm):
        return [DMA((2, NSEQ, nm - 1)), DMA((2, NSEQ, nm - 1))]

    def __init__(self, geo, full, sems):
        self.geo, self.full = geo, full
        self.send, self.recv = sems
        self.span = full.shape[1] // geo.nm

    def place(self, piece, origin):
        return self.full.at[piece, pl.ds(pl.multiple_of(origin * self.span, self.span), self.span)]

    def copy(self, way, piece, hop, incoming=False):
        m = self.geo.m
        sign = 1 if way == 0 else -1
        origin = m - sign * (hop + (1 if incoming else 0))
        place = self.place(piece, origin)
        return remote(
            place, place, self.send.at[way, piece, hop], self.recv.at[way, piece, hop],
            (self.geo.s, m + sign),
        )

    def sends(self, way, hop):
        m, nm = self.geo.m, self.geo.nm
        if way == 0:
            return jnp.logical_and(m >= hop, m < nm - 1)
        return jnp.logical_and(m <= nm - 1 - hop, m > 0)

    def receives(self, way, hop):
        m, nm = self.geo.m, self.geo.nm
        return m >= hop + 1 if way == 0 else m <= nm - 2 - hop

    def begin(self, piece):
        for way in range(2):
            @pl.when(self.sends(way, 0))
            def _(way=way):
                self.copy(way, piece, 0).start()

    def advance(self, piece, hop):
        for way in range(2):
            @pl.when(self.receives(way, hop))
            def _(way=way):
                self.copy(way, piece, hop, incoming=True).wait_recv()

            if hop + 1 < self.geo.nm - 1:
                @pl.when(self.sends(way, hop + 1))
                def _(way=way):
                    self.copy(way, piece, hop + 1).start()

    def finish(self, piece):
        for way in range(2):
            for hop in range(self.geo.nm - 1):
                @pl.when(self.sends(way, hop))
                def _(way=way, hop=hop):
                    self.copy(way, piece, hop).wait_send()


class LineScatter:
    @staticmethod
    def scratch(nm, span, cols):
        return [
            pltpu.VMEM((2, NSEQ, nm, span, cols), BF),
            DMA((2, NSEQ, nm)),
            DMA((2, NSEQ, nm)),
        ]

    def __init__(self, geo, part, scratch):
        self.geo, self.part = geo, part
        self.slots, self.send, self.recv = scratch
        self.span = self.slots.shape[3]

    def place(self, way):
        return self.geo.m if way == 0 else self.geo.nm - 1 - self.geo.m

    def own(self, way, piece, block):
        at = self.geo.nm - 1 - block if way == 0 else block
        start = at * self.span
        if not isinstance(start, int):
            start = pl.multiple_of(start, self.span)
        return self.part.at[piece, pl.ds(start, self.span)]

    def copy(self, way, piece, block, first=False):
        slot = self.slots.at[way, piece, block]
        src = self.own(way, piece, block) if first else slot
        step = 1 if way == 0 else -1
        return remote(
            src, slot, self.send.at[way, piece, block], self.recv.at[way, piece, block],
            (self.geo.s, self.geo.m + step),
        )

    def begin(self, piece):
        for way in range(2):
            @pl.when(self.place(way) == 0)
            def _(way=way):
                self.copy(way, piece, 0, True).start()

    def advance(self, piece, turn):
        forward = turn <= self.geo.nm - 2
        for way in range(2):
            at = self.place(way)
            if forward:
                @pl.when(at == 0)
                def _(way=way):
                    self.copy(way, piece, turn - 1, True).wait_send()
                    self.copy(way, piece, turn, True).start()

            @pl.when(jnp.logical_and(at >= 1, at <= turn))
            def _(way=way, block=turn - at):
                self.copy(way, piece, block).wait_recv()
                if forward:
                    slot = self.slots.at[way, piece, block]
                    own = self.own(way, piece, block)
                    slot[...] = (slot[...].astype(F32) + own[...].astype(F32)).astype(BF)
                    self.copy(way, piece, block).start()

    def result(self, piece, out):
        m, nm = self.geo.m, self.geo.nm
        own = self.part[piece, pl.ds(pl.multiple_of(m * self.span, self.span), self.span), :]
        out[piece] = own.astype(F32)

        @pl.when(m >= 1)
        def _():
            out[piece] = out[piece] + self.slots[0, piece, nm - 1 - m].astype(F32)

        @pl.when(m <= nm - 2)
        def _():
            out[piece] = out[piece] + self.slots[1, piece, m].astype(F32)

    def finish(self, piece):
        nm = self.geo.nm
        for way in range(2):
            at = self.place(way)
            for block in range(nm - 1):
                first = 0 if block == nm - 2 else 1

                @pl.when(jnp.logical_and(at >= first, at <= nm - 2 - block))
                def _(way=way, block=block):
                    self.copy(way, piece, block).wait_send()


def comm_params(collective, limit=60):
    return pltpu.CompilerParams(
        collective_id=collective, has_side_effects=True, vmem_limit_bytes=limit * 2**20
    )


def load(pairs):
    for src, dst, sem in pairs:
        pltpu.make_async_copy(src, dst, sem).start()


def ready(pairs):
    for src, dst, sem in pairs:
        pltpu.make_async_copy(src, dst, sem).wait()


GROUP = 4


def conv_row(conv, group, tap, column):
    return conv[group, pl.ds(tap, 1), pl.ds(pl.multiple_of(column, LANES), LANES)]


def before_silu(extended, conv, piece, group, head, width, rank):
    span = extended.shape[1] - LEAD
    cols = pl.ds(pl.multiple_of(group * width + head * LANES, LANES), LANES)
    total = None
    for tap in range(4):
        term = conv_row(conv, group, tap, rank * width + head * LANES) * extended[
            piece, pl.ds(LEAD - tap, span), cols
        ]
        total = term if total is None else total + term
    return total


def strengths_of(geo, logits, lengths, bias, local_heads, piece):
    span = logits.shape[1]
    lane = iota((span, LANES), 1)
    offset = jnp.zeros((span, LANES), F32)
    for head in range(local_heads):
        offset = jnp.where(lane == head, bias[geo.m * local_heads + head], offset)
    position = geo.s * span + iota((span, LANES), 0)
    live = jnp.where(position < lengths[piece], 1.0, 0.0)
    return sigmoid(logits[piece] + offset), live


def column_of(values, head):
    return jnp.sum(jnp.where(iota(values.shape, 1) == head, values, 0.0), -1, keepdims=True)


def fill_extended(extended, projected, edge, piece):
    extended[piece, LEAD:, :] = projected[piece].astype(F32)
    extended[piece, :LEAD, :] = edge[piece, EDGE - LEAD :, :].astype(F32)


class Chains:
    @staticmethod
    def scratch(ns, chains):
        return [
            pltpu.VMEM((ns, LANES, LANES), F32),
            DMA((chains,)), DMA((ns,)), DMA((ns,)), DMA((chains,)),
        ]

    def __init__(self, geo, chains, pair, links, entries, scratch):
        self.geo, self.chains = geo, chains
        self.pair, self.links, self.entries = pair, links, entries
        self.states, self.pair_send, self.pair_recv, self.back_send, self.back_recv = scratch
        self.stride = geo.ns // chains
        self.mine = geo.s // self.stride
        self.holds = geo.s == self.mine * self.stride

    def link_copy(self, chain):
        s, m = self.geo.s, self.geo.m
        return remote(
            self.pair.at[chain], self.links.at[s], self.pair_send.at[chain], self.pair_recv.at[s],
            (chain * self.stride, m),
        )

    def give(self, chain, link):
        owner = chain * self.stride

        @pl.when(owner == self.geo.s)
        def _():
            self.links[self.geo.s] = link

        @pl.when(owner != self.geo.s)
        def _():
            self.link_copy(chain).start()

    def state_copy(self, other):
        return remote(
            self.states.at[other], self.entries.at[self.mine], self.back_send.at[other],
            self.back_recv.at[self.mine], (other, self.geo.m),
        )

    def run(self, first, count, advance, start, reverse, last):
        ns, s, m = self.geo.ns, self.geo.s, self.geo.m

        @pl.when(jnp.logical_and(self.holds, jnp.logical_and(self.mine >= first, self.mine < first + count)))
        def _():
            def step(lap, carry):
                at = ns - 1 - lap if reverse else lap
                state = carry[0]
                self.states[at] = state

                @pl.when(at == s)
                def _():
                    self.entries[self.mine] = state

                @pl.when(at != s)
                def _():
                    self.state_copy(at).start()
                    remote(
                        self.pair.at[0], self.links.at[at], self.pair_send.at[0],
                        self.pair_recv.at[at], (s, m),
                    ).wait_recv()

                return advance(carry, at)

            last(lax.fori_loop(0, ns, step, start))

    def receive(self, chain):
        @pl.when(chain * self.stride != self.geo.s)
        def _():
            remote(
                self.states.at[0], self.entries.at[chain], self.back_send.at[0],
                self.back_recv.at[chain], (self.geo.s, self.geo.m),
            ).wait_recv()

    def finish(self):
        def sent(chain, carry):
            @pl.when(chain * self.stride != self.geo.s)
            def _():
                self.link_copy(chain).wait_send()

            return carry

        lax.fori_loop(0, self.chains, sent, 0)

        @pl.when(self.holds)
        def _():
            def done(other, carry):
                @pl.when(other != self.geo.s)
                def _():
                    self.state_copy(other).wait_send()

                return carry

            lax.fori_loop(0, self.geo.ns, done, 0)


def mixer_kernel(
    sizes, tokens, cotangent, query_w, key_w, value_w, beta_w, out_in, gate_hbm, up_hbm, down_in,
    conv, lengths, bias, mixer_gain, head_gain, feed_gain,
    rows_o, proj_w_o, out_w_o, gate_w_o, up_w_o, down_w_o, grad_rows_o, feed_rows_o,
    hidden_in, head_rows, projected, logits, edge, links, norm_o, entry_o,
    solve_h, wkeys_h, fresh_h, error_h, outputs_h, queries_h, keys_h,
    solve_o, wkeys_o, fresh_o, error_o, outputs_o, queries_o, keys_o,
    proj_shard, out_shard, gate_shard, up_shard, down_shard,
    rows, weight, out_w, grad_rows, feed_rows, part, extended, betas, wvalues, pair,
    keep, edge_send, edge_recv, *rest,
):
    geo = Geo(sizes)
    ns, nm, s, m = geo.ns, geo.nm, geo.s, geo.m
    mates = line_mates(geo) + all_mates(geo)
    greet(mates)
    shards = [(gate_hbm, gate_shard, keep.at[0]), (up_hbm, up_shard, keep.at[1])]
    load(shards)
    width = query_w.shape[1]
    heads = width // LANES
    chains = NSEQ * heads
    span = projected.shape[1]
    proj_shard[:, 0:width] = query_w[...]
    proj_shard[:, width : 2 * width] = key_w[...]
    proj_shard[:, 2 * width : 3 * width] = value_w[...]
    proj_shard[:, 3 * width :] = jnp.zeros((proj_shard.shape[0], LANES), BF)
    proj_shard[:, 3 * width : 3 * width + heads] = beta_w[...].astype(F32).T.astype(BF)
    out_shard[...] = out_in[...].T
    await_all(mates)

    weights = CubeGather(geo, proj_shard, weight, rest[0:3])
    outs = CubeGather(geo, out_shard, out_w, rest[3:6])
    gates = CubeGather(geo, gate_shard, gate_w_o, rest[6:9])
    ups = CubeGather(geo, up_shard, up_w_o, rest[9:12])
    downs = CubeGather(geo, down_shard, down_w_o, rest[12:15])
    spread = LineGather(geo, rows, rest[15:17])
    spread_grad = LineGather(geo, grad_rows, rest[17:19])
    spread_feed = LineGather(geo, feed_rows, rest[19:21])
    collect = LineScatter(geo, part, rest[21:24])
    chain = Chains(geo, chains, pair, links, entry_o, rest[24:29])

    weights.begin()
    own_rows = tokens.shape[1]
    mine = pl.ds(pl.multiple_of(m * own_rows, own_rows), own_rows)
    for piece in range(NSEQ):
        values = tokens[piece].astype(F32)
        rows[piece, mine, :] = (values * row_scale(values) * mixer_gain[...]).astype(BF)
        grad_rows[piece, mine, :] = cotangent[piece]
        if piece == 0:
            spread.begin(0)
    down_shard[...] = down_in[...].T
    spread.advance(0, 0)
    spread.begin(1)
    weights.advance(2)
    outs.begin()
    for hop in range(1, nm - 1):
        spread.advance(0, hop)
        weights.advance(2)
        spread.advance(1, hop - 1)
    outs.advance(2)
    weights.settle()
    ready(shards)
    kept = [(weight, proj_w_o, keep.at[2])]
    load(kept)
    strict = lower_mask(span, True)
    whole = lower_mask(span, False)
    norm_o[...] = jnp.zeros(norm_o.shape, F32)

    def edge_copy(piece):
        return remote(
            projected.at[piece, pl.ds(span - EDGE, EDGE)], edge.at[piece],
            edge_send.at[piece], edge_recv.at[piece], (s + 1, m),
        )

    def run_chains(piece):
        def advance(carry, at):
            state, total = carry
            link = links[at]
            high, low = halves(state)
            move = link[:, :LANES]
            state = state - (dot(move, high) + dot(move, low)) + link[:, LANES:].astype(F32)
            return state, total + jnp.sqrt(jnp.sum(state * state, (0, 1), keepdims=True))

        def last(carry):
            norm_o[...] = norm_o[...] + carry[1]

        start = (jnp.zeros((LANES, LANES), F32), jnp.zeros((1, 1), F32))
        chain.run(piece * heads, heads, advance, start, False, last)

    groups = heads // GROUP

    def solve(piece, carry):
        @pl.when(piece == 1)
        def _():
            for hop in range(nm - 2, nm - 1):
                spread.advance(1, hop)

        result = dot(rows[piece], weight[...])
        projected[piece] = result[:, : 3 * width].astype(BF)
        logits[piece] = result[:, 3 * width :]

        @pl.when(s < ns - 1)
        def _():
            edge_copy(piece).start()

        strength, live = strengths_of(geo, logits, lengths, bias, heads, piece)
        betas[piece] = strength * live

        @pl.when(piece == 0)
        def _():
            gates.begin((0,))
            for at in range(NSEQ):
                spread_grad.begin(at)

        @pl.when(s > 0)
        def _():
            edge_copy(piece).wait_recv()

        @pl.when(s == 0)
        def _():
            edge[piece] = jnp.zeros(edge.shape[1:], BF)

        fill_extended(extended, projected, edge, piece)
        for first in range(0, heads, GROUP):
            which = [first + k for k in range(GROUP)]
            mixed = [
                [before_silu(extended, conv, piece, g, head, width, m) for g in range(3)]
                for head in which
            ]
            mixed = [[z * sigmoid(z) for z in three] for three in mixed]
            queries = [three[0] for three in mixed]
            keys = [
                key * lax.rsqrt(jnp.sum(key * key, -1, keepdims=True) + KEY_EPSILON)
                for _, key, _ in mixed
            ]
            values = [three[2] for three in mixed]
            strengths = [column_of(betas[piece], head) for head in which]
            key_pairs = [halves(key) for key in keys]
            grams = [jnp.where(strict, fine(key, key, NT), 0.0) for key in key_pairs]
            inverses = unit_lower_inverses([gram * beta for gram, beta in zip(grams, strengths)])
            both = [
                halves(jnp.concatenate((key * beta, value * beta), 1))
                for key, value, beta in zip(keys, values, strengths)
            ]
            both = [fine(halves(inverse), right) for inverse, right in zip(inverses, both)]
            found = [fine(key, halves(two), TN).astype(BF) for key, two in zip(key_pairs, both)]
            done = list(zip(queries, keys, values, inverses, both, found))
            for k, (query, key, value, inverse, both, link) in enumerate(done):
                at = piece * heads + first + k
                pair[at] = link
                solve_o[at] = inverse
                wkeys_o[at] = both[:, :LANES]
                wvalues[at] = both[:, LANES:]
                queries_o[at] = query
                keys_o[at] = key
                error_o[at] = value
            for k, found in enumerate(done):
                chain.give(piece * heads + first + k, found[-1])
        return carry

    lax.fori_loop(0, NSEQ, solve, 0)
    saved = [
        (solve_o, solve_h, keep.at[7]), (wkeys_o, wkeys_h, keep.at[8]),
        (queries_o, queries_h, keep.at[9]), (keys_o, keys_h, keep.at[10]),
    ]
    load(saved)
    for piece in range(NSEQ):
        spread_grad.advance(piece, 0)
    outs.settle()
    for piece in range(NSEQ):
        run_chains(piece)

    def gates_on():
        gates.begin(range(1, len(gates.orders[0])))
        gates.advance(2)
        ups.begin()
        downs.begin()

    def apply(piece, then=None):
        def step(lap, carry):
            first = piece * heads + lap * GROUP
            for k in range(GROUP):
                chain.receive(first + k)
            if then is not None:
                then()
            which = [first + k for k in range(GROUP)]
            states = [halves(entry_o[at]) for at in which]
            key_pairs = [halves(keys_o[at]) for at in which]
            query_pairs = [halves(queries_o[at]) for at in which]
            fresh = [
                wvalues[at] - fine(halves(wkeys_o[at]), state) for at, state in zip(which, states)
            ]
            fresh_pairs = [halves(one) for one in fresh]
            grams = [jnp.where(strict, fine(key, key, NT), 0.0) for key in key_pairs]
            scores = [
                jnp.where(whole, fine(query, key, NT), 0.0)
                for query, key in zip(query_pairs, key_pairs)
            ]
            errors = [
                error_o[at] - fine(key, state) - fine(halves(gram), new)
                for at, key, state, gram, new in zip(which, key_pairs, states, grams, fresh_pairs)
            ]
            outputs = [
                fine(query, state) + fine(halves(score), new)
                for query, state, score, new in zip(query_pairs, states, scores, fresh_pairs)
            ]
            done = list(zip(fresh, errors, outputs))
            for k, (fresh, error, output) in enumerate(done):
                at = first + k
                fresh_o[at] = fresh
                error_o[at] = error
                outputs_o[at] = output
                cols = pl.ds(pl.multiple_of((lap * GROUP + k) * LANES, LANES), LANES)
                head_rows[piece, :, cols] = (output * row_scale(output) * head_gain[...]).astype(BF)
            return carry

        lax.fori_loop(0, groups, step, 0)
        part[piece] = dot(head_rows[piece], out_w[...], NT).astype(BF)

    def close(piece):
        collect.result(piece, hidden_in)
        values = hidden_in[piece] + tokens[piece].astype(F32)
        hidden_in[piece] = values
        feed_rows[piece, mine, :] = (values * row_scale(values) * feed_gain[...]).astype(BF)
        spread_feed.begin(piece)

    for piece in range(NSEQ):
        spread_grad.advance(piece, 1)
    apply(0)
    collect.begin(0)
    apply(1, gates_on)
    kept.append((out_w, out_w_o, keep.at[4]))
    later = [
        (fresh_o, fresh_h, keep.at[11]), (error_o, error_h, keep.at[12]),
        (outputs_o, outputs_h, keep.at[13]),
    ]
    load(kept[-1:] + later)
    collect.advance(0, 1)
    for piece in range(NSEQ):
        for hop in range(2, nm - 2):
            spread_grad.advance(piece, hop)
    collect.advance(0, 2)
    collect.begin(1)
    for turn in range(3, nm):
        collect.advance(0, turn)
    close(0)
    collect.advance(1, 1)
    gates.advance(4)
    spread_feed.advance(0, 0)
    collect.advance(1, 2)
    gates.advance()
    spread_feed.advance(0, 1)
    for turn in range(3, nm):
        collect.advance(1, turn)
    close(1)
    ups.advance(4)
    downs.advance(4)
    for hop in range(2, nm - 1):
        spread_feed.advance(0, hop)
    for piece in range(NSEQ):
        spread_grad.advance(piece, nm - 2)
    late = [
        (feed_rows.at[0], feed_rows_o.at[0], keep.at[5]), (grad_rows, grad_rows_o, keep.at[6]),
        (rows, rows_o, keep.at[3]), (feed_rows.at[1], feed_rows_o.at[1], keep.at[14]),
    ]
    load(late[:3])
    spread_feed.advance(1, 0)
    ups.advance(2)
    for hop in range(1, nm - 1):
        spread_feed.advance(1, hop)
    load(late[3:])
    downs.advance(2)
    ups.advance()
    downs.advance()
    for piece in range(NSEQ):
        spread.finish(piece)
        collect.finish(piece)
        spread_grad.finish(piece)
        spread_feed.finish(piece)
    for gather in (gates, ups, downs):
        gather.settle()
    for gather in (weights, outs, gates, ups, downs):
        gather.finish()
    for piece in range(NSEQ):
        @pl.when(s < ns - 1)
        def _(piece=piece):
            edge_copy(piece).wait_send()

    chain.finish()
    ready(kept + saved + later + late)


def mixer(
    sizes, tokens, cotangent, query_w, key_w, value_w, beta_w, out_in, gate_in, up_in, down_in,
    conv, lengths, bias, mixer_gain, head_gain, feed_gain,
):
    ns, nm = sizes
    width = query_w.shape[1]
    shard = query_w.shape[0]
    depth = ns * shard
    cols = gate_in.shape[1]
    own = tokens.shape
    span = own[1] * nm
    heads = width // LANES
    chains = NSEQ * heads
    rows = (NSEQ, span, depth)
    joined = 3 * width + LANES
    shape = jax.ShapeDtypeStruct
    per_chain = (chains, span, LANES)
    return pl.pallas_call(
        functools.partial(mixer_kernel, sizes),
        out_shape=(
            shape(rows, BF), shape((depth, joined), BF), shape((depth, width), BF),
            shape((depth, cols), BF), shape((depth, cols), BF), shape((depth, cols), BF),
            shape(rows, BF), shape(rows, BF),
            shape(own, F32), shape((NSEQ, span, width), BF), shape((NSEQ, span, 3 * width), BF),
            shape((NSEQ, span, LANES), F32), shape((NSEQ, EDGE, 3 * width), BF),
            shape((ns, LANES, 2 * LANES), BF), shape((8, LANES), F32),
            shape((chains, LANES, LANES), F32), shape((chains, span, span), F32),
        )
        + (shape(per_chain, F32),) * 6,
        in_specs=[VMEM] * 7 + [ANY, ANY, VMEM, VMEM, SMEM, SMEM, VMEM, VMEM, VMEM],
        out_specs=(ANY,) * 8 + (VMEM,) * 8 + (ANY,) * 7,
        scratch_shapes=[pltpu.VMEM((chains, span, span), F32)]
        + [pltpu.VMEM(per_chain, F32)] * 6
        + [
            pltpu.VMEM((shard, joined), BF), pltpu.VMEM((shard, width), BF),
            pltpu.VMEM((shard, cols), BF), pltpu.VMEM((shard, cols), BF), pltpu.VMEM((shard, cols), BF),
            pltpu.VMEM(rows, BF), pltpu.VMEM((depth, joined), BF), pltpu.VMEM((depth, width), BF),
            pltpu.VMEM(rows, BF), pltpu.VMEM(rows, BF), pltpu.VMEM(rows, BF),
            pltpu.VMEM((NSEQ, LEAD + span, 3 * width), F32),
            pltpu.VMEM((NSEQ, span, LANES), F32),
            pltpu.VMEM(per_chain, F32),
            pltpu.VMEM((chains, LANES, 2 * LANES), BF),
            DMA((15,)), DMA((NSEQ,)), DMA((NSEQ,)),
        ]
        + CubeGather.sems(ns) * 5
        + LineGather.sems(nm) * 3
        + LineScatter.scratch(nm, own[1], depth)
        + Chains.scratch(ns, chains),
        compiler_params=comm_params(0),
        name="mixer",
    )(
        tokens, cotangent, query_w, key_w, value_w, beta_w, out_in, gate_in, up_in, down_in,
        conv, lengths, bias, mixer_gain, head_gain, feed_gain,
    )


def feed_kernel(
    sizes, feed_rows_h, grad_rows_h, gate_hbm, up_hbm, down_hbm, hidden_in, gain, cotangent,
    grad_in, mix_rows_o, grad_gate_o, grad_up_o, grad_down_o, down_part_o, gain_o,
    feed_rows, grad_rows, gate_w, up_w, down_w, hidden, grad_gate, grad_up, part, mix_rows,
    keep, *rest,
):
    geo = Geo(sizes)
    nm = geo.nm
    mates = line_mates(geo) + cube_mates(geo)
    greet(mates)
    weights = [
        (gate_hbm, gate_w, keep.at[0]), (up_hbm, up_w, keep.at[1]), (down_hbm, down_w, keep.at[2])
    ]
    inputs = [(feed_rows_h, feed_rows, keep.at[3]), (grad_rows_h, grad_rows, keep.at[4])]
    load(inputs[:1] + weights[:2] + inputs[1:] + weights[2:])
    collect = LineScatter(geo, part, rest[0:3])
    spread = LineGather(geo, mix_rows, rest[3:5])
    first = CubeScatter(geo, gate_w, rest[5:8])
    second = CubeScatter(geo, up_w, rest[8:11])
    for piece in range(NSEQ):
        if piece == 0:
            ready(inputs[:1] + weights[:1])
        gate = dot(feed_rows[piece], gate_w[...])
        if piece == 0:
            ready(weights[1:2])
        up = dot(feed_rows[piece], up_w[...])
        sig = sigmoid(gate)
        active = gate * sig
        hidden[piece] = (active * up).astype(BF)
        if piece == 0:
            ready(inputs[1:] + weights[2:])
        grad_hidden = dot(grad_rows[piece], down_w[...])
        grad_gate[piece] = (grad_hidden * up * sig * (1.0 + gate * (1.0 - sig))).astype(BF)
        grad_up[piece] = (grad_hidden * active).astype(BF)
        part[piece] = (
            dot(grad_gate[piece], gate_w[...], NT) + dot(grad_up[piece], up_w[...], NT)
        ).astype(BF)
        if piece == 0:
            await_all(mates)
            collect.begin(0)
    depth, cols = gate_w.shape
    tile = 512
    span = hidden_in.shape[1]
    mine = pl.ds(pl.multiple_of(geo.m * span, span), span)

    def weight_grad(rows, grads, out):
        def step(at, carry):
            window = pl.ds(pl.multiple_of(at * tile, tile), tile)
            total = dot(rows[0, :, window], grads[0], TN) + dot(rows[1, :, window], grads[1], TN)
            out[window, :] = total.astype(BF)
            return carry

        lax.fori_loop(0, depth // tile, step, 0)

    def close(piece):
        collect.result(piece, grad_in)
        grad_feed = grad_in[piece]
        rows = hidden_in[piece]
        scale = row_scale(rows)
        unit = rows * scale
        part_gain = jnp.sum(grad_feed * unit, 0, keepdims=True)
        if piece == 0:
            gain_o[...] = part_gain
        else:
            gain_o[...] = gain_o[...] + part_gain
        back = cotangent[piece].astype(F32) + norm_backward(grad_feed * gain[...], unit, scale)
        grad_in[piece] = back
        mix_rows[piece, mine, :] = back.astype(BF)
        spread.begin(piece)

    collect.advance(0, 1)
    weight_grad(feed_rows, grad_gate, gate_w)
    first.begin()
    collect.advance(0, 2)
    collect.begin(1)
    weight_grad(feed_rows, grad_up, up_w)
    second.begin()
    first.advance(8)
    for turn in range(3, nm):
        collect.advance(0, turn)
    close(0)
    collect.advance(1, 1)
    second.advance(8)
    spread.advance(0, 0)
    collect.advance(1, 2)
    first.advance(4)
    spread.advance(0, 1)
    for turn in range(3, nm):
        collect.advance(1, turn)
    close(1)
    for piece in range(NSEQ):
        collect.finish(piece)
        part[piece] = dot(hidden[piece], down_w[...], NT).astype(BF)
    later = [(part, down_part_o, keep.at[0])]
    load(later)
    for hop in range(2, nm - 1):
        spread.advance(0, hop)
    second.advance(4)
    spread.advance(1, 0)
    weight_grad(grad_rows, hidden, down_w)
    later.append((down_w, grad_down_o, keep.at[1]))
    load(later[1:])
    for hop in range(1, nm - 1):
        spread.advance(1, hop)
    for piece in range(NSEQ):
        spread.finish(piece)
    later.append((mix_rows, mix_rows_o, keep.at[2]))
    load(later[2:])
    first.finish(grad_gate_o)
    second.finish(grad_up_o)
    ready(later)


def feed(sizes, feed_rows, grad_rows, gate_w, up_w, down_w, hidden_in, gain, cotangent):
    ns, nm = sizes
    depth, cols = gate_w.shape
    span = hidden_in.shape[1]
    shard = depth // ns
    rows = (NSEQ, span * nm, depth)
    inner = (NSEQ, span * nm, cols)
    return pl.pallas_call(
        functools.partial(feed_kernel, sizes),
        out_shape=(
            jax.ShapeDtypeStruct((NSEQ, span, depth), F32),
            jax.ShapeDtypeStruct(rows, BF),
            jax.ShapeDtypeStruct((shard, cols), F32),
            jax.ShapeDtypeStruct((shard, cols), F32),
            jax.ShapeDtypeStruct((depth, cols), BF),
            jax.ShapeDtypeStruct(rows, BF),
            jax.ShapeDtypeStruct((1, depth), F32),
        ),
        in_specs=[ANY] * 5 + [VMEM] * 3,
        out_specs=(VMEM, ANY, VMEM, VMEM, ANY, ANY, VMEM),
        scratch_shapes=[
            pltpu.VMEM(rows, BF), pltpu.VMEM(rows, BF),
            pltpu.VMEM((depth, cols), BF), pltpu.VMEM((depth, cols), BF), pltpu.VMEM((depth, cols), BF),
            pltpu.VMEM(inner, BF), pltpu.VMEM(inner, BF), pltpu.VMEM(inner, BF),
            pltpu.VMEM(rows, BF), pltpu.VMEM(rows, BF), DMA((5,)),
        ]
        + LineScatter.scratch(nm, span, depth)
        + LineGather.sems(nm)
        + CubeScatter.scratch(ns, shard, cols) * 2,
        compiler_params=comm_params(1, 63),
        name="feed",
    )(feed_rows, grad_rows, gate_w, up_w, down_w, hidden_in, gain, cotangent)


def backward_kernel(
    sizes, mix_rows_h, out_weight_h, head_rows, projected, logits, conv, lengths, bias, gain,
    edge, links, solve_h, wkeys_h, fresh_h, error_h, outputs_h, queries_h, keys_h, entry,
    grad_down_hbm, down_part_hbm, hidden_in,
    grads_o, block_o, grad_down_o, conv_o, gain_o, bias_o, out_total_o,
    mix_rows, out_weight, solve, fresh, error, queries, keys,
    extended, betas, grad_output, held, grad_mixed, grad_tail, grad_logit,
    pair, gathered, leaving, edge_out, edge_in, out_total, down_total, down_part, keep,
    edge_send, edge_recv, *rest,
):
    geo = Geo(sizes)
    ns, nm, s, m = geo.ns, geo.nm, geo.s, geo.m
    span, width = projected.shape[1], projected.shape[2] // 3
    heads = width // LANES
    chains = NSEQ * heads
    which = range(heads)
    mates = line_mates(geo) + all_mates(geo)
    greet(mates)
    kept = [(out_total, out_total_o, keep.at[11])]
    loads = [
        (down_part_hbm, down_part, keep.at[0]), (grad_down_hbm, down_total, keep.at[1]),
        (mix_rows_h, mix_rows, keep.at[2]), (out_weight_h, out_weight, keep.at[3]),
        (outputs_h, grad_output, keep.at[4]), (queries_h, queries, keep.at[5]),
        (keys_h, keys, keep.at[6]), (wkeys_h, held, keep.at[7]),
        (fresh_h, fresh, keep.at[8]), (solve_h, solve, keep.at[9]), (error_h, error, keep.at[10]),
    ]
    load(loads)
    collect = LineScatter(geo, down_part, rest[0:3])
    first = CubeScatter(geo, down_total, rest[3:6])
    chain = Chains(geo, chains, pair, gathered, leaving, rest[6:11])
    strict = lower_mask(span, True)
    whole = lower_mask(span, False)
    gain_o[...] = jnp.zeros(gain_o.shape, F32)
    conv_o[...] = jnp.zeros(conv_o.shape, F32)
    pad = grad_mixed.shape[1] - LEAD - span
    for piece in range(NSEQ):
        grad_mixed[piece, :LEAD, :] = jnp.zeros((LEAD, 3 * width), F32)
        grad_mixed[piece, LEAD + span :, :] = jnp.zeros((pad, 3 * width), F32)
        fill_extended(extended, projected, edge, piece)
        strength, live = strengths_of(geo, logits, lengths, bias, heads, piece)
        betas[piece] = strength * live
    await_all(mates)
    ready(loads[:1])
    for piece in range(NSEQ):
        collect.begin(piece)
    ready(loads[1:2])
    first.begin()
    ready(loads[2:8])

    def start(piece, carry):
        grad_head = dot(mix_rows[piece], out_weight[...])
        scaled = [grad_output[piece * heads + h] for h in which]
        scales = [row_scale(output) for output in scaled]
        units = [output * scale for output, scale in zip(scaled, scales)]
        grads = [grad_head[:, h * LANES : (h + 1) * LANES] for h in which]
        share = [jnp.sum(grad * unit, 0, keepdims=True) for grad, unit in zip(grads, units)]
        gain_o[...] = gain_o[...] + sum(share)
        grads = [
            norm_backward(grad * gain[...], unit, scale)
            for grad, unit, scale in zip(grads, units, scales)
        ]
        grad_pairs = [halves(grad) for grad in grads]
        query_pairs = [halves(queries[piece * heads + h]) for h in which]
        scores = [
            jnp.where(whole, fine(query, halves(keys[piece * heads + h]), NT), 0.0)
            for h, query in zip(which, query_pairs)
        ]
        spread = [fine(halves(score), grad, TN) for score, grad in zip(scores, grad_pairs)]
        found = [
            fine(query, grad, TN) - fine(halves(held[piece * heads + h]), halves(one), TN)
            for h, query, grad, one in zip(which, query_pairs, grad_pairs, spread)
        ]
        found = [link.astype(BF) for link in found]
        for h in which:
            at = piece * heads + h
            grad_output[at] = grads[h]
            held[at] = spread[h]
            pair[at] = found[h]
        for h in which:
            chain.give(piece * heads + h, found[h])
        return carry

    lax.fori_loop(0, NSEQ, start, 0)
    first.advance(2)
    ready(loads[8:])

    def through_conv(piece, h, group, grad, key=None):
        z = before_silu(extended, conv, piece, group, h, width, m)
        sig = sigmoid(z)
        if key is not None:
            raw = z * sig
            scale = lax.rsqrt(jnp.sum(raw * raw, -1, keepdims=True) + KEY_EPSILON)
            grad = scale * (grad - key * jnp.sum(key * grad, -1, keepdims=True))
        grad = grad * sig * (1.0 + z * (1.0 - sig))
        cols = slice(group * width + h * LANES, group * width + (h + 1) * LANES)
        local = slice(h * LANES, (h + 1) * LANES)
        grad_mixed[piece, pl.ds(LEAD, span), cols] = grad
        back = None
        for tap in range(4):
            share = jnp.sum(grad * extended[piece, pl.ds(LEAD - tap, span), cols], 0, keepdims=True)
            row = slice(group * 4 + tap, group * 4 + tap + 1)
            conv_o[row, local] = conv_o[row, local] + share
            term = (
                conv_row(conv, group, tap, m * width + h * LANES)
                * grad_mixed[piece, pl.ds(tap, LEAD + span), cols]
            )
            back = term if back is None else back + term
        edge_out[piece, :, cols] = back[:LEAD]
        grads_o[piece, :, cols] = back[LEAD:].astype(BF)
        grad_tail[piece, :, cols] = back[LEAD + span - EDGE :]

    def before_exit(piece):
        base = piece * heads
        grad_pairs = [halves(grad_output[base + h]) for h in which]
        key_pairs = [halves(keys[base + h]) for h in which]
        scores = [
            halves(jnp.where(whole, fine(grad, halves(fresh[base + h]), NT), 0.0))
            for h, grad in zip(which, grad_pairs)
        ]
        grads = [
            fine(score, key) + fine(grad, halves(entry[base + h]), NT)
            for h, score, key, grad in zip(which, scores, key_pairs, grad_pairs)
        ]
        to_keys = [
            fine(score, halves(queries[base + h]), TN) for h, score in zip(which, scores)
        ]
        for h in which:
            grad_output[base + h] = to_keys[h]
        for h in which:
            through_conv(piece, h, 0, grads[h])

    def after_exit(piece):
        base = piece * heads
        for h in which:
            chain.receive(base + h)

        @pl.when(piece == 0)
        def _():
            first.advance(6)

        key_pairs = [halves(keys[base + h]) for h in which]
        exits = [halves(leaving[base + h]) for h in which]
        fresh_pairs = [halves(fresh[base + h]) for h in which]
        strengths = [column_of(betas[piece], h) for h in which]
        weak = [halves(held[base + h] + fine(key, out)) for h, key, out in zip(which, key_pairs, exits)]
        weak = [fine(halves(solve[base + h]), one, TN) for h, one in zip(which, weak)]
        grad_beta = [jnp.sum(one * error[base + h], -1, keepdims=True) for h, one in zip(which, weak)]
        values = [one * beta for one, beta in zip(weak, strengths)]
        value_pairs = [halves(value) for value in values]
        scores = [
            halves(jnp.where(strict, -fine(value, new, NT), 0.0))
            for value, new in zip(value_pairs, fresh_pairs)
        ]
        grads = [
            grad_output[base + h]
            - fine(value, halves(entry[base + h]), NT)
            + fine(score, key)
            + fine(score, key, TN)
            + fine(new, out, NT)
            for h, value, score, key, new, out in zip(
                which, value_pairs, scores, key_pairs, fresh_pairs, exits
            )
        ]
        lane = iota((span, LANES), 1)
        grad_logit[piece] = sum(jnp.where(lane == h, grad_beta[h], 0.0) for h in which)
        for h in which:
            through_conv(piece, h, 1, grads[h], keys[base + h])
            through_conv(piece, h, 2, values[h])

    def run_chains(piece):
        def advance(carry, at):
            (state,) = carry
            high, low = halves(state)
            move = links[at][:, :LANES]
            state = state - (dot(move, high, TN) + dot(move, low, TN)) + gathered[at].astype(F32)
            return (state,)

        chain.run(
            piece * heads, heads, advance, (jnp.zeros((LANES, LANES), F32),), True, lambda carry: None
        )

    def edge_copy(piece):
        return remote(
            edge_out.at[piece], edge_in.at[piece], edge_send.at[piece], edge_recv.at[piece],
            (s - 1, m),
        )

    depth = out_weight.shape[0]
    tile = 512

    def weight_grad(at, carry):
        window = pl.ds(pl.multiple_of(at * tile, tile), tile)
        total = dot(mix_rows[0, :, window], head_rows[0], TN) + dot(
            mix_rows[1, :, window], head_rows[1], TN
        )
        out_total[window, :] = total.astype(BF)
        return carry

    def leave(piece, carry):
        before_exit(piece)

        @pl.when(piece == 0)
        def _():
            for at in range(NSEQ):
                run_chains(at)
            lax.fori_loop(0, depth // tile, weight_grad, 0)
            load(kept)
            for at in range(NSEQ):
                collect.advance(at, 1)

        return carry

    lax.fori_loop(0, NSEQ, leave, 0)

    def enter(piece, carry):
        after_exit(piece)

        @pl.when(s > 0)
        def _():
            edge_copy(piece).start()

        @pl.when(piece == 0)
        def _():
            for at in range(NSEQ):
                collect.advance(at, 2)

        return carry

    lax.fori_loop(0, NSEQ, enter, 0)
    bias_sum = jnp.zeros((1, LANES), F32)
    for piece in range(NSEQ):
        sig, live = strengths_of(geo, logits, lengths, bias, heads, piece)
        grad = grad_logit[piece] * live * sig * (1.0 - sig)
        bias_sum = bias_sum + jnp.sum(grad, 0, keepdims=True)
        grads_o[piece, :, pl.ds(3 * width, LANES)] = grad.astype(BF)
    lane = iota((1, LANES), 1)
    spread_bias = jnp.zeros((1, LANES), F32)
    for h in which:
        spread_bias = spread_bias + jnp.where(lane == m * heads + h, column_of(bias_sum, h), 0.0)
    bias_o[...] = spread_bias
    first.advance(4)
    for turn in range(3, nm):
        for piece in range(NSEQ):
            collect.advance(piece, turn)
    for piece in range(NSEQ):
        collect.result(piece, block_o)
        block_o[piece] = block_o[piece] + hidden_in[piece]
        collect.finish(piece)

    for piece in range(NSEQ):
        @pl.when(s < ns - 1)
        def _(piece=piece):
            edge_copy(piece).wait_recv()
            tail = pl.ds(EDGE - LEAD, LEAD)
            grad_tail[piece, tail, :] = grad_tail[piece, tail, :] + edge_in[piece]
            grads_o[piece, pl.ds(span - EDGE, EDGE), pl.ds(0, 3 * width)] = grad_tail[piece].astype(BF)

        @pl.when(s > 0)
        def _(piece=piece):
            edge_copy(piece).wait_send()

    first.finish(grad_down_o)
    chain.finish()
    ready(kept)


def backward(
    sizes, mix_rows, out_weight, head_rows, projected, logits, conv, lengths, bias, gain, saved,
    grad_down, down_part, hidden_in,
):
    ns, nm = sizes
    span, width = projected.shape[1], projected.shape[2] // 3
    heads = width // LANES
    chains = NSEQ * heads
    depth, cols = grad_down.shape
    shard = depth // ns
    local = hidden_in.shape
    rows = (NSEQ, span, depth)
    per_chain = (chains, span, LANES)
    return pl.pallas_call(
        functools.partial(backward_kernel, sizes),
        out_shape=(
            jax.ShapeDtypeStruct((NSEQ, span, 3 * width + LANES), BF),
            jax.ShapeDtypeStruct(local, F32),
            jax.ShapeDtypeStruct((shard, cols), F32),
            jax.ShapeDtypeStruct((12, width), F32),
            jax.ShapeDtypeStruct((1, LANES), F32),
            jax.ShapeDtypeStruct((1, LANES), F32),
            jax.ShapeDtypeStruct((depth, width), BF),
        ),
        in_specs=[ANY, ANY] + [VMEM] * 4 + [SMEM, SMEM] + [VMEM] * 3 + [ANY] * 7 + [VMEM, ANY, ANY, VMEM],
        out_specs=(VMEM,) * 6 + (ANY,),
        scratch_shapes=[
            pltpu.VMEM(rows, BF), pltpu.VMEM((depth, width), BF),
            pltpu.VMEM((chains, span, span), F32),
        ]
        + [pltpu.VMEM(per_chain, F32)] * 4
        + [
            pltpu.VMEM((NSEQ, LEAD + span, 3 * width), F32),
            pltpu.VMEM((NSEQ, span, LANES), F32),
            pltpu.VMEM(per_chain, F32),
            pltpu.VMEM(per_chain, F32),
            pltpu.VMEM((NSEQ, LEAD + span + LEAD, 3 * width), F32),
            pltpu.VMEM((NSEQ, EDGE, 3 * width), F32),
            pltpu.VMEM((NSEQ, span, LANES), F32),
            pltpu.VMEM((chains, LANES, LANES), BF),
            pltpu.VMEM((ns, LANES, LANES), BF),
            pltpu.VMEM((chains, LANES, LANES), F32),
            pltpu.VMEM((NSEQ, LEAD, 3 * width), F32),
            pltpu.VMEM((NSEQ, LEAD, 3 * width), F32),
            pltpu.VMEM((depth, width), BF),
            pltpu.VMEM((depth, cols), BF),
            pltpu.VMEM(rows, BF),
            DMA((12,)), DMA((NSEQ,)), DMA((NSEQ,)),
        ]
        + LineScatter.scratch(nm, local[1], depth)
        + CubeScatter.scratch(ns, shard, cols)
        + Chains.scratch(ns, chains),
        compiler_params=comm_params(2, 63),
        name="recurrence_back",
    )(
        mix_rows, out_weight, head_rows, projected, logits, conv, lengths, bias, gain, *saved,
        grad_down, down_part, hidden_in,
    )


def last_kernel(
    sizes, rows_h, grads_h, proj_w_h, out_total_h, tokens, gain, grad_in,
    conv_part, head_gain, bias, norms, feed_gain,
    grad_tokens, grad_weight_o, grad_out_o,
    conv_o, head_gain_o, bias_o, norm_o, feed_gain_o, gain_o,
    rows, grads, proj_w, part, total, out_total, vector, over_seq, over_mp,
    keep, seq_send, seq_recv, mp_send, mp_recv, *rest,
):
    geo = Geo(sizes)
    ns, nm, s, m = geo.ns, geo.nm, geo.s, geo.m
    mates = [(s, (m + k) % nm) for k in range(1, nm)] + all_mates(geo)
    greet(mates)
    loads = [
        (out_total_h, out_total, keep.at[0]), (rows_h, rows, keep.at[1]), (grads_h, grads, keep.at[2]),
        (proj_w_h, proj_w, keep.at[3]),
    ]
    load(loads[2:] + loads[:2])
    depth = proj_w.shape[0]
    width = vector.shape[1]
    wide = depth // width
    row = conv_part.shape[0]
    vector[...] = jnp.zeros(vector.shape, F32)
    vector[0:row, :] = conv_part[...]
    vector[row : row + 1, 0:LANES] = head_gain[...]
    vector[row : row + 1, LANES : 2 * LANES] = bias[...]
    vector[row : row + 1, 2 * LANES : 3 * LANES] = norms[0:1, :]
    for at in range(wide):
        vector[row + 1 + at : row + 2 + at, :] = feed_gain[:, at * width : (at + 1) * width]
    await_all(mates)
    collect = LineScatter(geo, part, rest[0:3])
    scatter = CubeScatter(geo, total, rest[3:6])
    outs = CubeScatter(geo, out_total, rest[6:9])
    shares = []

    def spread(piece):
        if piece == 0:
            ready(loads[2:])
        value = dot(grads[piece], proj_w[...], NT)
        part[piece] = value.astype(BF)
        collect.begin(piece)
        if piece == 0:
            ready(loads[1:2])
        shares.append(jnp.sum(value * rows[piece].astype(F32), 0, keepdims=True))

    tile = 512

    def weight_grad(left, right, out):
        def step(at, carry):
            window = pl.ds(pl.multiple_of(at * tile, tile), tile)
            value = dot(left[0, :, window], right[0], TN) + dot(left[1, :, window], right[1], TN)
            out[window, :] = value.astype(BF)
            return carry

        lax.fori_loop(0, depth // tile, step, 0)

    ready(loads[:1])
    outs.begin()
    spread(0)
    outs.advance(8)
    weight_grad(rows, grads, total)
    scatter.begin()
    spread(1)
    outs.advance(2)
    share = (shares[0] + shares[1]) / gain[...]
    for at in range(wide):
        vector[row + 1 + wide + at : row + 2 + wide + at, :] = share[:, at * width : (at + 1) * width]

    def seq_copy(k):
        return remote(
            vector, over_seq.at[k], seq_send.at[k], seq_recv.at[k], ((s + 1 + k) % ns, m)
        )

    def mp_copy(k):
        return remote(
            over_mp.at[0], over_mp.at[1 + k], mp_send.at[k], mp_recv.at[k], (s, (m + 1 + k) % nm)
        )

    def seq_start(k, carry):
        seq_copy(k).start()
        return carry

    lax.fori_loop(0, ns - 1, seq_start, 0)
    collect.advance(0, 1)
    scatter.advance(8)

    def seq_add(k, value):
        seq_copy(k).wait_recv()
        return value + over_seq[k]

    over_mp[0] = lax.fori_loop(0, ns - 1, seq_add, vector[...])
    for k in range(nm - 1):
        mp_copy(k).start()
    collect.advance(1, 1)
    collect.advance(0, 2)
    outs.advance(2)
    for k in range(nm - 1):
        mp_copy(k).wait_recv()
    scatter.advance(2)
    collect.advance(1, 2)
    for turn in range(3, nm):
        collect.advance(0, turn)
        scatter.advance(2)
        collect.advance(1, turn)
    for piece in range(NSEQ):
        collect.result(piece, grad_tokens)
        values = tokens[piece].astype(F32)
        scale = row_scale(values)
        grad_tokens[piece] = grad_in[piece] + norm_backward(
            grad_tokens[piece] * gain[...], values * scale, scale
        )
        collect.finish(piece)
    for k in range(nm):
        origin = (m + nm - k) % nm
        cols = pl.ds(pl.multiple_of(origin * width, width), width)
        for group in range(3):
            for tap in range(4):
                at = group * 4 + tap
                conv_o[group, tap : tap + 1, cols] = over_mp[k, at : at + 1, :]
    summed = over_mp[0]
    for k in range(1, nm):
        summed = summed + over_mp[k]
    head_gain_o[...] = summed[row : row + 1, 0:LANES]
    bias_o[...] = summed[row : row + 1, LANES : 2 * LANES]
    norm_o[...] = summed[row : row + 1, 2 * LANES : 3 * LANES] / (NSEQ * HEADS * ns)
    for at in range(wide):
        cols = slice(at * width, (at + 1) * width)
        feed_gain_o[:, cols] = summed[row + 1 + at : row + 2 + at, :]
        gain_o[:, cols] = summed[row + 1 + wide + at : row + 2 + wide + at, :]
    outs.finish(grad_out_o)
    scatter.finish(grad_weight_o)

    def seq_done(k, carry):
        seq_copy(k).wait_send()
        return carry

    lax.fori_loop(0, ns - 1, seq_done, 0)
    for k in range(nm - 1):
        mp_copy(k).wait_send()


def last(sizes, rows, grads, proj_w, out_total, tokens, gain, grad_in, small):
    ns, nm = sizes
    depth, cols = proj_w.shape
    span = tokens.shape[1]
    shard = depth // ns
    width = (cols - LANES) // 3
    vector = (-(-(13 + 2 * (depth // width)) // 8) * 8, width)
    shape = jax.ShapeDtypeStruct
    line = shape((1, LANES), F32)
    return pl.pallas_call(
        functools.partial(last_kernel, sizes),
        out_shape=(
            shape(grad_in.shape, F32), shape((shard, cols), F32), shape((shard, width), F32),
            shape((3, 4, depth), F32), line, line, line, shape((1, depth), F32), shape((1, depth), F32),
        ),
        in_specs=[ANY] * 4 + [VMEM] * 8,
        out_specs=(VMEM,) * 9,
        scratch_shapes=[
            pltpu.VMEM(rows.shape, BF),
            pltpu.VMEM(grads.shape, BF),
            pltpu.VMEM((depth, cols), BF),
            pltpu.VMEM(rows.shape, BF),
            pltpu.VMEM((depth, cols), BF),
            pltpu.VMEM((depth, width), BF),
            pltpu.VMEM(vector, F32),
            pltpu.VMEM((ns - 1,) + vector, F32),
            pltpu.VMEM((nm,) + vector, F32),
            DMA((4,)), DMA((ns - 1,)), DMA((ns - 1,)), DMA((nm - 1,)), DMA((nm - 1,)),
        ]
        + LineScatter.scratch(nm, span, depth)
        + CubeScatter.scratch(ns, shard, cols)
        + CubeScatter.scratch(ns, shard, width),
        compiler_params=comm_params(3),
        name="last",
    )(rows, grads, proj_w, out_total, tokens, gain, grad_in, *small)


def deliver_kernel(
    block, grad_tokens, grad_proj, grad_gate, grad_up, grad_down, grad_out, conv, *rest
):
    lines, rest = rest[:5], rest[5:]
    (
        block_o, grad_tokens_o, query_o, key_o, value_o, grad_gate_o, grad_up_o, beta_o, grad_down_o,
        grad_out_o, conv_o,
    ) = rest[:11]
    line_os, rest = rest[11:16], rest[16:]
    block_v, tokens_v, proj_v, gate_v, up_v, down_v, out_v, down_t, out_t, conv_v = rest[:10]
    line_vs, sems = rest[10:15], rest[15]
    width = query_o.shape[1]
    coming = [
        (src, held, sems.at[k])
        for k, (src, held) in enumerate(
            (
                (grad_gate, gate_v), (grad_up, up_v), (block, block_v), (grad_tokens, tokens_v),
                (grad_proj, proj_v), (grad_out, out_v), (grad_down, down_v), (conv, conv_v),
            )
            + tuple(zip(lines, line_vs))
        )
    ]
    load(coming)
    going = []

    def send(held, dst):
        going.append((held, dst, sems.at[len(coming) + len(going)]))
        load(going[-1:])

    ready(coming[0:4])
    send(gate_v, grad_gate_o)
    send(up_v, grad_up_o)
    send(block_v, block_o)
    send(tokens_v, grad_tokens_o)
    ready(coming[4:5])
    for k, dst in enumerate((query_o, key_o, value_o)):
        send(proj_v.at[:, pl.ds(k * width, width)], dst)
    ready(coming[5:])
    out_t[...] = out_v[...].T
    send(out_t, grad_out_o)
    down_t[...] = down_v[...].T
    send(down_t, grad_down_o)
    beta_o[...] = proj_v[:, 3 * width :].T[: beta_o.shape[0], :]
    conv_o[...] = conv_v[...]
    for line, dst in zip(line_vs, line_os):
        dst[...] = line[:, : dst.shape[1]]
    ready(going)


def deliver(block, grad_tokens, grad_proj, grad_gate, grad_up, grad_down, grad_out, conv, lines, counts):
    shard, cols = grad_gate.shape
    width = (grad_proj.shape[1] - LANES) // 3
    heads = width // LANES
    shape = jax.ShapeDtypeStruct
    square = shape((shard, width), F32)
    wide = shape((shard, cols), F32)
    there = pl.BlockSpec(memory_space=pltpu.HBM)
    held = [
        block.shape, grad_tokens.shape, grad_proj.shape, (shard, cols), (shard, cols), (shard, cols),
        (shard, width), (cols, shard), (width, shard), conv.shape,
    ] + [line.shape for line in lines]
    return pl.pallas_call(
        deliver_kernel,
        out_shape=(
            shape(block.shape, F32), shape(grad_tokens.shape, F32), square, square, square, wide, wide,
            shape((heads, shard), F32), shape((cols, shard), F32), shape((width, shard), F32),
            shape(conv.shape, F32),
        )
        + tuple(shape((1, count), F32) for count in counts),
        in_specs=[there] * 13,
        out_specs=(there,) * 7 + (VMEM, there, there) + (VMEM,) * 6,
        scratch_shapes=[pltpu.VMEM(dims, F32) for dims in held] + [DMA((24,))],
        compiler_params=pltpu.CompilerParams(vmem_limit_bytes=63 * 2**20),
        name="deliver",
    )(block, grad_tokens, grad_proj, grad_gate, grad_up, grad_down, grad_out, conv, *lines)


def on_device(
    sizes,
    tokens,
    lengths,
    mixer_gain,
    query_weight,
    key_weight,
    value_weight,
    beta_weight,
    beta_bias,
    conv_weight,
    head_gain,
    out_weight,
    feed_gain,
    gate_weight,
    up_weight,
    down_weight,
    cotangent,
):
    ns, nm = sizes
    depth = tokens.shape[2]
    width = query_weight.shape[1]
    heads = width // LANES
    mixer_gain_row = mixer_gain.reshape(1, depth)
    feed_gain_row = feed_gain.reshape(1, depth)
    head_gain_row = head_gain.reshape(1, LANES)
    (
        rows, proj_w, out_w, gate_w, up_w, down_w, grad_rows, feed_rows,
        hidden_in, head_rows, projected, logits, edge, links, norms, entry, *saved,
    ) = mixer(
        sizes, tokens, cotangent, query_weight, key_weight, value_weight, beta_weight.T, out_weight,
        gate_weight, up_weight, down_weight, conv_weight, lengths, beta_bias, mixer_gain_row,
        head_gain_row, feed_gain_row,
    )
    grad_in, mix_rows, grad_gate, grad_up, grad_down_part, down_part, feed_gain_part = feed(
        sizes, feed_rows, grad_rows, gate_w, up_w, down_w, hidden_in, feed_gain_row, cotangent
    )
    grads, block_output, grad_down, conv_part, gain_part, bias_part, grad_out_part = backward(
        sizes, mix_rows, out_w, head_rows, projected, logits, conv_weight, lengths, beta_bias,
        head_gain_row, (edge, links, *saved, entry), grad_down_part, down_part, hidden_in,
    )
    (
        grad_tokens, grad_proj_w, grad_out, conv_grad, gain_grad, bias_grad, norm, feed_gain_grad,
        mixer_grad,
    ) = last(
        sizes, rows, grads, proj_w, grad_out_part, tokens, mixer_gain_row, grad_in,
        (conv_part, gain_part, bias_part, norms, feed_gain_part),
    )
    (
        block_output, grad_tokens, grad_query, grad_key, grad_value, grad_gate, grad_up, grad_beta,
        grad_down, grad_out, conv_grad, mixer_grad, feed_gain_grad, gain_grad, bias_grad, norm,
    ) = deliver(
        block_output, grad_tokens, grad_proj_w, grad_gate, grad_up, grad_down, grad_out, conv_grad,
        (mixer_grad, feed_gain_grad, gain_grad, bias_grad, norm), (depth, depth, LANES, nm * heads, 1),
    )
    return (
        block_output,
        grad_tokens,
        mixer_grad.reshape(depth),
        grad_query,
        grad_key,
        grad_value,
        grad_beta.T,
        bias_grad.reshape(nm * heads),
        conv_grad,
        gain_grad.reshape(LANES),
        grad_out,
        feed_gain_grad.reshape(depth),
        grad_gate,
        grad_up,
        grad_down,
        norm[0, 0],
    )


def solution(mesh):
    sizes = (mesh.shape["seq"], mesh.shape["mp"])
    by_rows = P("seq", "mp")
    by_cols = P("mp", "seq")
    placed = P(None, ("seq", "mp"), None)
    return jax.shard_map(
        functools.partial(on_device, sizes),
        mesh=mesh,
        in_specs=(
            placed, P(), P(), by_rows, by_rows, by_rows, by_rows, P(), P(), P(), by_cols, P(),
            by_rows, by_rows, by_cols, placed,
        ),
        out_specs=(
            placed, placed, P(), by_rows, by_rows, by_rows, by_rows, P(), P(), P(), by_cols, P(),
            by_rows, by_rows, by_cols, P(),
        ),
        check_vma=False,
    )
```

```python
import functools

import jax
import jax.numpy as jnp
from jax import lax
from jax.experimental import pallas as pl
from jax.experimental.pallas import tpu as pltpu
from jax.sharding import PartitionSpec as P

HEADS = 16
HEAD_DIM = 128
NSEQ = 2
EPSILON = 1e-05
KEY_EPSILON = 1e-06
LANES = 128
LEAD = 8
EDGE = 16
BF = jnp.bfloat16
F32 = jnp.float32
MESH = pl.DeviceIdType.MESH
VMEM = pl.BlockSpec(memory_space=pltpu.VMEM)
SMEM = pl.BlockSpec(memory_space=pltpu.SMEM)
ANY = pl.BlockSpec(memory_space=pl.ANY)
NN = (((1,), (0,)), ((), ()))
NT = (((1,), (1,)), ((), ()))
TN = (((0,), (0,)), ((), ()))
DMA = pltpu.SemaphoreType.DMA


def dot(left, right, dims=NN):
    return lax.dot_general(left, right, dims, preferred_element_type=F32)


def halves(values):
    high = values.astype(BF)
    return high, (values - high.astype(F32)).astype(BF)


def fine(left, right, dims=NN):
    return (
        dot(left[0], right[0], dims)
        + dot(left[0], right[1], dims)
        + dot(left[1], right[0], dims)
    )


def row_scale(values):
    return lax.rsqrt(jnp.mean(values * values, -1, keepdims=True) + EPSILON)


def norm_backward(grad_normed, unit_rows, scale):
    return scale * (grad_normed - unit_rows * jnp.mean(grad_normed * unit_rows, -1, keepdims=True))


def sigmoid(values):
    return 1.0 / (1.0 + jnp.exp(-values))


def iota(shape, dim):
    return lax.broadcasted_iota(jnp.int32, shape, dim)


def lower_mask(size, strict):
    rows, cols = iota((size, size), 0), iota((size, size), 1)
    return rows > cols if strict else rows >= cols


def unit_lower_inverses(lowers):
    size = LANES
    rows, cols = iota((size, size), 0), iota((size, size), 1)
    eye = (rows == cols).astype(F32)
    blocks = [low[at : at + size, at : at + size] for low in lowers for at in (0, size)]
    base = 16
    same = (rows // base) == (cols // base)
    minus = [jnp.where(same, -block, 0.0) for block in blocks]
    inverses = [eye + one for one in minus]
    pairs = [halves(one) for one in minus]
    powers = [fine(pair, pair) for pair in pairs]
    covered = 2
    while covered * 2 < base:
        lefts = [halves(jnp.concatenate((i, p), 0)) for i, p in zip(inverses, powers)]
        both = [fine(left, (left[0][size:], left[1][size:])) for left in lefts]
        inverses = [i + b[:size] for i, b in zip(inverses, both)]
        powers = [b[size:] for b in both]
        covered *= 2
    inverses = [i + fine(halves(i), halves(p)) for i, p in zip(inverses, powers)]
    while base < size:
        joined = (rows // (2 * base)) == (cols // (2 * base))
        cross = jnp.logical_and(joined, jnp.logical_not(same))
        pairs = [halves(i) for i in inverses]
        inner = [fine(halves(jnp.where(cross, b, 0.0)), i) for b, i in zip(blocks, pairs)]
        inverses = [i - fine(p, halves(x)) for i, p, x in zip(inverses, pairs, inner)]
        same = joined
        base *= 2
    pairs = [halves(i) for i in inverses]
    corners = [fine(halves(low[size:, :size]), pairs[2 * k]) for k, low in enumerate(lowers)]
    corners = [-fine(pairs[2 * k + 1], halves(c)) for k, c in enumerate(corners)]
    zero = jnp.zeros((size, size), F32)
    return [
        jnp.concatenate(
            (
                jnp.concatenate((inverses[2 * k], zero), 1),
                jnp.concatenate((corner, inverses[2 * k + 1]), 1),
            ),
            0,
        )
        for k, corner in enumerate(corners)
    ]


def flip(index, mask):
    out = index
    bit = 1
    while bit <= mask:
        if mask & bit:
            out = out + bit * (1 - 2 * ((index // bit) % 2))
        bit *= 2
    return out


def bits_of(count):
    out = []
    bit = 1
    while bit < count:
        out.insert(0, bit)
        bit *= 2
    return out


def two_orders(bits):
    if len(bits) < 2:
        return (bits, bits)
    return (list(bits), [bits[1], bits[0]] + list(bits[2:]))


def spans(bits):
    masks = [0]
    for bit in bits:
        masks = masks + [mask ^ bit for mask in masks]
    return masks


def remote(src, dst, send, recv, target):
    return pltpu.make_async_remote_copy(
        src_ref=src,
        dst_ref=dst,
        send_sem=send,
        recv_sem=recv,
        device_id=target,
        device_id_type=MESH,
    )


def greet(targets):
    barrier = pltpu.get_barrier_semaphore()
    for target in targets:
        pl.semaphore_signal(barrier, inc=1, device_id=target, device_id_type=MESH)


def await_all(targets):
    pl.semaphore_wait(pltpu.get_barrier_semaphore(), len(targets))


def meet(targets):
    greet(targets)
    await_all(targets)


def line_mates(geo):
    s, m = geo.s, geo.m
    return [(s, (m + 1) % geo.nm), (s, (m + geo.nm - 1) % geo.nm)]


def cube_mates(geo):
    return [(flip(geo.s, bit), geo.m) for bit in bits_of(geo.ns)]


def all_mates(geo):
    return [((geo.s + k) % geo.ns, geo.m) for k in range(1, geo.ns)]


class Geo:
    def __init__(self, sizes):
        self.ns, self.nm = sizes
        self.s = lax.axis_index("seq")
        self.m = lax.axis_index("mp")


class CubeGather:
    @staticmethod
    def sems(ns):
        return [DMA((2, ns - 1)), DMA((2, ns - 1)), DMA(())]

    def __init__(self, geo, shard, full, sems):
        self.geo, self.shard, self.full = geo, shard, full
        self.send, self.recv, self.local = sems
        self.rows = shard.shape[0]
        self.orders = two_orders(bits_of(geo.ns))
        self.ids = {}
        for order, bits in enumerate(self.orders):
            count = 0
            for step in range(len(bits)):
                for mask in spans(bits[:step]):
                    self.ids[order, step, mask] = count
                    count += 1
        self.todo = sorted(self.ids, key=lambda key: (key[1], bin(key[2]).count("1"), key[2], key[0]))
        self.started = []

    def block(self, order, mask):
        half = self.rows // 2
        start = flip(self.geo.s, mask) * self.rows + order * half
        return self.full.at[pl.ds(pl.multiple_of(start, half), half)]

    def copy(self, order, step, mask, incoming=False):
        bit = self.orders[order][step]
        half = self.rows // 2
        place = self.block(order, mask ^ bit if incoming else mask)
        src = self.shard.at[pl.ds(order * half, half)] if mask == 0 and not incoming else place
        at = self.ids[order, step, mask]
        return remote(
            src, place, self.send.at[order, at], self.recv.at[order, at],
            (flip(self.geo.s, bit), self.geo.m),
        )

    def own(self):
        start = pl.multiple_of(self.geo.s * self.rows, self.rows)
        return pltpu.make_async_copy(self.shard, self.full.at[pl.ds(start, self.rows)], self.local)

    def begin(self, steps=None):
        depth = len(self.orders[0])
        for step in range(depth) if steps is None else steps:
            for order in range(2):
                self.copy(order, step, 0).start()
            if step == depth - 1:
                self.own().start()

    def advance(self, count=None):
        count = len(self.todo) if count is None else count
        for order, step, mask in self.todo[:count]:
            self.copy(order, step, mask, incoming=True).wait_recv()
            after = mask ^ self.orders[order][step]
            for later in range(step + 1, len(self.orders[order])):
                self.copy(order, later, after).start()
        self.todo = self.todo[count:]

    def settle(self):
        self.advance()
        self.own().wait()

    def finish(self):
        for order, step, mask in self.ids:
            self.copy(order, step, mask).wait_send()


class CubeScatter:
    @staticmethod
    def scratch(ns, rows, cols):
        return [pltpu.VMEM((2, ns - 1, rows // 2, cols), BF), DMA((2, ns - 1)), DMA((2, ns - 1))]

    def __init__(self, geo, total, scratch):
        self.geo, self.total = geo, total
        self.slots, self.send, self.recv = scratch
        self.half = self.slots.shape[2]
        self.orders = [list(reversed(bits)) for bits in two_orders(bits_of(geo.ns))]
        self.ids = {}
        for order, bits in enumerate(self.orders):
            count = 0
            for step in range(len(bits)):
                for mask in reversed(spans(bits[step + 1 :])):
                    self.ids[order, step, mask] = count
                    count += 1
        depth = len(self.orders[0])

        def urgency(key):
            order, step, mask = key
            ahead = [k for k in range(depth) if mask & self.orders[order][k]]
            return (step, ahead[0] if ahead else depth, -mask, order)

        self.todo = sorted(self.ids, key=urgency)

    def rows(self, order, mask):
        start = flip(self.geo.s, mask) * (2 * self.half) + order * self.half
        return pl.ds(pl.multiple_of(start, self.half), self.half)

    def copy(self, order, step, mask):
        bit = self.orders[order][step]
        at = self.ids[order, step, mask]
        return remote(
            self.total.at[self.rows(order, mask ^ bit)], self.slots.at[order, at],
            self.send.at[order, at], self.recv.at[order, at],
            (flip(self.geo.s, bit), self.geo.m),
        )

    def begin(self):
        for order, step, mask in self.todo:
            if step == 0:
                self.copy(order, 0, mask).start()

    def advance(self, count=None):
        count = len(self.todo) if count is None else count
        for order, step, mask in self.todo[:count]:
            self.copy(order, step, mask).wait_recv()
            if mask == 0 and step == len(self.orders[order]) - 1:
                continue
            rows = self.rows(order, mask)
            slot = self.slots[order, self.ids[order, step, mask]]
            self.total[rows, :] = (self.total[rows, :].astype(F32) + slot.astype(F32)).astype(BF)
            bits = self.orders[order]
            if step + 1 < len(bits) and mask & bits[step + 1]:
                self.copy(order, step + 1, mask ^ bits[step + 1]).start()
        self.todo = self.todo[count:]

    def finish(self, out):
        self.advance()
        for order in range(2):
            last = self.ids[order, len(self.orders[order]) - 1, 0]
            out[pl.ds(order * self.half, self.half), :] = self.total[self.rows(order, 0), :].astype(
                F32
            ) + self.slots[order, last].astype(F32)
        for order, step, mask in self.ids:
            self.copy(order, step, mask).wait_send()


class LineGather:
    @staticmethod
    def sems(nm):
        return [DMA((2, NSEQ, nm - 1)), DMA((2, NSEQ, nm - 1))]

    def __init__(self, geo, full, sems):
        self.geo, self.full = geo, full
        self.send, self.recv = sems
        self.span = full.shape[1] // geo.nm

    def place(self, piece, origin):
        return self.full.at[piece, pl.ds(pl.multiple_of(origin * self.span, self.span), self.span)]

    def copy(self, way, piece, hop, incoming=False):
        m = self.geo.m
        sign = 1 if way == 0 else -1
        origin = m - sign * (hop + (1 if incoming else 0))
        place = self.place(piece, origin)
        return remote(
            place, place, self.send.at[way, piece, hop], self.recv.at[way, piece, hop],
            (self.geo.s, m + sign),
        )

    def sends(self, way, hop):
        m, nm = self.geo.m, self.geo.nm
        if way == 0:
            return jnp.logical_and(m >= hop, m < nm - 1)
        return jnp.logical_and(m <= nm - 1 - hop, m > 0)

    def receives(self, way, hop):
        m, nm = self.geo.m, self.geo.nm
        return m >= hop + 1 if way == 0 else m <= nm - 2 - hop

    def begin(self, piece):
        for way in range(2):
            @pl.when(self.sends(way, 0))
            def _(way=way):
                self.copy(way, piece, 0).start()

    def advance(self, piece, hop):
        for way in range(2):
            @pl.when(self.receives(way, hop))
            def _(way=way):
                self.copy(way, piece, hop, incoming=True).wait_recv()

            if hop + 1 < self.geo.nm - 1:
                @pl.when(self.sends(way, hop + 1))
                def _(way=way):
                    self.copy(way, piece, hop + 1).start()

    def finish(self, piece):
        for way in range(2):
            for hop in range(self.geo.nm - 1):
                @pl.when(self.sends(way, hop))
                def _(way=way, hop=hop):
                    self.copy(way, piece, hop).wait_send()


class LineScatter:
    @staticmethod
    def scratch(nm, span, cols):
        return [
            pltpu.VMEM((2, NSEQ, nm, span, cols), BF),
            DMA((2, NSEQ, nm)),
            DMA((2, NSEQ, nm)),
        ]

    def __init__(self, geo, part, scratch):
        self.geo, self.part = geo, part
        self.slots, self.send, self.recv = scratch
        self.span = self.slots.shape[3]

    def place(self, way):
        return self.geo.m if way == 0 else self.geo.nm - 1 - self.geo.m

    def own(self, way, piece, block):
        at = self.geo.nm - 1 - block if way == 0 else block
        start = at * self.span
        if not isinstance(start, int):
            start = pl.multiple_of(start, self.span)
        return self.part.at[piece, pl.ds(start, self.span)]

    def copy(self, way, piece, block, first=False):
        slot = self.slots.at[way, piece, block]
        src = self.own(way, piece, block) if first else slot
        step = 1 if way == 0 else -1
        return remote(
            src, slot, self.send.at[way, piece, block], self.recv.at[way, piece, block],
            (self.geo.s, self.geo.m + step),
        )

    def begin(self, piece):
        for way in range(2):
            @pl.when(self.place(way) == 0)
            def _(way=way):
                self.copy(way, piece, 0, True).start()

    def advance(self, piece, turn):
        forward = turn <= self.geo.nm - 2
        for way in range(2):
            at = self.place(way)
            if forward:
                @pl.when(at == 0)
                def _(way=way):
                    self.copy(way, piece, turn - 1, True).wait_send()
                    self.copy(way, piece, turn, True).start()

            @pl.when(jnp.logical_and(at >= 1, at <= turn))
            def _(way=way, block=turn - at):
                self.copy(way, piece, block).wait_recv()
                if forward:
                    slot = self.slots.at[way, piece, block]
                    own = self.own(way, piece, block)
                    slot[...] = (slot[...].astype(F32) + own[...].astype(F32)).astype(BF)
                    self.copy(way, piece, block).start()

    def result(self, piece, out):
        m, nm = self.geo.m, self.geo.nm
        own = self.part[piece, pl.ds(pl.multiple_of(m * self.span, self.span), self.span), :]
        out[piece] = own.astype(F32)

        @pl.when(m >= 1)
        def _():
            out[piece] = out[piece] + self.slots[0, piece, nm - 1 - m].astype(F32)

        @pl.when(m <= nm - 2)
        def _():
            out[piece] = out[piece] + self.slots[1, piece, m].astype(F32)

    def finish(self, piece):
        nm = self.geo.nm
        for way in range(2):
            at = self.place(way)
            for block in range(nm - 1):
                first = 0 if block == nm - 2 else 1

                @pl.when(jnp.logical_and(at >= first, at <= nm - 2 - block))
                def _(way=way, block=block):
                    self.copy(way, piece, block).wait_send()


def comm_params(collective, limit=60):
    return pltpu.CompilerParams(
        collective_id=collective, has_side_effects=True, vmem_limit_bytes=limit * 2**20
    )


def load(pairs):
    for src, dst, sem in pairs:
        pltpu.make_async_copy(src, dst, sem).start()


def ready(pairs):
    for src, dst, sem in pairs:
        pltpu.make_async_copy(src, dst, sem).wait()


GROUP = 4


def conv_row(conv, group, tap, column):
    return conv[group, pl.ds(tap, 1), pl.ds(pl.multiple_of(column, LANES), LANES)]


def before_silu(extended, conv, piece, group, head, width, rank):
    span = extended.shape[1] - LEAD
    cols = pl.ds(pl.multiple_of(group * width + head * LANES, LANES), LANES)
    total = None
    for tap in range(4):
        term = conv_row(conv, group, tap, rank * width + head * LANES) * extended[
            piece, pl.ds(LEAD - tap, span), cols
        ]
        total = term if total is None else total + term
    return total


def strengths_of(geo, logits, lengths, bias, local_heads, piece):
    span = logits.shape[1]
    lane = iota((span, LANES), 1)
    offset = jnp.zeros((span, LANES), F32)
    for head in range(local_heads):
        offset = jnp.where(lane == head, bias[geo.m * local_heads + head], offset)
    position = geo.s * span + iota((span, LANES), 0)
    live = jnp.where(position < lengths[piece], 1.0, 0.0)
    return sigmoid(logits[piece] + offset), live


def column_of(values, head):
    return jnp.sum(jnp.where(iota(values.shape, 1) == head, values, 0.0), -1, keepdims=True)


def fill_extended(extended, projected, edge, piece):
    extended[piece, LEAD:, :] = projected[piece].astype(F32)
    extended[piece, :LEAD, :] = edge[piece, EDGE - LEAD :, :].astype(F32)


class Chains:
    @staticmethod
    def scratch(ns, chains):
        return [
            pltpu.VMEM((ns, LANES, LANES), F32),
            DMA((chains,)), DMA((ns,)), DMA((ns,)), DMA((chains,)),
        ]

    def __init__(self, geo, chains, pair, links, entries, scratch):
        self.geo, self.chains = geo, chains
        self.pair, self.links, self.entries = pair, links, entries
        self.states, self.pair_send, self.pair_recv, self.back_send, self.back_recv = scratch
        self.stride = geo.ns // chains
        self.mine = geo.s // self.stride
        self.holds = geo.s == self.mine * self.stride

    def link_copy(self, chain):
        s, m = self.geo.s, self.geo.m
        return remote(
            self.pair.at[chain], self.links.at[s], self.pair_send.at[chain], self.pair_recv.at[s],
            (chain * self.stride, m),
        )

    def give(self, chain, link):
        owner = chain * self.stride

        @pl.when(owner == self.geo.s)
        def _():
            self.links[self.geo.s] = link

        @pl.when(owner != self.geo.s)
        def _():
            self.link_copy(chain).start()

    def state_copy(self, other):
        return remote(
            self.states.at[other], self.entries.at[self.mine], self.back_send.at[other],
            self.back_recv.at[self.mine], (other, self.geo.m),
        )

    def run(self, first, count, advance, start, reverse, last):
        ns, s, m = self.geo.ns, self.geo.s, self.geo.m

        @pl.when(jnp.logical_and(self.holds, jnp.logical_and(self.mine >= first, self.mine < first + count)))
        def _():
            def step(lap, carry):
                at = ns - 1 - lap if reverse else lap
                state = carry[0]
                self.states[at] = state

                @pl.when(at == s)
                def _():
                    self.entries[self.mine] = state

                @pl.when(at != s)
                def _():
                    self.state_copy(at).start()
                    remote(
                        self.pair.at[0], self.links.at[at], self.pair_send.at[0],
                        self.pair_recv.at[at], (s, m),
                    ).wait_recv()

                return advance(carry, at)

            last(lax.fori_loop(0, ns, step, start))

    def receive(self, chain):
        @pl.when(chain * self.stride != self.geo.s)
        def _():
            remote(
                self.states.at[0], self.entries.at[chain], self.back_send.at[0],
                self.back_recv.at[chain], (self.geo.s, self.geo.m),
            ).wait_recv()

    def finish(self):
        def sent(chain, carry):
            @pl.when(chain * self.stride != self.geo.s)
            def _():
                self.link_copy(chain).wait_send()

            return carry

        lax.fori_loop(0, self.chains, sent, 0)

        @pl.when(self.holds)
        def _():
            def done(other, carry):
                @pl.when(other != self.geo.s)
                def _():
                    self.state_copy(other).wait_send()

                return carry

            lax.fori_loop(0, self.geo.ns, done, 0)


def mixer_kernel(
    sizes, tokens, cotangent, query_w, key_w, value_w, beta_w, out_in, gate_hbm, up_hbm, down_in,
    conv, lengths, bias, mixer_gain, head_gain, feed_gain,
    rows_o, proj_w_o, out_w_o, gate_w_o, up_w_o, down_w_o, grad_rows_o, feed_rows_o,
    hidden_in, head_rows, projected, logits, edge, links, norm_o, entry_o,
    solve_h, wkeys_h, fresh_h, error_h, outputs_h, queries_h, keys_h,
    solve_o, wkeys_o, fresh_o, error_o, outputs_o, queries_o, keys_o,
    proj_shard, out_shard, gate_shard, up_shard, down_shard,
    rows, weight, out_w, grad_rows, feed_rows, part, extended, betas, wvalues, pair,
    keep, edge_send, edge_recv, *rest,
):
    geo = Geo(sizes)
    ns, nm, s, m = geo.ns, geo.nm, geo.s, geo.m
    mates = line_mates(geo) + all_mates(geo)
    greet(mates)
    shards = [(gate_hbm, gate_shard, keep.at[0]), (up_hbm, up_shard, keep.at[1])]
    load(shards)
    width = query_w.shape[1]
    heads = width // LANES
    chains = NSEQ * heads
    span = projected.shape[1]
    proj_shard[:, 0:width] = query_w[...]
    proj_shard[:, width : 2 * width] = key_w[...]
    proj_shard[:, 2 * width : 3 * width] = value_w[...]
    proj_shard[:, 3 * width :] = jnp.zeros((proj_shard.shape[0], LANES), BF)
    proj_shard[:, 3 * width : 3 * width + heads] = beta_w[...].astype(F32).T.astype(BF)
    out_shard[...] = out_in[...].T
    await_all(mates)

    weights = CubeGather(geo, proj_shard, weight, rest[0:3])
    outs = CubeGather(geo, out_shard, out_w, rest[3:6])
    gates = CubeGather(geo, gate_shard, gate_w_o, rest[6:9])
    ups = CubeGather(geo, up_shard, up_w_o, rest[9:12])
    downs = CubeGather(geo, down_shard, down_w_o, rest[12:15])
    spread = LineGather(geo, rows, rest[15:17])
    spread_grad = LineGather(geo, grad_rows, rest[17:19])
    spread_feed = LineGather(geo, feed_rows, rest[19:21])
    collect = LineScatter(geo, part, rest[21:24])
    chain = Chains(geo, chains, pair, links, entry_o, rest[24:29])

    weights.begin()
    own_rows = tokens.shape[1]
    mine = pl.ds(pl.multiple_of(m * own_rows, own_rows), own_rows)
    for piece in range(NSEQ):
        values = tokens[piece].astype(F32)
        rows[piece, mine, :] = (values * row_scale(values) * mixer_gain[...]).astype(BF)
        grad_rows[piece, mine, :] = cotangent[piece]
        if piece == 0:
            spread.begin(0)
    down_shard[...] = down_in[...].T
    spread.advance(0, 0)
    spread.begin(1)
    weights.advance(2)
    outs.begin()
    for hop in range(1, nm - 1):
        spread.advance(0, hop)
        weights.advance(2)
        spread.advance(1, hop - 1)
    outs.advance(2)
    weights.settle()
    ready(shards)
    kept = [(weight, proj_w_o, keep.at[2])]
    load(kept)
    strict = lower_mask(span, True)
    whole = lower_mask(span, False)
    norm_o[...] = jnp.zeros(norm_o.shape, F32)

    def edge_copy(piece):
        return remote(
            projected.at[piece, pl.ds(span - EDGE, EDGE)], edge.at[piece],
            edge_send.at[piece], edge_recv.at[piece], (s + 1, m),
        )

    def run_chains(piece):
        def advance(carry, at):
            state, total = carry
            link = links[at]
            high, low = halves(state)
            move = link[:, :LANES]
            state = state - (dot(move, high) + dot(move, low)) + link[:, LANES:].astype(F32)
            return state, total + jnp.sqrt(jnp.sum(state * state, (0, 1), keepdims=True))

        def last(carry):
            norm_o[...] = norm_o[...] + carry[1]

        start = (jnp.zeros((LANES, LANES), F32), jnp.zeros((1, 1), F32))
        chain.run(piece * heads, heads, advance, start, False, last)

    groups = heads // GROUP

    def solve(piece, carry):
        @pl.when(piece == 1)
        def _():
            for hop in range(nm - 2, nm - 1):
                spread.advance(1, hop)

        result = dot(rows[piece], weight[...])
        projected[piece] = result[:, : 3 * width].astype(BF)
        logits[piece] = result[:, 3 * width :]

        @pl.when(s < ns - 1)
        def _():
            edge_copy(piece).start()

        strength, live = strengths_of(geo, logits, lengths, bias, heads, piece)
        betas[piece] = strength * live

        @pl.when(piece == 0)
        def _():
            gates.begin((0,))
            for at in range(NSEQ):
                spread_grad.begin(at)

        @pl.when(s > 0)
        def _():
            edge_copy(piece).wait_recv()

        @pl.when(s == 0)
        def _():
            edge[piece] = jnp.zeros(edge.shape[1:], BF)

        fill_extended(extended, projected, edge, piece)
        for first in range(0, heads, GROUP):
            which = [first + k for k in range(GROUP)]
            mixed = [
                [before_silu(extended, conv, piece, g, head, width, m) for g in range(3)]
                for head in which
            ]
            mixed = [[z * sigmoid(z) for z in three] for three in mixed]
            queries = [three[0] for three in mixed]
            keys = [
                key * lax.rsqrt(jnp.sum(key * key, -1, keepdims=True) + KEY_EPSILON)
                for _, key, _ in mixed
            ]
            values = [three[2] for three in mixed]
            strengths = [column_of(betas[piece], head) for head in which]
            key_pairs = [halves(key) for key in keys]
            grams = [jnp.where(strict, fine(key, key, NT), 0.0) for key in key_pairs]
            inverses = unit_lower_inverses([gram * beta for gram, beta in zip(grams, strengths)])
            both = [
                halves(jnp.concatenate((key * beta, value * beta), 1))
                for key, value, beta in zip(keys, values, strengths)
            ]
            both = [fine(halves(inverse), right) for inverse, right in zip(inverses, both)]
            found = [fine(key, halves(two), TN).astype(BF) for key, two in zip(key_pairs, both)]
            done = list(zip(queries, keys, values, inverses, both, found))
            for k, (query, key, value, inverse, both, link) in enumerate(done):
                at = piece * heads + first + k
                pair[at] = link
                solve_o[at] = inverse
                wkeys_o[at] = both[:, :LANES]
                wvalues[at] = both[:, LANES:]
                queries_o[at] = query
                keys_o[at] = key
                error_o[at] = value
            for k, found in enumerate(done):
                chain.give(piece * heads + first + k, found[-1])
        return carry

    lax.fori_loop(0, NSEQ, solve, 0)
    saved = [
        (solve_o, solve_h, keep.at[7]), (wkeys_o, wkeys_h, keep.at[8]),
        (queries_o, queries_h, keep.at[9]), (keys_o, keys_h, keep.at[10]),
    ]
    load(saved)
    for piece in range(NSEQ):
        spread_grad.advance(piece, 0)
    outs.settle()
    for piece in range(NSEQ):
        run_chains(piece)

    def gates_on():
        gates.begin(range(1, len(gates.orders[0])))
        gates.advance(2)
        ups.begin()
        downs.begin()

    def apply(piece, then=None):
        def step(lap, carry):
            first = piece * heads + lap * GROUP
            for k in range(GROUP):
                chain.receive(first + k)
            if then is not None:
                then()
            which = [first + k for k in range(GROUP)]
            states = [halves(entry_o[at]) for at in which]
            key_pairs = [halves(keys_o[at]) for at in which]
            query_pairs = [halves(queries_o[at]) for at in which]
            fresh = [
                wvalues[at] - fine(halves(wkeys_o[at]), state) for at, state in zip(which, states)
            ]
            fresh_pairs = [halves(one) for one in fresh]
            grams = [jnp.where(strict, fine(key, key, NT), 0.0) for key in key_pairs]
            scores = [
                jnp.where(whole, fine(query, key, NT), 0.0)
                for query, key in zip(query_pairs, key_pairs)
            ]
            errors = [
                error_o[at] - fine(key, state) - fine(halves(gram), new)
                for at, key, state, gram, new in zip(which, key_pairs, states, grams, fresh_pairs)
            ]
            outputs = [
                fine(query, state) + fine(halves(score), new)
                for query, state, score, new in zip(query_pairs, states, scores, fresh_pairs)
            ]
            done = list(zip(fresh, errors, outputs))
            for k, (fresh, error, output) in enumerate(done):
                at = first + k
                fresh_o[at] = fresh
                error_o[at] = error
                outputs_o[at] = output
                cols = pl.ds(pl.multiple_of((lap * GROUP + k) * LANES, LANES), LANES)
                head_rows[piece, :, cols] = (output * row_scale(output) * head_gain[...]).astype(BF)
            return carry

        lax.fori_loop(0, groups, step, 0)
        part[piece] = dot(head_rows[piece], out_w[...], NT).astype(BF)

    def close(piece):
        collect.result(piece, hidden_in)
        values = hidden_in[piece] + tokens[piece].astype(F32)
        hidden_in[piece] = values
        feed_rows[piece, mine, :] = (values * row_scale(values) * feed_gain[...]).astype(BF)
        spread_feed.begin(piece)

    for piece in range(NSEQ):
        spread_grad.advance(piece, 1)
    apply(0)
    collect.begin(0)
    apply(1, gates_on)
    kept.append((out_w, out_w_o, keep.at[4]))
    later = [
        (fresh_o, fresh_h, keep.at[11]), (error_o, error_h, keep.at[12]),
        (outputs_o, outputs_h, keep.at[13]),
    ]
    load(kept[-1:] + later)
    collect.advance(0, 1)
    for piece in range(NSEQ):
        for hop in range(2, nm - 2):
            spread_grad.advance(piece, hop)
    collect.advance(0, 2)
    collect.begin(1)
    for turn in range(3, nm):
        collect.advance(0, turn)
    close(0)
    collect.advance(1, 1)
    gates.advance(4)
    spread_feed.advance(0, 0)
    collect.advance(1, 2)
    gates.advance()
    spread_feed.advance(0, 1)
    for turn in range(3, nm):
        collect.advance(1, turn)
    close(1)
    ups.advance(4)
    downs.advance(4)
    for hop in range(2, nm - 1):
        spread_feed.advance(0, hop)
    for piece in range(NSEQ):
        spread_grad.advance(piece, nm - 2)
    late = [
        (feed_rows.at[0], feed_rows_o.at[0], keep.at[5]), (grad_rows, grad_rows_o, keep.at[6]),
        (rows, rows_o, keep.at[3]), (feed_rows.at[1], feed_rows_o.at[1], keep.at[14]),
    ]
    load(late[:3])
    spread_feed.advance(1, 0)
    ups.advance(2)
    for hop in range(1, nm - 1):
        spread_feed.advance(1, hop)
    load(late[3:])
    downs.advance(2)
    ups.advance()
    downs.advance()
    for piece in range(NSEQ):
        spread.finish(piece)
        collect.finish(piece)
        spread_grad.finish(piece)
        spread_feed.finish(piece)
    for gather in (gates, ups, downs):
        gather.settle()
    for gather in (weights, outs, gates, ups, downs):
        gather.finish()
    for piece in range(NSEQ):
        @pl.when(s < ns - 1)
        def _(piece=piece):
            edge_copy(piece).wait_send()

    chain.finish()
    ready(kept + saved + later + late)


def mixer(
    sizes, tokens, cotangent, query_w, key_w, value_w, beta_w, out_in, gate_in, up_in, down_in,
    conv, lengths, bias, mixer_gain, head_gain, feed_gain,
):
    ns, nm = sizes
    width = query_w.shape[1]
    shard = query_w.shape[0]
    depth = ns * shard
    cols = gate_in.shape[1]
    own = tokens.shape
    span = own[1] * nm
    heads = width // LANES
    chains = NSEQ * heads
    rows = (NSEQ, span, depth)
    joined = 3 * width + LANES
    shape = jax.ShapeDtypeStruct
    per_chain = (chains, span, LANES)
    return pl.pallas_call(
        functools.partial(mixer_kernel, sizes),
        out_shape=(
            shape(rows, BF), shape((depth, joined), BF), shape((depth, width), BF),
            shape((depth, cols), BF), shape((depth, cols), BF), shape((depth, cols), BF),
            shape(rows, BF), shape(rows, BF),
            shape(own, F32), shape((NSEQ, span, width), BF), shape((NSEQ, span, 3 * width), BF),
            shape((NSEQ, span, LANES), F32), shape((NSEQ, EDGE, 3 * width), BF),
            shape((ns, LANES, 2 * LANES), BF), shape((8, LANES), F32),
            shape((chains, LANES, LANES), F32), shape((chains, span, span), F32),
        )
        + (shape(per_chain, F32),) * 6,
        in_specs=[VMEM] * 7 + [ANY, ANY, VMEM, VMEM, SMEM, SMEM, VMEM, VMEM, VMEM],
        out_specs=(ANY,) * 8 + (VMEM,) * 8 + (ANY,) * 7,
        scratch_shapes=[pltpu.VMEM((chains, span, span), F32)]
        + [pltpu.VMEM(per_chain, F32)] * 6
        + [
            pltpu.VMEM((shard, joined), BF), pltpu.VMEM((shard, width), BF),
            pltpu.VMEM((shard, cols), BF), pltpu.VMEM((shard, cols), BF), pltpu.VMEM((shard, cols), BF),
            pltpu.VMEM(rows, BF), pltpu.VMEM((depth, joined), BF), pltpu.VMEM((depth, width), BF),
            pltpu.VMEM(rows, BF), pltpu.VMEM(rows, BF), pltpu.VMEM(rows, BF),
            pltpu.VMEM((NSEQ, LEAD + span, 3 * width), F32),
            pltpu.VMEM((NSEQ, span, LANES), F32),
            pltpu.VMEM(per_chain, F32),
            pltpu.VMEM((chains, LANES, 2 * LANES), BF),
            DMA((15,)), DMA((NSEQ,)), DMA((NSEQ,)),
        ]
        + CubeGather.sems(ns) * 5
        + LineGather.sems(nm) * 3
        + LineScatter.scratch(nm, own[1], depth)
        + Chains.scratch(ns, chains),
        compiler_params=comm_params(0),
        name="mixer",
    )(
        tokens, cotangent, query_w, key_w, value_w, beta_w, out_in, gate_in, up_in, down_in,
        conv, lengths, bias, mixer_gain, head_gain, feed_gain,
    )


def feed_kernel(
    sizes, feed_rows_h, grad_rows_h, gate_hbm, up_hbm, down_hbm, hidden_in, gain, cotangent,
    grad_in, mix_rows_o, grad_gate_o, grad_up_o, grad_down_o, down_part_o, gain_o,
    feed_rows, grad_rows, gate_w, up_w, down_w, hidden, grad_gate, grad_up, part, mix_rows,
    keep, *rest,
):
    geo = Geo(sizes)
    nm = geo.nm
    mates = line_mates(geo) + cube_mates(geo)
    greet(mates)
    weights = [
        (gate_hbm, gate_w, keep.at[0]), (up_hbm, up_w, keep.at[1]), (down_hbm, down_w, keep.at[2])
    ]
    inputs = [(feed_rows_h, feed_rows, keep.at[3]), (grad_rows_h, grad_rows, keep.at[4])]
    load(inputs[:1] + weights[:2] + inputs[1:] + weights[2:])
    collect = LineScatter(geo, part, rest[0:3])
    spread = LineGather(geo, mix_rows, rest[3:5])
    first = CubeScatter(geo, gate_w, rest[5:8])
    second = CubeScatter(geo, up_w, rest[8:11])
    for piece in range(NSEQ):
        if piece == 0:
            ready(inputs[:1] + weights[:1])
        gate = dot(feed_rows[piece], gate_w[...])
        if piece == 0:
            ready(weights[1:2])
        up = dot(feed_rows[piece], up_w[...])
        sig = sigmoid(gate)
        active = gate * sig
        hidden[piece] = (active * up).astype(BF)
        if piece == 0:
            ready(inputs[1:] + weights[2:])
        grad_hidden = dot(grad_rows[piece], down_w[...])
        grad_gate[piece] = (grad_hidden * up * sig * (1.0 + gate * (1.0 - sig))).astype(BF)
        grad_up[piece] = (grad_hidden * active).astype(BF)
        part[piece] = (
            dot(grad_gate[piece], gate_w[...], NT) + dot(grad_up[piece], up_w[...], NT)
        ).astype(BF)
        if piece == 0:
            await_all(mates)
            collect.begin(0)
    depth, cols = gate_w.shape
    tile = 512
    span = hidden_in.shape[1]
    mine = pl.ds(pl.multiple_of(geo.m * span, span), span)

    def weight_grad(rows, grads, out):
        def step(at, carry):
            window = pl.ds(pl.multiple_of(at * tile, tile), tile)
            total = dot(rows[0, :, window], grads[0], TN) + dot(rows[1, :, window], grads[1], TN)
            out[window, :] = total.astype(BF)
            return carry

        lax.fori_loop(0, depth // tile, step, 0)

    def close(piece):
        collect.result(piece, grad_in)
        grad_feed = grad_in[piece]
        rows = hidden_in[piece]
        scale = row_scale(rows)
        unit = rows * scale
        part_gain = jnp.sum(grad_feed * unit, 0, keepdims=True)
        if piece == 0:
            gain_o[...] = part_gain
        else:
            gain_o[...] = gain_o[...] + part_gain
        back = cotangent[piece].astype(F32) + norm_backward(grad_feed * gain[...], unit, scale)
        grad_in[piece] = back
        mix_rows[piece, mine, :] = back.astype(BF)
        spread.begin(piece)

    collect.advance(0, 1)
    weight_grad(feed_rows, grad_gate, gate_w)
    first.begin()
    collect.advance(0, 2)
    collect.begin(1)
    weight_grad(feed_rows, grad_up, up_w)
    second.begin()
    first.advance(8)
    for turn in range(3, nm):
        collect.advance(0, turn)
    close(0)
    collect.advance(1, 1)
    second.advance(8)
    spread.advance(0, 0)
    collect.advance(1, 2)
    first.advance(4)
    spread.advance(0, 1)
    for turn in range(3, nm):
        collect.advance(1, turn)
    close(1)
    for piece in range(NSEQ):
        collect.finish(piece)
        part[piece] = dot(hidden[piece], down_w[...], NT).astype(BF)
    later = [(part, down_part_o, keep.at[0])]
    load(later)
    for hop in range(2, nm - 1):
        spread.advance(0, hop)
    second.advance(4)
    spread.advance(1, 0)
    weight_grad(grad_rows, hidden, down_w)
    later.append((down_w, grad_down_o, keep.at[1]))
    load(later[1:])
    for hop in range(1, nm - 1):
        spread.advance(1, hop)
    for piece in range(NSEQ):
        spread.finish(piece)
    later.append((mix_rows, mix_rows_o, keep.at[2]))
    load(later[2:])
    first.finish(grad_gate_o)
    second.finish(grad_up_o)
    ready(later)


def feed(sizes, feed_rows, grad_rows, gate_w, up_w, down_w, hidden_in, gain, cotangent):
    ns, nm = sizes
    depth, cols = gate_w.shape
    span = hidden_in.shape[1]
    shard = depth // ns
    rows = (NSEQ, span * nm, depth)
    inner = (NSEQ, span * nm, cols)
    return pl.pallas_call(
        functools.partial(feed_kernel, sizes),
        out_shape=(
            jax.ShapeDtypeStruct((NSEQ, span, depth), F32),
            jax.ShapeDtypeStruct(rows, BF),
            jax.ShapeDtypeStruct((shard, cols), F32),
            jax.ShapeDtypeStruct((shard, cols), F32),
            jax.ShapeDtypeStruct((depth, cols), BF),
            jax.ShapeDtypeStruct(rows, BF),
            jax.ShapeDtypeStruct((1, depth), F32),
        ),
        in_specs=[ANY] * 5 + [VMEM] * 3,
        out_specs=(VMEM, ANY, VMEM, VMEM, ANY, ANY, VMEM),
        scratch_shapes=[
            pltpu.VMEM(rows, BF), pltpu.VMEM(rows, BF),
            pltpu.VMEM((depth, cols), BF), pltpu.VMEM((depth, cols), BF), pltpu.VMEM((depth, cols), BF),
            pltpu.VMEM(inner, BF), pltpu.VMEM(inner, BF), pltpu.VMEM(inner, BF),
            pltpu.VMEM(rows, BF), pltpu.VMEM(rows, BF), DMA((5,)),
        ]
        + LineScatter.scratch(nm, span, depth)
        + LineGather.sems(nm)
        + CubeScatter.scratch(ns, shard, cols) * 2,
        compiler_params=comm_params(1, 63),
        name="feed",
    )(feed_rows, grad_rows, gate_w, up_w, down_w, hidden_in, gain, cotangent)


def backward_kernel(
    sizes, mix_rows_h, out_weight_h, head_rows, projected, logits, conv, lengths, bias, gain,
    edge, links, solve_h, wkeys_h, fresh_h, error_h, outputs_h, queries_h, keys_h, entry,
    grad_down_hbm, down_part_hbm, hidden_in,
    grads_o, block_o, grad_down_o, conv_o, gain_o, bias_o, out_total_o,
    mix_rows, out_weight, solve, fresh, error, queries, keys,
    extended, betas, grad_output, held, grad_mixed, grad_tail, grad_logit,
    pair, gathered, leaving, edge_out, edge_in, out_total, down_total, down_part, keep,
    edge_send, edge_recv, *rest,
):
    geo = Geo(sizes)
    ns, nm, s, m = geo.ns, geo.nm, geo.s, geo.m
    span, width = projected.shape[1], projected.shape[2] // 3
    heads = width // LANES
    chains = NSEQ * heads
    which = range(heads)
    mates = line_mates(geo) + all_mates(geo)
    greet(mates)
    kept = [(out_total, out_total_o, keep.at[11])]
    loads = [
        (down_part_hbm, down_part, keep.at[0]), (grad_down_hbm, down_total, keep.at[1]),
        (mix_rows_h, mix_rows, keep.at[2]), (out_weight_h, out_weight, keep.at[3]),
        (outputs_h, grad_output, keep.at[4]), (queries_h, queries, keep.at[5]),
        (keys_h, keys, keep.at[6]), (wkeys_h, held, keep.at[7]),
        (fresh_h, fresh, keep.at[8]), (solve_h, solve, keep.at[9]), (error_h, error, keep.at[10]),
    ]
    load(loads)
    collect = LineScatter(geo, down_part, rest[0:3])
    first = CubeScatter(geo, down_total, rest[3:6])
    chain = Chains(geo, chains, pair, gathered, leaving, rest[6:11])
    strict = lower_mask(span, True)
    whole = lower_mask(span, False)
    gain_o[...] = jnp.zeros(gain_o.shape, F32)
    conv_o[...] = jnp.zeros(conv_o.shape, F32)
    pad = grad_mixed.shape[1] - LEAD - span
    for piece in range(NSEQ):
        grad_mixed[piece, :LEAD, :] = jnp.zeros((LEAD, 3 * width), F32)
        grad_mixed[piece, LEAD + span :, :] = jnp.zeros((pad, 3 * width), F32)
        fill_extended(extended, projected, edge, piece)
        strength, live = strengths_of(geo, logits, lengths, bias, heads, piece)
        betas[piece] = strength * live
    await_all(mates)
    ready(loads[:1])
    for piece in range(NSEQ):
        collect.begin(piece)
    ready(loads[1:2])
    first.begin()
    ready(loads[2:8])

    def start(piece, carry):
        grad_head = dot(mix_rows[piece], out_weight[...])
        scaled = [grad_output[piece * heads + h] for h in which]
        scales = [row_scale(output) for output in scaled]
        units = [output * scale for output, scale in zip(scaled, scales)]
        grads = [grad_head[:, h * LANES : (h + 1) * LANES] for h in which]
        share = [jnp.sum(grad * unit, 0, keepdims=True) for grad, unit in zip(grads, units)]
        gain_o[...] = gain_o[...] + sum(share)
        grads = [
            norm_backward(grad * gain[...], unit, scale)
            for grad, unit, scale in zip(grads, units, scales)
        ]
        grad_pairs = [halves(grad) for grad in grads]
        query_pairs = [halves(queries[piece * heads + h]) for h in which]
        scores = [
            jnp.where(whole, fine(query, halves(keys[piece * heads + h]), NT), 0.0)
            for h, query in zip(which, query_pairs)
        ]
        spread = [fine(halves(score), grad, TN) for score, grad in zip(scores, grad_pairs)]
        found = [
            fine(query, grad, TN) - fine(halves(held[piece * heads + h]), halves(one), TN)
            for h, query, grad, one in zip(which, query_pairs, grad_pairs, spread)
        ]
        found = [link.astype(BF) for link in found]
        for h in which:
            at = piece * heads + h
            grad_output[at] = grads[h]
            held[at] = spread[h]
            pair[at] = found[h]
        for h in which:
            chain.give(piece * heads + h, found[h])
        return carry

    lax.fori_loop(0, NSEQ, start, 0)
    first.advance(2)
    ready(loads[8:])

    def through_conv(piece, h, group, grad, key=None):
        z = before_silu(extended, conv, piece, group, h, width, m)
        sig = sigmoid(z)
        if key is not None:
            raw = z * sig
            scale = lax.rsqrt(jnp.sum(raw * raw, -1, keepdims=True) + KEY_EPSILON)
            grad = scale * (grad - key * jnp.sum(key * grad, -1, keepdims=True))
        grad = grad * sig * (1.0 + z * (1.0 - sig))
        cols = slice(group * width + h * LANES, group * width + (h + 1) * LANES)
        local = slice(h * LANES, (h + 1) * LANES)
        grad_mixed[piece, pl.ds(LEAD, span), cols] = grad
        back = None
        for tap in range(4):
            share = jnp.sum(grad * extended[piece, pl.ds(LEAD - tap, span), cols], 0, keepdims=True)
            row = slice(group * 4 + tap, group * 4 + tap + 1)
            conv_o[row, local] = conv_o[row, local] + share
            term = (
                conv_row(conv, group, tap, m * width + h * LANES)
                * grad_mixed[piece, pl.ds(tap, LEAD + span), cols]
            )
            back = term if back is None else back + term
        edge_out[piece, :, cols] = back[:LEAD]
        grads_o[piece, :, cols] = back[LEAD:].astype(BF)
        grad_tail[piece, :, cols] = back[LEAD + span - EDGE :]

    def before_exit(piece):
        base = piece * heads
        grad_pairs = [halves(grad_output[base + h]) for h in which]
        key_pairs = [halves(keys[base + h]) for h in which]
        scores = [
            halves(jnp.where(whole, fine(grad, halves(fresh[base + h]), NT), 0.0))
            for h, grad in zip(which, grad_pairs)
        ]
        grads = [
            fine(score, key) + fine(grad, halves(entry[base + h]), NT)
            for h, score, key, grad in zip(which, scores, key_pairs, grad_pairs)
        ]
        to_keys = [
            fine(score, halves(queries[base + h]), TN) for h, score in zip(which, scores)
        ]
        for h in which:
            grad_output[base + h] = to_keys[h]
        for h in which:
            through_conv(piece, h, 0, grads[h])

    def after_exit(piece):
        base = piece * heads
        for h in which:
            chain.receive(base + h)

        @pl.when(piece == 0)
        def _():
            first.advance(6)

        key_pairs = [halves(keys[base + h]) for h in which]
        exits = [halves(leaving[base + h]) for h in which]
        fresh_pairs = [halves(fresh[base + h]) for h in which]
        strengths = [column_of(betas[piece], h) for h in which]
        weak = [halves(held[base + h] + fine(key, out)) for h, key, out in zip(which, key_pairs, exits)]
        weak = [fine(halves(solve[base + h]), one, TN) for h, one in zip(which, weak)]
        grad_beta = [jnp.sum(one * error[base + h], -1, keepdims=True) for h, one in zip(which, weak)]
        values = [one * beta for one, beta in zip(weak, strengths)]
        value_pairs = [halves(value) for value in values]
        scores = [
            halves(jnp.where(strict, -fine(value, new, NT), 0.0))
            for value, new in zip(value_pairs, fresh_pairs)
        ]
        grads = [
            grad_output[base + h]
            - fine(value, halves(entry[base + h]), NT)
            + fine(score, key)
            + fine(score, key, TN)
            + fine(new, out, NT)
            for h, value, score, key, new, out in zip(
                which, value_pairs, scores, key_pairs, fresh_pairs, exits
            )
        ]
        lane = iota((span, LANES), 1)
        grad_logit[piece] = sum(jnp.where(lane == h, grad_beta[h], 0.0) for h in which)
        for h in which:
            through_conv(piece, h, 1, grads[h], keys[base + h])
            through_conv(piece, h, 2, values[h])

    def run_chains(piece):
        def advance(carry, at):
            (state,) = carry
            high, low = halves(state)
            move = links[at][:, :LANES]
            state = state - (dot(move, high, TN) + dot(move, low, TN)) + gathered[at].astype(F32)
            return (state,)

        chain.run(
            piece * heads, heads, advance, (jnp.zeros((LANES, LANES), F32),), True, lambda carry: None
        )

    def edge_copy(piece):
        return remote(
            edge_out.at[piece], edge_in.at[piece], edge_send.at[piece], edge_recv.at[piece],
            (s - 1, m),
        )

    depth = out_weight.shape[0]
    tile = 512

    def weight_grad(at, carry):
        window = pl.ds(pl.multiple_of(at * tile, tile), tile)
        total = dot(mix_rows[0, :, window], head_rows[0], TN) + dot(
            mix_rows[1, :, window], head_rows[1], TN
        )
        out_total[window, :] = total.astype(BF)
        return carry

    def leave(piece, carry):
        before_exit(piece)

        @pl.when(piece == 0)
        def _():
            for at in range(NSEQ):
                run_chains(at)
            lax.fori_loop(0, depth // tile, weight_grad, 0)
            load(kept)
            for at in range(NSEQ):
                collect.advance(at, 1)

        return carry

    lax.fori_loop(0, NSEQ, leave, 0)

    def enter(piece, carry):
        after_exit(piece)

        @pl.when(s > 0)
        def _():
            edge_copy(piece).start()

        @pl.when(piece == 0)
        def _():
            for at in range(NSEQ):
                collect.advance(at, 2)

        return carry

    lax.fori_loop(0, NSEQ, enter, 0)
    bias_sum = jnp.zeros((1, LANES), F32)
    for piece in range(NSEQ):
        sig, live = strengths_of(geo, logits, lengths, bias, heads, piece)
        grad = grad_logit[piece] * live * sig * (1.0 - sig)
        bias_sum = bias_sum + jnp.sum(grad, 0, keepdims=True)
        grads_o[piece, :, pl.ds(3 * width, LANES)] = grad.astype(BF)
    lane = iota((1, LANES), 1)
    spread_bias = jnp.zeros((1, LANES), F32)
    for h in which:
        spread_bias = spread_bias + jnp.where(lane == m * heads + h, column_of(bias_sum, h), 0.0)
    bias_o[...] = spread_bias
    first.advance(4)
    for turn in range(3, nm):
        for piece in range(NSEQ):
            collect.advance(piece, turn)
    for piece in range(NSEQ):
        collect.result(piece, block_o)
        block_o[piece] = block_o[piece] + hidden_in[piece]
        collect.finish(piece)

    for piece in range(NSEQ):
        @pl.when(s < ns - 1)
        def _(piece=piece):
            edge_copy(piece).wait_recv()
            tail = pl.ds(EDGE - LEAD, LEAD)
            grad_tail[piece, tail, :] = grad_tail[piece, tail, :] + edge_in[piece]
            grads_o[piece, pl.ds(span - EDGE, EDGE), pl.ds(0, 3 * width)] = grad_tail[piece].astype(BF)

        @pl.when(s > 0)
        def _(piece=piece):
            edge_copy(piece).wait_send()

    first.finish(grad_down_o)
    chain.finish()
    ready(kept)


def backward(
    sizes, mix_rows, out_weight, head_rows, projected, logits, conv, lengths, bias, gain, saved,
    grad_down, down_part, hidden_in,
):
    ns, nm = sizes
    span, width = projected.shape[1], projected.shape[2] // 3
    heads = width // LANES
    chains = NSEQ * heads
    depth, cols = grad_down.shape
    shard = depth // ns
    local = hidden_in.shape
    rows = (NSEQ, span, depth)
    per_chain = (chains, span, LANES)
    return pl.pallas_call(
        functools.partial(backward_kernel, sizes),
        out_shape=(
            jax.ShapeDtypeStruct((NSEQ, span, 3 * width + LANES), BF),
            jax.ShapeDtypeStruct(local, F32),
            jax.ShapeDtypeStruct((shard, cols), F32),
            jax.ShapeDtypeStruct((12, width), F32),
            jax.ShapeDtypeStruct((1, LANES), F32),
            jax.ShapeDtypeStruct((1, LANES), F32),
            jax.ShapeDtypeStruct((depth, width), BF),
        ),
        in_specs=[ANY, ANY] + [VMEM] * 4 + [SMEM, SMEM] + [VMEM] * 3 + [ANY] * 7 + [VMEM, ANY, ANY, VMEM],
        out_specs=(VMEM,) * 6 + (ANY,),
        scratch_shapes=[
            pltpu.VMEM(rows, BF), pltpu.VMEM((depth, width), BF),
            pltpu.VMEM((chains, span, span), F32),
        ]
        + [pltpu.VMEM(per_chain, F32)] * 4
        + [
            pltpu.VMEM((NSEQ, LEAD + span, 3 * width), F32),
            pltpu.VMEM((NSEQ, span, LANES), F32),
            pltpu.VMEM(per_chain, F32),
            pltpu.VMEM(per_chain, F32),
            pltpu.VMEM((NSEQ, LEAD + span + LEAD, 3 * width), F32),
            pltpu.VMEM((NSEQ, EDGE, 3 * width), F32),
            pltpu.VMEM((NSEQ, span, LANES), F32),
            pltpu.VMEM((chains, LANES, LANES), BF),
            pltpu.VMEM((ns, LANES, LANES), BF),
            pltpu.VMEM((chains, LANES, LANES), F32),
            pltpu.VMEM((NSEQ, LEAD, 3 * width), F32),
            pltpu.VMEM((NSEQ, LEAD, 3 * width), F32),
            pltpu.VMEM((depth, width), BF),
            pltpu.VMEM((depth, cols), BF),
            pltpu.VMEM(rows, BF),
            DMA((12,)), DMA((NSEQ,)), DMA((NSEQ,)),
        ]
        + LineScatter.scratch(nm, local[1], depth)
        + CubeScatter.scratch(ns, shard, cols)
        + Chains.scratch(ns, chains),
        compiler_params=comm_params(2, 63),
        name="recurrence_back",
    )(
        mix_rows, out_weight, head_rows, projected, logits, conv, lengths, bias, gain, *saved,
        grad_down, down_part, hidden_in,
    )


def last_kernel(
    sizes, rows_h, grads_h, proj_w_h, out_total_h, tokens, gain, grad_in,
    conv_part, head_gain, bias, norms, feed_gain,
    grad_tokens, grad_weight_o, grad_out_o,
    conv_o, head_gain_o, bias_o, norm_o, feed_gain_o, gain_o,
    rows, grads, proj_w, part, total, out_total, vector, over_seq, over_mp,
    keep, seq_send, seq_recv, mp_send, mp_recv, *rest,
):
    geo = Geo(sizes)
    ns, nm, s, m = geo.ns, geo.nm, geo.s, geo.m
    mates = [(s, (m + k) % nm) for k in range(1, nm)] + all_mates(geo)
    greet(mates)
    loads = [
        (out_total_h, out_total, keep.at[0]), (rows_h, rows, keep.at[1]), (grads_h, grads, keep.at[2]),
        (proj_w_h, proj_w, keep.at[3]),
    ]
    load(loads[2:] + loads[:2])
    depth = proj_w.shape[0]
    width = vector.shape[1]
    wide = depth // width
    row = conv_part.shape[0]
    early = -(-(row + 1 + wide) // 8) * 8
    vector[...] = jnp.zeros(vector.shape, F32)
    vector[0:row, :] = conv_part[...]
    vector[row : row + 1, 0:LANES] = head_gain[...]
    vector[row : row + 1, LANES : 2 * LANES] = bias[...]
    vector[row : row + 1, 2 * LANES : 3 * LANES] = norms[0:1, :]
    for at in range(wide):
        vector[row + 1 + at : row + 2 + at, :] = feed_gain[:, at * width : (at + 1) * width]
    await_all(mates)

    def seq_copy(stage, k):
        rows_of = pl.ds(0, early) if stage == 0 else pl.ds(early, vector.shape[0] - early)
        return remote(
            vector.at[rows_of], over_seq.at[k, rows_of], seq_send.at[stage, k], seq_recv.at[stage, k],
            ((s + 1 + k) % ns, m),
        )

    def seq_start(stage):
        def step(k, carry):
            seq_copy(stage, k).start()
            return carry

        lax.fori_loop(0, ns - 1, step, 0)

    seq_start(0)
    collect = LineScatter(geo, part, rest[0:3])
    scatter = CubeScatter(geo, total, rest[3:6])
    outs = CubeScatter(geo, out_total, rest[6:9])
    shares = []

    def spread(piece):
        if piece == 0:
            ready(loads[2:])
        value = dot(grads[piece], proj_w[...], NT)
        part[piece] = value.astype(BF)
        collect.begin(piece)
        if piece == 0:
            ready(loads[1:2])
        shares.append(jnp.sum(value * rows[piece].astype(F32), 0, keepdims=True))

    tile = 512

    def weight_grad(left, right, out):
        def step(at, carry):
            window = pl.ds(pl.multiple_of(at * tile, tile), tile)
            value = dot(left[0, :, window], right[0], TN) + dot(left[1, :, window], right[1], TN)
            out[window, :] = value.astype(BF)
            return carry

        lax.fori_loop(0, depth // tile, step, 0)

    ready(loads[:1])
    outs.begin()
    spread(0)
    outs.advance(8)
    weight_grad(rows, grads, total)
    scatter.begin()
    spread(1)
    outs.advance(2)
    share = (shares[0] + shares[1]) / gain[...]
    for at in range(wide):
        vector[early + at : early + 1 + at, :] = share[:, at * width : (at + 1) * width]

    def mp_copy(k):
        return remote(
            over_mp.at[0], over_mp.at[1 + k], mp_send.at[k], mp_recv.at[k], (s, (m + 1 + k) % nm)
        )

    seq_start(1)
    collect.advance(0, 1)
    scatter.advance(8)

    def seq_add(k, value):
        for stage in range(2):
            seq_copy(stage, k).wait_recv()
        return value + over_seq[k]

    over_mp[0] = lax.fori_loop(0, ns - 1, seq_add, vector[...])
    for k in range(nm - 1):
        mp_copy(k).start()
    collect.advance(1, 1)
    collect.advance(0, 2)
    outs.advance(2)
    for k in range(nm - 1):
        mp_copy(k).wait_recv()
    scatter.advance(2)
    collect.advance(1, 2)
    for turn in range(3, nm):
        collect.advance(0, turn)
        scatter.advance(2)
        collect.advance(1, turn)
    for piece in range(NSEQ):
        collect.result(piece, grad_tokens)
        values = tokens[piece].astype(F32)
        scale = row_scale(values)
        grad_tokens[piece] = grad_in[piece] + norm_backward(
            grad_tokens[piece] * gain[...], values * scale, scale
        )
        collect.finish(piece)
    for k in range(nm):
        origin = (m + nm - k) % nm
        cols = pl.ds(pl.multiple_of(origin * width, width), width)
        for group in range(3):
            for tap in range(4):
                at = group * 4 + tap
                conv_o[group, tap : tap + 1, cols] = over_mp[k, at : at + 1, :]
    summed = over_mp[0]
    for k in range(1, nm):
        summed = summed + over_mp[k]
    head_gain_o[...] = summed[row : row + 1, 0:LANES]
    bias_o[...] = summed[row : row + 1, LANES : 2 * LANES]
    norm_o[...] = summed[row : row + 1, 2 * LANES : 3 * LANES] / (NSEQ * HEADS * ns)
    for at in range(wide):
        cols = slice(at * width, (at + 1) * width)
        feed_gain_o[:, cols] = summed[row + 1 + at : row + 2 + at, :]
        gain_o[:, cols] = summed[early + at : early + 1 + at, :]
    outs.finish(grad_out_o)
    scatter.finish(grad_weight_o)

    def seq_done(k, carry):
        for stage in range(2):
            seq_copy(stage, k).wait_send()
        return carry

    lax.fori_loop(0, ns - 1, seq_done, 0)
    for k in range(nm - 1):
        mp_copy(k).wait_send()


def last(sizes, rows, grads, proj_w, out_total, tokens, gain, grad_in, small):
    ns, nm = sizes
    depth, cols = proj_w.shape
    span = tokens.shape[1]
    shard = depth // ns
    width = (cols - LANES) // 3
    wide = depth // width
    vector = (-(-(13 + wide) // 8) * 8 + -(-wide // 8) * 8, width)
    shape = jax.ShapeDtypeStruct
    line = shape((1, LANES), F32)
    return pl.pallas_call(
        functools.partial(last_kernel, sizes),
        out_shape=(
            shape(grad_in.shape, F32), shape((shard, cols), F32), shape((shard, width), F32),
            shape((3, 4, depth), F32), line, line, line, shape((1, depth), F32), shape((1, depth), F32),
        ),
        in_specs=[ANY] * 4 + [VMEM] * 8,
        out_specs=(VMEM,) * 9,
        scratch_shapes=[
            pltpu.VMEM(rows.shape, BF),
            pltpu.VMEM(grads.shape, BF),
            pltpu.VMEM((depth, cols), BF),
            pltpu.VMEM(rows.shape, BF),
            pltpu.VMEM((depth, cols), BF),
            pltpu.VMEM((depth, width), BF),
            pltpu.VMEM(vector, F32),
            pltpu.VMEM((ns - 1,) + vector, F32),
            pltpu.VMEM((nm,) + vector, F32),
            DMA((4,)), DMA((2, ns - 1)), DMA((2, ns - 1)), DMA((nm - 1,)), DMA((nm - 1,)),
        ]
        + LineScatter.scratch(nm, span, depth)
        + CubeScatter.scratch(ns, shard, cols)
        + CubeScatter.scratch(ns, shard, width),
        compiler_params=comm_params(3),
        name="last",
    )(rows, grads, proj_w, out_total, tokens, gain, grad_in, *small)


def deliver_kernel(
    block, grad_tokens, grad_proj, grad_gate, grad_up, grad_down, grad_out, conv, *rest
):
    lines, rest = rest[:5], rest[5:]
    (
        block_o, grad_tokens_o, query_o, key_o, value_o, grad_gate_o, grad_up_o, beta_o, grad_down_o,
        grad_out_o, conv_o,
    ) = rest[:11]
    line_os, rest = rest[11:16], rest[16:]
    block_v, tokens_v, proj_v, gate_v, up_v, down_v, out_v, down_t, out_t, conv_v = rest[:10]
    line_vs, sems = rest[10:15], rest[15]
    width = query_o.shape[1]
    coming = [
        (src, held, sems.at[k])
        for k, (src, held) in enumerate(
            (
                (grad_gate, gate_v), (grad_up, up_v), (block, block_v), (grad_tokens, tokens_v),
                (grad_proj, proj_v), (grad_out, out_v), (grad_down, down_v), (conv, conv_v),
            )
            + tuple(zip(lines, line_vs))
        )
    ]
    load(coming)
    going = []

    def send(held, dst):
        going.append((held, dst, sems.at[len(coming) + len(going)]))
        load(going[-1:])

    ready(coming[0:4])
    send(gate_v, grad_gate_o)
    send(up_v, grad_up_o)
    send(block_v, block_o)
    send(tokens_v, grad_tokens_o)
    ready(coming[4:5])
    for k, dst in enumerate((query_o, key_o, value_o)):
        send(proj_v.at[:, pl.ds(k * width, width)], dst)
    ready(coming[5:])
    out_t[...] = out_v[...].T
    send(out_t, grad_out_o)
    down_t[...] = down_v[...].T
    send(down_t, grad_down_o)
    beta_o[...] = proj_v[:, 3 * width :].T[: beta_o.shape[0], :]
    conv_o[...] = conv_v[...]
    for line, dst in zip(line_vs, line_os):
        dst[...] = line[:, : dst.shape[1]]
    ready(going)


def deliver(block, grad_tokens, grad_proj, grad_gate, grad_up, grad_down, grad_out, conv, lines, counts):
    shard, cols = grad_gate.shape
    width = (grad_proj.shape[1] - LANES) // 3
    heads = width // LANES
    shape = jax.ShapeDtypeStruct
    square = shape((shard, width), F32)
    wide = shape((shard, cols), F32)
    there = pl.BlockSpec(memory_space=pltpu.HBM)
    held = [
        block.shape, grad_tokens.shape, grad_proj.shape, (shard, cols), (shard, cols), (shard, cols),
        (shard, width), (cols, shard), (width, shard), conv.shape,
    ] + [line.shape for line in lines]
    return pl.pallas_call(
        deliver_kernel,
        out_shape=(
            shape(block.shape, F32), shape(grad_tokens.shape, F32), square, square, square, wide, wide,
            shape((heads, shard), F32), shape((cols, shard), F32), shape((width, shard), F32),
            shape(conv.shape, F32),
        )
        + tuple(shape((1, count), F32) for count in counts),
        in_specs=[there] * 13,
        out_specs=(there,) * 7 + (VMEM, there, there) + (VMEM,) * 6,
        scratch_shapes=[pltpu.VMEM(dims, F32) for dims in held] + [DMA((24,))],
        compiler_params=pltpu.CompilerParams(vmem_limit_bytes=63 * 2**20),
        name="deliver",
    )(block, grad_tokens, grad_proj, grad_gate, grad_up, grad_down, grad_out, conv, *lines)


def on_device(
    sizes,
    tokens,
    lengths,
    mixer_gain,
    query_weight,
    key_weight,
    value_weight,
    beta_weight,
    beta_bias,
    conv_weight,
    head_gain,
    out_weight,
    feed_gain,
    gate_weight,
    up_weight,
    down_weight,
    cotangent,
):
    ns, nm = sizes
    depth = tokens.shape[2]
    width = query_weight.shape[1]
    heads = width // LANES
    mixer_gain_row = mixer_gain.reshape(1, depth)
    feed_gain_row = feed_gain.reshape(1, depth)
    head_gain_row = head_gain.reshape(1, LANES)
    (
        rows, proj_w, out_w, gate_w, up_w, down_w, grad_rows, feed_rows,
        hidden_in, head_rows, projected, logits, edge, links, norms, entry, *saved,
    ) = mixer(
        sizes, tokens, cotangent, query_weight, key_weight, value_weight, beta_weight.T, out_weight,
        gate_weight, up_weight, down_weight, conv_weight, lengths, beta_bias, mixer_gain_row,
        head_gain_row, feed_gain_row,
    )
    grad_in, mix_rows, grad_gate, grad_up, grad_down_part, down_part, feed_gain_part = feed(
        sizes, feed_rows, grad_rows, gate_w, up_w, down_w, hidden_in, feed_gain_row, cotangent
    )
    grads, block_output, grad_down, conv_part, gain_part, bias_part, grad_out_part = backward(
        sizes, mix_rows, out_w, head_rows, projected, logits, conv_weight, lengths, beta_bias,
        head_gain_row, (edge, links, *saved, entry), grad_down_part, down_part, hidden_in,
    )
    (
        grad_tokens, grad_proj_w, grad_out, conv_grad, gain_grad, bias_grad, norm, feed_gain_grad,
        mixer_grad,
    ) = last(
        sizes, rows, grads, proj_w, grad_out_part, tokens, mixer_gain_row, grad_in,
        (conv_part, gain_part, bias_part, norms, feed_gain_part),
    )
    (
        block_output, grad_tokens, grad_query, grad_key, grad_value, grad_gate, grad_up, grad_beta,
        grad_down, grad_out, conv_grad, mixer_grad, feed_gain_grad, gain_grad, bias_grad, norm,
    ) = deliver(
        block_output, grad_tokens, grad_proj_w, grad_gate, grad_up, grad_down, grad_out, conv_grad,
        (mixer_grad, feed_gain_grad, gain_grad, bias_grad, norm), (depth, depth, LANES, nm * heads, 1),
    )
    return (
        block_output,
        grad_tokens,
        mixer_grad.reshape(depth),
        grad_query,
        grad_key,
        grad_value,
        grad_beta.T,
        bias_grad.reshape(nm * heads),
        conv_grad,
        gain_grad.reshape(LANES),
        grad_out,
        feed_gain_grad.reshape(depth),
        grad_gate,
        grad_up,
        grad_down,
        norm[0, 0],
    )


def solution(mesh):
    sizes = (mesh.shape["seq"], mesh.shape["mp"])
    by_rows = P("seq", "mp")
    by_cols = P("mp", "seq")
    placed = P(None, ("seq", "mp"), None)
    return jax.shard_map(
        functools.partial(on_device, sizes),
        mesh=mesh,
        in_specs=(
            placed, P(), P(), by_rows, by_rows, by_rows, by_rows, P(), P(), P(), by_cols, P(),
            by_rows, by_rows, by_cols, placed,
        ),
        out_specs=(
            placed, placed, P(), by_rows, by_rows, by_rows, by_rows, P(), P(), P(), by_cols, P(),
            by_rows, by_rows, by_cols, P(),
        ),
        check_vma=False,
    )
```
